32 devices in a mesh: dp: 16 (over z, y, core), seq: 2 (over x).
Axes of the slice: x: 2, y: 2, z: 4, core: 2. Of those that a mesh axis runs over, the one named last changes fastest.
Arguments:
- tokens: bfloat16 [16, 1024, 768], P('dp', 'seq'), may hold values from -6 to 6
- cotangent: bfloat16 [16, 1024, 768], P('dp', 'seq'), may hold values from -6 to 6
- time_index: int32 [16], P('dp'), may hold values from 0 to 999
- step_table: float32 [1000, 128], replicated, may hold values from -6 to 6
- first_gain: bfloat16 [768], replicated, may hold values from 0.5 to 1.5
- attn_qkv: bfloat16 [768, 2304], replicated, may hold values from -0.21875 to 0.21875
- attn_out: bfloat16 [768, 768], replicated, may hold values from -2.5 to 2.5
- second_gain: bfloat16 [768], replicated, may hold values from 0.5 to 1.5
- mlp_up: bfloat16 [768, 3072], replicated, may hold values from -0.21875 to 0.21875
- up_bias: bfloat16 [3072], replicated, may hold values from -3 to 3
- mlp_down: bfloat16 [3072, 768], replicated, may hold values from -0.109375 to 0.109375
- down_bias: bfloat16 [768], replicated, may hold values from -3 to 3
- ada_weight: bfloat16 [128, 4608], replicated, may hold values from -0.5 to 0.5
- ada_bias: bfloat16 [4608], replicated, may hold values from -3 to 3
Outputs:
- mixed: bfloat16 [16, 1024, 768], P('dp', 'seq')
- tokens_grad: float32 [16, 1024, 768], P('dp', 'seq')
- cond_grad: float32 [16, 128], P('dp')
- first_gain_grad: float32 [768], replicated
- attn_qkv_grad: float32 [768, 2304], P('dp')
- attn_out_grad: float32 [768, 768], P('dp')
- second_gain_grad: float32 [768], replicated
- mlp_up_grad: float32 [768, 3072], P('dp')
- up_bias_grad: float32 [3072], replicated
- mlp_down_grad: float32 [3072, 768], P('dp')
- down_bias_grad: float32 [768], replicated
- ada_weight_grad: float32 [128, 4608], P(None, 'dp')
- ada_bias_grad: float32 [4608], replicated
The draws below stay inside these ranges and needn't reach their ends.
All inputs are finite; a program needn't handle non-finite values.
Results may differ from the reference program's by a relative error of at most 0.014.
The reference program's roundings to bfloat16 on the way count: a program that leaves them out, or rounds other values in their place, can miss the bound.
Values may be sent and summed in bfloat16 or wider, within the bound.
No kernel may reach another device: no remote copies, remote signals or barrier semaphores. Data moves between devices by JAX's collectives and lax.ppermute only.
A program may use at most 192 MiB of HBM per device.

```python
import jax
import jax.numpy as jnp
from jax import lax

D = 768
H = 12
HD = 64
FF = 3072
C = 128
STEPS = 1000
ROWS = 16
LEN = 1024


def plant(array, own_key, low, high):
    longest = array.shape.index(max(array.shape))
    spots = []
    for shift in (0, 1):
        where = [jax.random.randint(jax.random.fold_in(own_key, axis), (), 0, length) for axis, length in enumerate(array.shape)]
        where[longest] = (where[longest] + shift) % array.shape[longest]
        spots.append(tuple(where))
    return array.at[spots[0]].set(low).at[spots[1]].set(high)


def block_levels(own_key, dims, split, smallest, largest):
    level = 1.0
    for axis_at, blocks in split:
        heights = jax.random.uniform(jax.random.fold_in(jax.random.fold_in(own_key, 6), axis_at), (blocks,), jnp.float32, smallest / len(split), largest / len(split))
        level = level * jnp.repeat(jnp.exp(heights), dims[axis_at] // blocks).reshape((-1,) + (1,) * (len(dims) - 1 - axis_at))
    return level


def noise(stream_key, dims, scale, bound, split=(), kind=jnp.bfloat16):
    values = jax.random.normal(stream_key, dims, jnp.float32) * scale
    if len(split) > 0:
        values = block_levels(stream_key, dims, split, -0.22, 0.18) * values
    return jnp.clip(values, min=-bound, max=bound).astype(kind)


def setup_inputs(seed: int = 0) -> dict:
    seeds = jax.random.split(jax.random.key(seed), 15)
    tokens = noise(seeds[0], (ROWS, LEN, D), 1.0, 6.0, ((0, 16), (1, 2)))
    cotangent = noise(seeds[1], (ROWS, LEN, D), 1.0, 6.0, ((0, 16), (1, 2)))
    time_index = plant(jax.random.randint(seeds[2], (ROWS,), 0, STEPS), jax.random.fold_in(seeds[2], 1), 0, STEPS - 1).astype(jnp.int32)
    step_table = noise(seeds[3], (STEPS, C), 1.0, 6.0, (), jnp.float32)
    first_gain = jnp.clip(1.0 + 0.1 * jax.random.normal(seeds[4], (D,), jnp.float32), 0.5, 1.5).astype(jnp.bfloat16)
    attn_qkv = noise(seeds[5], (D, 3 * D), D ** -0.5, 0.21875)
    attn_out = noise(seeds[6], (D, D), (max(D // 128, 1)) ** -0.5, 2.5)
    second_gain = jnp.clip(1.0 + 0.1 * jax.random.normal(seeds[7], (D,), jnp.float32), 0.5, 1.5).astype(jnp.bfloat16)
    mlp_up = noise(seeds[8], (D, FF), D ** -0.5, 0.21875)
    up_bias = noise(seeds[9], (FF,), 0.5, 3.0)
    mlp_down = noise(seeds[10], (FF, D), FF ** -0.5, 0.109375)
    down_bias = noise(seeds[11], (D,), 0.5, 3.0)
    ada_weight = noise(seeds[12], (C, 6 * D), C ** -0.5, 0.5)
    ada_bias = noise(seeds[13], (6 * D,), 0.5, 3.0)
    return {"tokens": tokens, "cotangent": cotangent, "time_index": time_index, "step_table": step_table, "first_gain": first_gain, "attn_qkv": attn_qkv, "attn_out": attn_out, "second_gain": second_gain, "mlp_up": mlp_up, "up_bias": up_bias, "mlp_down": mlp_down, "down_bias": down_bias, "ada_weight": ada_weight, "ada_bias": ada_bias}


@jax.custom_vjp
def low(v):
    return lax.optimization_barrier(v.astype(jnp.bfloat16)).astype(jnp.float32)

@jax.custom_vjp
def low_back(v):
    return v

def low_keep(v):
    return (low(v), None)

def low_pass(kept, grad):
    return (grad,)

def back_keep(v):
    return (v, None)

def back_low(kept, grad):
    return (low(grad),)
low.defvjp(low_keep, low_pass)
low_back.defvjp(back_keep, back_low)
highest = lax.Precision.HIGHEST

def norm_mod(inputs, gain, shift, scale):
    center = inputs - lax.optimization_barrier(jnp.mean(inputs, axis=-1, keepdims=True))
    spread = lax.optimization_barrier(jnp.mean(center * center, axis=-1, keepdims=True))
    return center * lax.rsqrt(spread + 1e-05) * gain * (1.0 + scale) + shift

def tables(positions, head_dim):
    half_dim = head_dim // 2
    frequency = jnp.exp(-jnp.log(10000.0) * (2.0 * jnp.arange(half_dim, dtype=jnp.float32) / head_dim))
    angles = positions.astype(jnp.float32)[:, None] * frequency[None, :]
    return (jnp.cos(angles)[:, None, :], jnp.sin(angles)[:, None, :])

def rotate(heads_in, cosine, sine_table):
    half_dim = heads_in.shape[-1] // 2
    lower_half = heads_in[..., :half_dim]
    upper_half = heads_in[..., half_dim:]
    return jnp.concatenate([lower_half * cosine - upper_half * sine_table, upper_half * cosine + lower_half * sine_table], -1)

def attend(members):
    query, keys_in, values_in = members
    length = query.shape[0]
    query_heads = query.reshape(length, H, HD)
    key_heads = keys_in.reshape(length, H, HD)
    value_heads = values_in.reshape(length, H, HD)
    scores = low_back(jnp.einsum('qhd,khd->hqk', query_heads, key_heads, precision=highest) * HD ** (-0.5))
    probs = low(jax.nn.softmax(scores, axis=-1))
    result = jnp.einsum('hqk,khd->qhd', probs, value_heads, precision=highest)
    return result.reshape(length, H * HD)

def forward(tokens, embedded, first_gain, attn_qkv, attn_out, second_gain, mlp_up, up_bias, mlp_down, down_bias, ada_weight, ada_bias):
    cond = jax.nn.silu(embedded)
    modulation = jnp.dot(cond, ada_weight, precision=highest) + ada_bias
    blocks = [modulation[:, None, index * D:(index + 1) * D] for index in range(6)]
    shift1, scale1, gate1, shift2, scale2, gate2 = blocks
    normed = low(norm_mod(tokens, first_gain, shift1, scale1))
    projected = low_back(jnp.einsum('rld,de->rle', normed, attn_qkv, precision=highest))
    cosine, sine_table = tables(jnp.arange(LEN, dtype=jnp.int32), HD)
    query = low(rotate(projected[..., :D].reshape(ROWS, LEN, H, HD), cosine, sine_table)).reshape(ROWS, LEN, D)
    keys_rot = low(rotate(projected[..., D:2 * D].reshape(ROWS, LEN, H, HD), cosine, sine_table)).reshape(ROWS, LEN, D)
    values_low = low(projected[..., 2 * D:])
    attended = lax.map(jax.checkpoint(attend), (query, keys_rot, values_low))
    attended = low_back(low(attended))
    branch = low_back(jnp.einsum('rld,de->rle', attended, attn_out, precision=highest))
    middle = tokens + gate1 * branch
    normed2 = low(norm_mod(middle, second_gain, shift2, scale2))
    pre_act = low_back(jnp.einsum('rld,df->rlf', normed2, mlp_up, precision=highest) + up_bias)
    activated = low(jax.nn.gelu(pre_act, approximate=True))
    ffn_out = low_back(jnp.einsum('rlf,fd->rld', activated, mlp_down, precision=highest) + down_bias)
    return middle + gate2 * ffn_out

def reference(tokens, cotangent, time_index, step_table, first_gain, attn_qkv, attn_out, second_gain, mlp_up, up_bias, mlp_down, down_bias, ada_weight, ada_bias):
    embedded = jnp.take(step_table, time_index.astype(jnp.int32), axis=0)
    output, pullback = jax.vjp(forward, tokens.astype(jnp.float32), embedded, first_gain.astype(jnp.float32), attn_qkv.astype(jnp.float32), attn_out.astype(jnp.float32), second_gain.astype(jnp.float32), mlp_up.astype(jnp.float32), up_bias.astype(jnp.float32), mlp_down.astype(jnp.float32), down_bias.astype(jnp.float32), ada_weight.astype(jnp.float32), ada_bias.astype(jnp.float32))
    grads = pullback(cotangent.astype(jnp.float32))
    return (output.astype(jnp.bfloat16), grads[0], grads[1], grads[2], grads[3], grads[4], grads[5], grads[6], grads[7], grads[8], grads[9], grads[10], grads[11])
```

```python
import jax
import jax.numpy as jnp
from jax import lax
from jax.sharding import PartitionSpec as P

H = 12
HD = 64


highest = lax.Precision.HIGHEST


def norm_mod(inputs, gain, shift, scale):
    center = inputs - jnp.mean(inputs, axis=-1, keepdims=True)
    spread = jnp.mean(center * center, axis=-1, keepdims=True)
    return center * lax.rsqrt(spread + 1e-05) * gain * (1.0 + scale) + shift


def tables(positions, head_dim):
    half_dim = head_dim // 2
    frequency = jnp.exp(
        -jnp.log(10000.0) * (2.0 * jnp.arange(half_dim, dtype=jnp.float32) / head_dim)
    )
    angles = positions.astype(jnp.float32)[:, None] * frequency[None, :]
    return (jnp.cos(angles)[:, None, :], jnp.sin(angles)[:, None, :])


def rotate(heads_in, cosine, sine_table):
    half_dim = heads_in.shape[-1] // 2
    lower_half = heads_in[..., :half_dim]
    upper_half = heads_in[..., half_dim:]
    return jnp.concatenate(
        [
            lower_half * cosine - upper_half * sine_table,
            upper_half * cosine + lower_half * sine_table,
        ],
        -1,
    )


def gelu_tanh(inputs):
    return jax.nn.gelu(inputs, approximate=True)


def outer_sum(left, right):
    return lax.dot_general(
        left, right, (((0,), (0,)), ((), ())), preferred_element_type=jnp.float32
    )


def back_mult(left, right):
    return lax.dot_general(
        left, right, (((1,), (1,)), ((), ())), preferred_element_type=jnp.float32
    )


def swap_halves(block):
    count = lax.axis_size("dp") * lax.axis_size("seq")
    target = {1: 2, 2: 1}
    perm = [(i, i - i % 4 + target.get(i % 4, i % 4)) for i in range(count)]
    return lax.ppermute(block, ("dp", "seq"), perm)


def swap_bit(block, bit):
    return lax.ppermute(block, "dp", [(i, i ^ bit) for i in range(lax.axis_size("dp"))])


def swap_cores(block):
    return swap_bit(block, 1)


def swap_seq(block):
    return lax.ppermute(block, "seq", [(0, 1), (1, 0)])


def dp_bits():
    bits, bit = [], 1
    while bit < lax.axis_size("dp"):
        bits.append(bit)
        bit *= 2
    return bits


def pick(block, axis, index):
    return lax.dynamic_index_in_dim(block, index, axis, keepdims=False)


def scatter_sum(matrix, seq_first):
    dp_size = lax.axis_size("dp")
    dp_rank = lax.axis_index("dp")
    seq_rank = lax.axis_index("seq")
    rows, columns = matrix.shape
    own = rows // dp_size
    low = jnp.bfloat16
    block = matrix.astype(low).reshape(dp_size, own, columns)

    def by_bit(block, bit, done):
        mine = (dp_rank // bit) % 2
        count, rest, width = block.shape
        inner = 1
        low_bit = 1
        while low_bit < bit:
            if low_bit not in done:
                inner *= 2
            low_bit *= 2
        split = block.reshape(count // (2 * inner), 2, inner, rest, width)
        got = swap_bit(pick(split, 1, 1 - mine), bit)
        kept = pick(split, 1, mine)
        total = kept.astype(jnp.float32) + got.astype(jnp.float32)
        return total.astype(low).reshape(count // 2, rest, width)

    block = by_bit(block, 1, [])
    done = [1]
    if seq_first:
        count, rest, width = block.shape
        split = block.reshape(count, 2, rest // 2, width)
        got = swap_seq(pick(split, 1, 1 - seq_rank))
        total = pick(split, 1, seq_rank).astype(jnp.float32) + got.astype(jnp.float32)
        block = total.astype(low)
    for bit in dp_bits()[1:]:
        block = by_bit(block, bit, done)
        done.append(bit)
    block = block[0]
    got = swap_seq(block)
    if seq_first:
        first = jnp.where(seq_rank == 0, block, got)
        second = jnp.where(seq_rank == 0, got, block)
        return jnp.concatenate([first, second], axis=0).astype(jnp.float32)
    return block.astype(jnp.float32) + got.astype(jnp.float32)


def share_small(per_sequence, cond, summed):
    dp_rank = lax.axis_index("dp")
    seq_rank = lax.axis_index("seq")
    sizes = [part.shape[0] for part in summed]
    totals = jnp.concatenate(summed)
    joined = jnp.concatenate([per_sequence[0], totals])
    joined = joined + swap_cores(joined)
    width = per_sequence.shape[1]
    gathered = jnp.concatenate([joined[:width], cond[0]])[None]
    totals = joined[width:]

    def double(gathered, totals, mine, move):
        count = gathered.shape[0]
        sent = jnp.concatenate([gathered.reshape(-1), totals])
        got = move(sent)
        theirs = got[: gathered.size].reshape(gathered.shape)
        first = jnp.where(mine == 0, gathered, theirs)
        second = jnp.where(mine == 0, theirs, gathered)
        return jnp.concatenate([first, second], axis=0), totals + got[gathered.size :]

    gathered, totals = double(gathered, totals, seq_rank, swap_seq)
    for bit in dp_bits()[1:]:
        gathered, totals = double(
            gathered, totals, (dp_rank // bit) % 2, lambda sent, bit=bit: swap_bit(sent, bit)
        )
    parts, start = [], 0
    for size in sizes:
        parts.append(totals[start : start + size])
        start += size
    return gathered[:, :width], gathered[:, width:], parts


def per_device(
    tokens,
    cotangent,
    time_index,
    step_table,
    first_gain,
    attn_qkv,
    attn_out,
    second_gain,
    mlp_up,
    up_bias,
    mlp_down,
    down_bias,
    ada_weight,
    ada_bias,
):
    rows_here, pos_here, model_width = tokens.shape
    head_count = H
    head_dim = HD
    seq_length = pos_here * lax.axis_size("seq")
    scale_factor = head_dim ** (-0.5)
    flat_rows = rows_here * pos_here
    dp_rank = lax.axis_index("dp")
    core = dp_rank % 2
    own_cond, silu_back = jax.vjp(
        jax.nn.silu, lax.dynamic_slice_in_dim(step_table, time_index[0], 1, axis=0)
    )
    tokens = swap_halves(tokens)
    cotangent = swap_halves(cotangent)
    time_index = swap_halves(time_index)
    embedded = lax.dynamic_slice_in_dim(step_table, time_index[0], 1, axis=0)
    cond = jax.nn.silu(embedded)
    ada_float = ada_weight.astype(jnp.float32)
    modulation = jnp.dot(cond, ada_float, precision=highest) + ada_bias.astype(jnp.float32)
    blocks = [
        modulation[:, None, index * model_width : (index + 1) * model_width] for index in range(6)
    ]
    shift1, scale1, gate1, shift2, scale2, gate2 = blocks
    inputs_f = tokens.astype(jnp.float32)
    normed, norm_back = jax.vjp(norm_mod, inputs_f, first_gain.astype(jnp.float32), shift1, scale1)
    normed_low = normed.astype(jnp.bfloat16).reshape(flat_rows, model_width)
    projected = jnp.dot(normed_low, attn_qkv, preferred_element_type=jnp.float32).reshape(
        rows_here, pos_here, 3 * model_width
    )
    positions = core * pos_here + jnp.arange(pos_here, dtype=jnp.int32)
    cosine, sine_table = tables(positions, head_dim)

    def turned(block):
        return rotate(
            block.reshape(rows_here, pos_here, head_count, head_dim), cosine, sine_table
        ).reshape(rows_here, pos_here, model_width)

    def unturned(block):
        return rotate(
            block.reshape(rows_here, pos_here, head_count, head_dim), cosine, -sine_table
        ).reshape(rows_here, pos_here, model_width)

    query_low = turned(projected[..., :model_width]).astype(jnp.bfloat16)
    keys_low = turned(projected[..., model_width : 2 * model_width]).astype(jnp.bfloat16)
    values_low = projected[..., 2 * model_width :].astype(jnp.bfloat16)
    all_keys = jnp.concatenate([keys_low, swap_cores(keys_low)], axis=1)
    all_values = jnp.concatenate([values_low, swap_cores(values_low)], axis=1)
    query_heads = query_low.reshape(rows_here, pos_here, head_count, head_dim)

    def scored(key_block):
        key_heads = key_block.reshape(rows_here, seq_length, head_count, head_dim)
        return (
            jnp.einsum(
                "bqhd,bkhd->bhqk", query_heads, key_heads, preferred_element_type=jnp.float32
            )
            * scale_factor
        )

    scores = scored(all_keys)
    top_score = jnp.max(scores, axis=-1, keepdims=True)
    totals = jnp.sum(jnp.exp(scores - top_score), axis=-1, keepdims=True)
    log_total = top_score + jnp.log(totals)
    probs_low = jnp.exp(scores - log_total).astype(jnp.bfloat16)
    value_heads = all_values.reshape(rows_here, seq_length, head_count, head_dim)
    attended = jnp.einsum(
        "bhqk,bkhd->bqhd", probs_low, value_heads, preferred_element_type=jnp.float32
    )
    attended_low = attended.reshape(flat_rows, model_width).astype(jnp.bfloat16)
    branch = jnp.dot(attended_low, attn_out, preferred_element_type=jnp.float32).reshape(
        rows_here, pos_here, model_width
    )
    middle = inputs_f + gate1 * branch
    normed2, norm2_back = jax.vjp(norm_mod, middle, second_gain.astype(jnp.float32), shift2, scale2)
    normed2_low = normed2.astype(jnp.bfloat16).reshape(flat_rows, model_width)
    pre_act = jnp.dot(normed2_low, mlp_up, preferred_element_type=jnp.float32) + up_bias.astype(
        jnp.float32
    )
    activated, gelu_back = jax.vjp(gelu_tanh, pre_act)
    activated_low = activated.astype(jnp.bfloat16)
    ffn_out = (
        jnp.dot(activated_low, mlp_down, preferred_element_type=jnp.float32)
        + down_bias.astype(jnp.float32)
    ).reshape(rows_here, pos_here, model_width)
    mixed = (middle + gate2 * ffn_out).astype(jnp.bfloat16)
    grad_out = cotangent.astype(jnp.float32)
    d_gate2 = jnp.sum(grad_out * ffn_out, axis=1)
    d_ffn = (gate2 * grad_out).astype(jnp.bfloat16).reshape(flat_rows, model_width)
    down_bias_grad = jnp.sum(d_ffn, axis=0, dtype=jnp.float32)
    mlp_down_grad = outer_sum(activated_low, d_ffn)
    d_activated = back_mult(d_ffn, mlp_down)
    (d_pre_f,) = gelu_back(d_activated)
    d_pre = d_pre_f.astype(jnp.bfloat16)
    up_bias_grad = jnp.sum(d_pre, axis=0, dtype=jnp.float32)
    mlp_up_grad = outer_sum(normed2_low, d_pre)
    d_normed2 = back_mult(d_pre, mlp_up).reshape(rows_here, pos_here, model_width)
    d_middle_norm, second_gain_grad, d_shift2, d_scale2 = norm2_back(d_normed2)
    d_middle = grad_out + d_middle_norm
    d_gate1 = jnp.sum(d_middle * branch, axis=1)
    d_branch = (gate1 * d_middle).astype(jnp.bfloat16).reshape(flat_rows, model_width)
    attn_out_grad = outer_sum(attended_low, d_branch)
    d_attended = (
        back_mult(d_branch, attn_out)
        .astype(jnp.bfloat16)
        .reshape(rows_here, pos_here, head_count, head_dim)
    )
    back_keys, back_values = (all_keys, all_values)
    scores_again = scored(back_keys)
    probs = jnp.exp(scores_again - log_total)
    probs_again = probs.astype(jnp.bfloat16)
    back_value_heads = back_values.reshape(rows_here, seq_length, head_count, head_dim)
    back_key_heads = back_keys.reshape(rows_here, seq_length, head_count, head_dim)
    d_probs = jnp.einsum(
        "bqhd,bkhd->bhqk", d_attended, back_value_heads, preferred_element_type=jnp.float32
    )
    delta_sum = jnp.sum(probs * d_probs, axis=-1, keepdims=True)
    d_scores = (probs * (d_probs - delta_sum)).astype(jnp.bfloat16)
    d_values_all = jnp.einsum(
        "bhqk,bqhd->bkhd", probs_again, d_attended, preferred_element_type=jnp.float32
    )
    d_query = (
        jnp.einsum("bhqk,bkhd->bqhd", d_scores, back_key_heads, preferred_element_type=jnp.float32)
        * scale_factor
    )
    d_keys_all = (
        jnp.einsum("bhqk,bqhd->bkhd", d_scores, query_heads, preferred_element_type=jnp.float32)
        * scale_factor
    )
    def from_pair(block):
        block = block.reshape(rows_here, seq_length, model_width)
        theirs = swap_cores(block[:, pos_here:].astype(jnp.bfloat16))
        return block[:, :pos_here] + theirs.astype(jnp.float32)

    d_keys_own = from_pair(d_keys_all)
    d_values_own = from_pair(d_values_all)
    d_projected = (
        jnp.concatenate(
            [
                unturned(d_query.reshape(rows_here, pos_here, model_width)),
                unturned(d_keys_own),
                d_values_own,
            ],
            -1,
        )
        .astype(jnp.bfloat16)
        .reshape(flat_rows, 3 * model_width)
    )
    attn_qkv_grad = outer_sum(normed_low, d_projected)
    d_normed = back_mult(d_projected, attn_qkv).reshape(rows_here, pos_here, model_width)
    d_inputs, first_gain_grad, d_shift1, d_scale1 = norm_back(d_normed)
    tokens_grad = d_middle + d_inputs
    d_modulation = jnp.concatenate(
        [d_shift1[:, 0], d_scale1[:, 0], d_gate1, d_shift2[:, 0], d_scale2[:, 0], d_gate2], -1
    )
    d_mod_all, cond_all, sums = share_small(
        d_modulation,
        cond,
        (first_gain_grad, second_gain_grad, up_bias_grad, down_bias_grad),
    )
    ada_bias_grad = jnp.sum(d_mod_all, axis=0)
    own_columns = d_mod_all.shape[1] // lax.axis_size("dp")
    mine = lax.dynamic_slice_in_dim(d_mod_all, dp_rank * own_columns, own_columns, axis=1)
    ada_weight_grad = lax.dot_general(
        cond_all, mine, (((0,), (0,)), ((), ())), precision=highest
    )
    d_mod_own = lax.dynamic_slice_in_dim(d_mod_all, dp_rank, 1, axis=0)
    (cond_grad,) = silu_back(jnp.dot(d_mod_own, ada_float.T, precision=highest))
    half = attn_qkv_grad.shape[1] // 2
    qkv_rows = jnp.concatenate(
        [
            scatter_sum(attn_qkv_grad[:, :half], False),
            scatter_sum(attn_qkv_grad[:, half:], True),
        ],
        axis=1,
    )
    return (
        swap_halves(mixed),
        swap_halves(tokens_grad.astype(jnp.bfloat16)).astype(jnp.float32),
        cond_grad,
        sums[0],
        qkv_rows,
        scatter_sum(attn_out_grad, True),
        sums[1],
        scatter_sum(mlp_up_grad, False),
        sums[2],
        scatter_sum(mlp_down_grad, True),
        sums[3],
        ada_weight_grad,
        ada_bias_grad,
    )


def solution(mesh):
    placed = (
        P("dp", "seq", None),
        P("dp", "seq", None),
        P("dp"),
        P(),
        P(),
        P(),
        P(),
        P(),
        P(),
        P(),
        P(),
        P(),
        P(),
        P(),
    )
    return jax.shard_map(
        per_device,
        mesh=mesh,
        in_specs=placed,
        out_specs=(
            P("dp", "seq", None),
            P("dp", "seq", None),
            P("dp", None),
            P(),
            P("dp", None),
            P("dp", None),
            P(),
            P("dp", None),
            P(),
            P("dp", None),
            P(),
            P(None, "dp"),
            P(),
        ),
        check_vma=False,
    )
```

```python
import jax
import jax.numpy as jnp
from jax import lax
from jax.experimental import pallas as pl
from jax.experimental.pallas import tpu as pltpu
from jax.sharding import PartitionSpec as P

HD = 64


highest = lax.Precision.HIGHEST


def tables(positions):
    half_dim = HD // 2
    frequency = jnp.exp(
        -jnp.log(10000.0) * (2.0 * jnp.arange(half_dim, dtype=jnp.float32) / HD)
    )
    angles = positions.astype(jnp.float32)[:, None] * frequency[None, :]
    cosine, sine = jnp.cos(angles), jnp.sin(angles)
    return (
        jnp.concatenate([cosine] * 4, axis=1),
        jnp.concatenate([-sine, sine, -sine, sine], axis=1),
    )


def full(shape):
    return pl.BlockSpec(shape, lambda step: (0,) * len(shape))


def columns(rows, width, first=0):
    return pl.BlockSpec((rows, width), lambda step: (0, step + first))


def shaped(shape, kind):
    return jax.ShapeDtypeStruct(shape, kind)


def kernel_call(body, steps, in_specs, out_specs, out_shape, scratch, flops, moved):
    return pl.pallas_call(
        body,
        grid=(steps,),
        in_specs=in_specs,
        out_specs=out_specs,
        out_shape=out_shape,
        scratch_shapes=scratch,
        compiler_params=pltpu.CompilerParams(
            dimension_semantics=("arbitrary",), vmem_limit_bytes=56 * 1024 * 1024
        ),
        cost_estimate=pl.CostEstimate(flops=flops, bytes_accessed=moved, transcendentals=0),
    )


def dot(left, right, left_axis=1, right_axis=0):
    return lax.dot_general(
        left,
        right,
        (((left_axis,), (right_axis,)), ((), ())),
        preferred_element_type=jnp.float32,
    )


def normalized(inputs):
    center = inputs - jnp.mean(inputs, axis=-1, keepdims=True)
    inverse = lax.rsqrt(jnp.mean(center * center, axis=-1, keepdims=True) + 1e-05)
    return center * inverse, inverse


def norm_back(back, hat, inverse, factor):
    scaled = back * factor
    return inverse * (
        scaled
        - jnp.mean(scaled, axis=-1, keepdims=True)
        - hat * jnp.mean(scaled * hat, axis=-1, keepdims=True)
    )


def column_sum(values):
    return jnp.sum(values, axis=0, keepdims=True)


SHIFT1, SCALE1, GATE1, SHIFT2, SCALE2, GATE2, GAIN1, GAIN2 = range(8)


def row(ref, index):
    return ref[index : index + 1, :]


def rotate_lanes(values, cosine, sine):
    lane = lax.broadcasted_iota(jnp.int32, cosine.shape, 1)
    lower = (lane % HD) < HD // 2
    parts = []
    for start in range(0, values.shape[1], 128):
        part = values[:, start : start + 128]
        other = jnp.where(lower, pltpu.roll(part, 128 - HD // 2, 1), pltpu.roll(part, HD // 2, 1))
        parts.append(part * cosine + other * sine)
    return jnp.concatenate(parts, axis=1)


COLUMNS = 384


def key_value_body(tokens, mods, weight, cosine, sine, normed, out):
    step = pl.program_id(0)
    turned_steps = pl.num_programs(0) // 2

    @pl.when(step == 0)
    def _():
        hat, _ = normalized(tokens[...].astype(jnp.float32))
        value = hat * row(mods, GAIN1) * (1.0 + row(mods, SCALE1)) + row(mods, SHIFT1)
        normed[...] = value.astype(jnp.bfloat16)

    @pl.when(step < turned_steps)
    def _():
        value = dot(normed[...], weight[...])
        out[...] = rotate_lanes(value, cosine[...], sine[...]).astype(jnp.bfloat16)

    @pl.when(step >= turned_steps)
    def _():
        out[...] = dot(normed[...], weight[...]).astype(jnp.bfloat16)


def project_key_value(tokens, mods, weight, cosine, sine):
    rows, width = tokens.shape
    first = width // COLUMNS
    return kernel_call(
        key_value_body,
        2 * first,
        [
            full((rows, width)),
            full((8, width)),
            columns(width, COLUMNS, first),
            full((rows, 128)),
            full((rows, 128)),
        ],
        [full((rows, width)), columns(rows, COLUMNS)],
        [shaped((rows, width), jnp.bfloat16), shaped((rows, 2 * width), jnp.bfloat16)],
        [],
        4 * rows * width * width,
        8 * width * width,
    )(tokens, mods, weight, cosine, sine)


def query_body(normed, weight, cosine, sine, out):
    value = dot(normed[...], weight[...])
    out[...] = rotate_lanes(value, cosine[...], sine[...]).astype(jnp.bfloat16)


def project_query(normed, weight, cosine, sine):
    rows, width = normed.shape
    return kernel_call(
        query_body,
        width // COLUMNS,
        [full((rows, width)), columns(width, COLUMNS), full((rows, 128)), full((rows, 128))],
        columns(rows, COLUMNS),
        shaped((rows, width), jnp.bfloat16),
        [],
        2 * rows * width * width,
        4 * width * width,
    )(normed, weight, cosine, sine)


def head_mask(shape, head, value):
    lane = lax.broadcasted_iota(jnp.int32, shape, 1)
    return jnp.where(lane // HD == head, value, 0.0).astype(jnp.bfloat16)


def attend_body(query, keys1, values1, keys2, values2, out, log_total):
    rows = query.shape[0]
    turned1 = values1[...].T
    turned2 = values2[...].T
    parts = []
    for head in range(2):
        own = query[...] * head_mask((rows, 128), head, HD ** (-0.5))
        scores1 = dot(keys1[...], own, 1, 1)
        scores2 = dot(keys2[...], own, 1, 1)
        top = jnp.maximum(
            jnp.max(scores1, axis=0, keepdims=True), jnp.max(scores2, axis=0, keepdims=True)
        )
        exps1 = jnp.exp(scores1 - top)
        exps2 = jnp.exp(scores2 - top)
        total = column_sum(exps1) + column_sum(exps2)
        lanes = slice(head * HD, (head + 1) * HD)
        mixed = dot(turned1[lanes], exps1.astype(jnp.bfloat16)) + dot(
            turned2[lanes], exps2.astype(jnp.bfloat16)
        )
        parts.append(mixed / total)
        log_total[0, head : head + 1, :] = top + jnp.log(total)
    out[...] = jnp.concatenate(parts, axis=0).T.astype(jnp.bfloat16)


def attend(query, own, peer):
    rows, width = query.shape
    pairs = width // 128
    return kernel_call(
        attend_body,
        pairs,
        [
            columns(rows, 128),
            columns(rows, 128),
            columns(rows, 128, pairs),
            columns(rows, 128),
            columns(rows, 128, pairs),
        ],
        [columns(rows, 128), pl.BlockSpec((1, 2, rows), lambda step: (step, 0, 0))],
        [shaped((rows, width), jnp.bfloat16), shaped((pairs, 2, rows), jnp.float32)],
        [],
        16 * rows * rows * width,
        8 * rows * width,
    )(query, own, own, peer, peer)


def attend_back_body(query, keys, values, grad, attended, log_total, *refs):
    if len(refs) == 4:
        before, d_query, d_keys, d_values = refs
    else:
        before, (d_query, d_keys, d_values) = None, refs
    rows = query.shape[0]
    keys_turned = keys[...].T
    product = (grad[...].astype(jnp.float32) * attended[...].astype(jnp.float32)).T
    parts = []
    keys_sum = values_sum = None
    for head in range(2):
        lanes = slice(head * HD, (head + 1) * HD)
        own = query[...] * head_mask((rows, 128), head, HD ** (-0.5))
        own_grad = grad[...] * head_mask((rows, 128), head, 1.0)
        delta = column_sum(product[lanes])
        scores = dot(keys[...], own, 1, 1)
        probs = jnp.exp(scores - log_total[0, head : head + 1, :])
        d_probs = dot(values[...], own_grad, 1, 1)
        d_scores = (probs * (d_probs - delta)).astype(jnp.bfloat16)
        values_part = dot(probs.astype(jnp.bfloat16), own_grad)
        keys_part = dot(d_scores, own)
        values_sum = values_part if values_sum is None else values_sum + values_part
        keys_sum = keys_part if keys_sum is None else keys_sum + keys_part
        parts.append(dot(keys_turned[lanes], d_scores))
    turned = jnp.concatenate(parts, axis=0).T * HD ** (-0.5)
    d_query[...] = turned if before is None else turned + before[...]
    d_keys[...] = keys_sum.astype(d_keys.dtype)
    d_values[...] = values_sum.astype(d_values.dtype)


def attend_back(query, pair, grad, attended, log_total, before, kind):
    rows, width = query.shape
    pairs = width // 128
    block = columns(rows, 128)
    extra = [] if before is None else [before]
    return kernel_call(
        attend_back_body,
        pairs,
        [
            block,
            block,
            columns(rows, 128, pairs),
            block,
            block,
            pl.BlockSpec((1, 2, rows), lambda step: (step, 0, 0)),
        ]
        + [block] * len(extra),
        [block, block, block],
        [
            shaped((rows, width), jnp.float32),
            shaped((rows, width), kind),
            shaped((rows, width), kind),
        ],
        [],
        20 * rows * rows * width,
        20 * rows * width,
    )(query, pair, pair, grad, attended, log_total, *extra)


def up_body(
    attended, tokens, cotangent, mods, out_weight, up_weight, bias,
    branch, middle, normed, d_ffn, activated, slope, down_grad,
):
    @pl.when(pl.program_id(0) == 0)
    def _():
        mixed = dot(attended[...], out_weight[...])
        branch[...] = mixed
        value = tokens[...].astype(jnp.float32) + row(mods, GATE1) * mixed
        middle[...] = value
        hat, _ = normalized(value)
        value = hat * row(mods, GAIN2) * (1.0 + row(mods, SCALE2)) + row(mods, SHIFT2)
        normed[...] = value.astype(jnp.bfloat16)
        d_ffn[...] = (row(mods, GATE2) * cotangent[...].astype(jnp.float32)).astype(jnp.bfloat16)

    pre = dot(normed[...], up_weight[...]) + bias[...]
    root = 0.7978845608028654
    square = pre * pre
    bent = jnp.tanh(root * pre * (1.0 + 0.044715 * square))
    half = 0.5 + 0.5 * bent
    slope[...] = (
        half + 0.5 * root * pre * (1.0 - bent * bent) * (1.0 + 0.134145 * square)
    ).astype(jnp.bfloat16)
    low = (pre * half).astype(jnp.bfloat16)
    activated[...] = low
    down_grad[...] = dot(low, d_ffn[...], 0, 0).astype(jnp.bfloat16)


def up_layer(attended, tokens, cotangent, mods, out_weight, up_weight, bias):
    rows, width = tokens.shape
    hidden = up_weight.shape[1]
    block = full((rows, width))
    tile = 512
    return kernel_call(
        up_body,
        hidden // tile,
        [
            block,
            block,
            block,
            full((8, width)),
            full((width, width)),
            columns(width, tile),
            columns(1, tile),
        ],
        [
            block,
            block,
            block,
            block,
            columns(rows, tile),
            columns(rows, tile),
            pl.BlockSpec((tile, width), lambda step: (step, 0)),
        ],
        [
            shaped((rows, width), jnp.float32),
            shaped((rows, width), jnp.float32),
            shaped((rows, width), jnp.bfloat16),
            shaped((rows, width), jnp.bfloat16),
            shaped((rows, hidden), jnp.bfloat16),
            shaped((rows, hidden), jnp.bfloat16),
            shaped((hidden, width), jnp.bfloat16),
        ],
        [],
        4 * rows * width * hidden + 2 * rows * width * width,
        8 * rows * hidden + 4 * hidden * width,
    )(attended, tokens, cotangent, mods, out_weight, up_weight, bias)


def up_back_body(d_ffn, normed, down_weight, slope, d_pre, up_grad, bias_grad):
    value = dot(d_ffn[...], down_weight[...], 1, 1) * slope[...].astype(jnp.float32)
    low = value.astype(jnp.bfloat16)
    d_pre[...] = low
    bias_grad[...] = column_sum(value)
    up_grad[...] = dot(normed[...], low, 0, 0).astype(jnp.bfloat16)


def up_back(d_ffn, normed, down_weight, slope):
    rows, width = normed.shape
    hidden = down_weight.shape[0]
    tile = 512
    return kernel_call(
        up_back_body,
        hidden // tile,
        [
            full((rows, width)),
            full((rows, width)),
            pl.BlockSpec((tile, width), lambda step: (step, 0)),
            columns(rows, tile),
        ],
        [columns(rows, tile), columns(width, tile), columns(1, tile)],
        [
            shaped((rows, hidden), jnp.bfloat16),
            shaped((width, hidden), jnp.bfloat16),
            shaped((1, hidden), jnp.float32),
        ],
        [],
        4 * rows * width * hidden,
        8 * rows * hidden + 4 * hidden * width,
    )(d_ffn, normed, down_weight, slope)


def down_body(
    activated, d_pre, down_weight, up_weight, cotangent, d_ffn, middle, branch, attended,
    mods, out_weight, bias,
    mixed, d_middle, d_attended, out_grad, sums, forward, backward,
):
    step = pl.program_id(0)

    @pl.when(step == 0)
    def _():
        forward[...] = jnp.zeros_like(forward)
        backward[...] = jnp.zeros_like(backward)

    forward[...] += dot(activated[...], down_weight[...])
    backward[...] += dot(d_pre[...], up_weight[...], 1, 1)

    @pl.when(step == pl.num_programs(0) - 1)
    def _():
        ffn = forward[...] + bias[...]
        value = middle[...]
        grad = cotangent[...].astype(jnp.float32)
        mixed[...] = (value + row(mods, GATE2) * ffn).astype(jnp.bfloat16)
        back = backward[...]
        hat, inverse = normalized(value)
        d_value = grad + norm_back(
            back, hat, inverse, row(mods, GAIN2) * (1.0 + row(mods, SCALE2))
        )
        d_middle[...] = d_value
        d_branch = (row(mods, GATE1) * d_value).astype(jnp.bfloat16)
        out_grad[...] = dot(attended[...], d_branch, 0, 0).astype(jnp.bfloat16)
        d_attended[...] = dot(d_branch, out_weight[...], 1, 1).astype(jnp.bfloat16)
        sums[0:1, :] = column_sum(back)
        sums[1:2, :] = column_sum(back * hat)
        sums[2:3, :] = column_sum(d_value * branch[...])
        sums[3:4, :] = column_sum(grad * ffn)
        sums[4:5, :] = column_sum(d_ffn[...].astype(jnp.float32))
        sums[5:8, :] = jnp.zeros_like(sums[5:8, :])


def down_layer(
    activated, d_pre, down_weight, up_weight, cotangent, d_ffn, middle, branch, attended,
    mods, out_weight, bias,
):
    rows, width = middle.shape
    hidden = down_weight.shape[0]
    tile = 512
    block = full((rows, width))
    return kernel_call(
        down_body,
        hidden // tile,
        [
            columns(rows, tile),
            columns(rows, tile),
            pl.BlockSpec((tile, width), lambda step: (step, 0)),
            columns(width, tile),
            block,
            block,
            block,
            block,
            block,
            full((8, width)),
            full((width, width)),
            full((1, width)),
        ],
        [block, block, block, full((width, width)), full((8, width))],
        [
            shaped((rows, width), jnp.bfloat16),
            shaped((rows, width), jnp.float32),
            shaped((rows, width), jnp.bfloat16),
            shaped((width, width), jnp.bfloat16),
            shaped((8, width), jnp.float32),
        ],
        [pltpu.VMEM((rows, width), jnp.float32), pltpu.VMEM((rows, width), jnp.float32)],
        4 * rows * width * hidden + 4 * rows * width * width,
        4 * rows * hidden + 4 * hidden * width,
    )(
        activated, d_pre, down_weight, up_weight, cotangent, d_ffn, middle, branch, attended,
        mods, out_weight, bias,
    )


def projected_back_body(
    d_query, d_keys, d_values, peer_keys, peer_values, normed, cosine, sine, d_projected, grad
):
    step = pl.program_id(0)
    per_part = pl.num_programs(0) // 3

    def finish(low):
        d_projected[...] = low
        grad[...] = dot(normed[...], low, 0, 0).astype(jnp.bfloat16)

    @pl.when(step < per_part)
    def _():
        finish(rotate_lanes(d_query[...], cosine[...], -sine[...]).astype(jnp.bfloat16))

    @pl.when((step >= per_part) & (step < 2 * per_part))
    def _():
        value = d_keys[...] + peer_keys[...].astype(jnp.float32)
        finish(rotate_lanes(value, cosine[...], -sine[...]).astype(jnp.bfloat16))

    @pl.when(step >= 2 * per_part)
    def _():
        value = d_values[...] + peer_values[...].astype(jnp.float32)
        finish(value.astype(jnp.bfloat16))


def projected_back(d_query, d_keys, d_values, peer_keys, peer_values, normed, cosine, sine):
    rows, width = normed.shape
    per_part = width // COLUMNS

    def part(index):
        return pl.BlockSpec(
            (rows, COLUMNS),
            lambda step: (0, jnp.clip(step - index * per_part, 0, per_part - 1)),
        )

    return kernel_call(
        projected_back_body,
        3 * per_part,
        [
            part(0),
            part(1),
            part(2),
            part(1),
            part(2),
            full((rows, width)),
            full((rows, 128)),
            full((rows, 128)),
        ],
        [columns(rows, COLUMNS), columns(width, COLUMNS)],
        [shaped((rows, 3 * width), jnp.bfloat16), shaped((width, 3 * width), jnp.bfloat16)],
        [],
        6 * rows * width * width,
        22 * rows * width,
    )(d_query, d_keys, d_values, peer_keys, peer_values, normed, cosine, sine)


def tokens_back_body(d_projected, weight, tokens, d_middle, mods, out, sums, total):
    step = pl.program_id(0)

    @pl.when(step == 0)
    def _():
        total[...] = jnp.zeros_like(total)

    total[...] += dot(d_projected[...], weight[...], 1, 1)

    @pl.when(step == pl.num_programs(0) - 1)
    def _():
        back = total[...]
        hat, inverse = normalized(tokens[...].astype(jnp.float32))
        factor = row(mods, GAIN1) * (1.0 + row(mods, SCALE1))
        out[...] = (d_middle[...] + norm_back(back, hat, inverse, factor)).astype(jnp.bfloat16)
        sums[0:1, :] = column_sum(back)
        sums[1:2, :] = column_sum(back * hat)
        sums[2:8, :] = jnp.zeros_like(sums[2:8, :])


def tokens_back(d_projected, weight, tokens, d_middle, mods):
    rows, width = tokens.shape
    block = full((rows, width))
    return kernel_call(
        tokens_back_body,
        3 * width // COLUMNS,
        [columns(rows, COLUMNS), columns(width, COLUMNS), block, block, full((8, width))],
        [block, full((8, width))],
        [shaped((rows, width), jnp.bfloat16), shaped((8, width), jnp.float32)],
        [pltpu.VMEM((rows, width), jnp.float32)],
        6 * rows * width * width,
        6 * width * width + 10 * rows * width,
    )(d_projected, weight, tokens, d_middle, mods)


def swap_halves(block):
    count = lax.axis_size("dp") * lax.axis_size("seq")
    target = {1: 2, 2: 1}
    perm = [(i, i - i % 4 + target.get(i % 4, i % 4)) for i in range(count)]
    return lax.ppermute(block, ("dp", "seq"), perm)


def swap_bit(block, bit):
    return lax.ppermute(block, "dp", [(i, i ^ bit) for i in range(lax.axis_size("dp"))])


def swap_cores(block):
    return swap_bit(block, 1)


def swap_seq(block):
    return lax.ppermute(block, "seq", [(0, 1), (1, 0)])


def dp_bits():
    bits, bit = [], 1
    while bit < lax.axis_size("dp"):
        bits.append(bit)
        bit *= 2
    return bits


def pick(block, axis, index):
    return lax.dynamic_index_in_dim(block, index, axis, keepdims=False)


def scatter_sum(matrix, seq_first):
    dp_size = lax.axis_size("dp")
    dp_rank = lax.axis_index("dp")
    seq_rank = lax.axis_index("seq")
    rows, columns = matrix.shape
    own = rows // dp_size
    low = jnp.bfloat16
    block = matrix.reshape(dp_size, own, columns)

    def by_bit(block, bit, done):
        mine = (dp_rank // bit) % 2
        count, rest, width = block.shape
        inner = 1
        low_bit = 1
        while low_bit < bit:
            if low_bit not in done:
                inner *= 2
            low_bit *= 2
        split = block.reshape(count // (2 * inner), 2, inner, rest, width)
        got = swap_bit(pick(split, 1, 1 - mine), bit)
        kept = pick(split, 1, mine)
        total = kept.astype(jnp.float32) + got.astype(jnp.float32)
        return total.astype(low).reshape(count // 2, rest, width)

    block = by_bit(block, 1, [])
    done = [1]
    if seq_first:
        count, rest, width = block.shape
        split = block.reshape(count, 2, rest // 2, width)
        got = swap_seq(pick(split, 1, 1 - seq_rank))
        total = pick(split, 1, seq_rank).astype(jnp.float32) + got.astype(jnp.float32)
        block = total.astype(low)
    for bit in dp_bits()[1:]:
        block = by_bit(block, bit, done)
        done.append(bit)
    block = block[0]
    got = swap_seq(block)
    if seq_first:
        first = jnp.where(seq_rank == 0, block, got)
        second = jnp.where(seq_rank == 0, got, block)
        return jnp.concatenate([first, second], axis=0).astype(jnp.float32)
    return block.astype(jnp.float32) + got.astype(jnp.float32)


def share_small(per_sequence, cond, summed):
    dp_rank = lax.axis_index("dp")
    seq_rank = lax.axis_index("seq")
    sizes = [part.shape[0] for part in summed]
    totals = jnp.concatenate(summed)
    joined = jnp.concatenate([per_sequence[0], totals])
    joined = joined + swap_cores(joined)
    width = per_sequence.shape[1]
    gathered = jnp.concatenate([joined[:width], cond[0]])[None]
    totals = joined[width:]

    def double(gathered, totals, mine, move):
        count = gathered.shape[0]
        sent = jnp.concatenate([gathered.reshape(-1), totals])
        got = move(sent)
        theirs = got[: gathered.size].reshape(gathered.shape)
        first = jnp.where(mine == 0, gathered, theirs)
        second = jnp.where(mine == 0, theirs, gathered)
        return jnp.concatenate([first, second], axis=0), totals + got[gathered.size :]

    gathered, totals = double(gathered, totals, seq_rank, swap_seq)
    for bit in dp_bits()[1:]:
        gathered, totals = double(
            gathered, totals, (dp_rank // bit) % 2, lambda sent, bit=bit: swap_bit(sent, bit)
        )
    parts, start = [], 0
    for size in sizes:
        parts.append(totals[start : start + size])
        start += size
    return gathered[:, :width], gathered[:, width:], parts


def per_device(
    tokens,
    cotangent,
    time_index,
    step_table,
    first_gain,
    attn_qkv,
    attn_out,
    second_gain,
    mlp_up,
    up_bias,
    mlp_down,
    down_bias,
    ada_weight,
    ada_bias,
):
    rows, width = tokens.shape[1:]
    dp_rank = lax.axis_index("dp")
    core = dp_rank % 2
    own_cond, silu_back = jax.vjp(
        jax.nn.silu, lax.dynamic_slice_in_dim(step_table, time_index[0], 1, axis=0)
    )
    tokens = swap_halves(tokens[0])
    time_index = swap_halves(time_index)
    cotangent = swap_halves(cotangent[0])
    cond = jax.nn.silu(lax.dynamic_slice_in_dim(step_table, time_index[0], 1, axis=0))
    ada_float = ada_weight.astype(jnp.float32)
    modulation = jnp.dot(cond, ada_float, precision=highest) + ada_bias.astype(jnp.float32)
    gain1 = first_gain.astype(jnp.float32)
    gain2 = second_gain.astype(jnp.float32)
    mods = jnp.concatenate([modulation.reshape(6, width), gain1[None], gain2[None]])
    positions = core * rows + jnp.arange(rows, dtype=jnp.int32)
    cosine, sine = tables(positions)

    normed1, own_pair = project_key_value(tokens, mods, attn_qkv, cosine, sine)
    peer_pair = swap_cores(own_pair)
    query = project_query(normed1, attn_qkv, cosine, sine)
    attended, log_total = attend(query, own_pair, peer_pair)
    branch, middle, normed2, d_ffn, activated, slope, mlp_down_grad = up_layer(
        attended, tokens, cotangent, mods, attn_out, mlp_up, up_bias.astype(jnp.float32)[None]
    )
    d_pre, mlp_up_grad, up_bias_grad = up_back(d_ffn, normed2, mlp_down, slope)
    mixed, d_middle, d_attended, attn_out_grad, sums2 = down_layer(
        activated, d_pre, mlp_down, mlp_up, cotangent, d_ffn, middle, branch, attended,
        mods, attn_out, down_bias.astype(jnp.float32)[None],
    )
    d_query, away_keys, away_values = attend_back(
        query, peer_pair, d_attended, attended, log_total, None, jnp.bfloat16
    )
    peer_keys, peer_values = swap_cores(away_keys), swap_cores(away_values)
    d_query, d_keys, d_values = attend_back(
        query, own_pair, d_attended, attended, log_total, d_query, jnp.float32
    )
    d_projected, attn_qkv_grad = projected_back(
        d_query, d_keys, d_values, peer_keys, peer_values, normed1, cosine, sine
    )
    tokens_grad, sums1 = tokens_back(d_projected, attn_qkv, tokens, d_middle, mods)

    d_modulation = jnp.concatenate(
        [sums1[0], sums1[1] * gain1, sums2[2], sums2[0], sums2[1] * gain2, sums2[3]]
    )[None]
    first_gain_grad = sums1[1] * (1.0 + mods[SCALE1])
    second_gain_grad = sums2[1] * (1.0 + mods[SCALE2])
    d_mod_all, cond_all, sums = share_small(
        d_modulation,
        cond,
        (first_gain_grad, second_gain_grad, up_bias_grad[0], sums2[4]),
    )
    ada_bias_grad = jnp.sum(d_mod_all, axis=0)
    own_columns = d_mod_all.shape[1] // lax.axis_size("dp")
    mine = lax.dynamic_slice_in_dim(d_mod_all, dp_rank * own_columns, own_columns, axis=1)
    ada_weight_grad = lax.dot_general(
        cond_all, mine, (((0,), (0,)), ((), ())), precision=highest
    )
    d_mod_own = lax.dynamic_slice_in_dim(d_mod_all, dp_rank, 1, axis=0)
    (cond_grad,) = silu_back(jnp.dot(d_mod_own, ada_float.T, precision=highest))
    half = attn_qkv_grad.shape[1] // 2
    qkv_rows = jnp.concatenate(
        [
            scatter_sum(attn_qkv_grad[:, :half], False),
            scatter_sum(attn_qkv_grad[:, half:], True),
        ],
        axis=1,
    )
    return (
        swap_halves(mixed)[None],
        swap_halves(tokens_grad).astype(jnp.float32)[None],
        cond_grad,
        sums[0],
        qkv_rows,
        scatter_sum(attn_out_grad, True),
        sums[1],
        scatter_sum(mlp_up_grad, False),
        sums[2],
        scatter_sum(mlp_down_grad, True),
        sums[3],
        ada_weight_grad,
        ada_bias_grad,
    )


def solution(mesh):
    placed = (
        P("dp", "seq", None),
        P("dp", "seq", None),
        P("dp"),
        P(),
        P(),
        P(),
        P(),
        P(),
        P(),
        P(),
        P(),
        P(),
        P(),
        P(),
    )
    return jax.shard_map(
        per_device,
        mesh=mesh,
        in_specs=placed,
        out_specs=(
            P("dp", "seq", None),
            P("dp", "seq", None),
            P("dp", None),
            P(),
            P("dp", None),
            P("dp", None),
            P(),
            P("dp", None),
            P(),
            P("dp", None),
            P(),
            P(None, "dp"),
            P(),
        ),
        check_vma=False,
    )
```

```python
import jax
import jax.numpy as jnp
from jax import lax
from jax.experimental import pallas as pl
from jax.experimental.pallas import tpu as pltpu
from jax.sharding import PartitionSpec as P

HD = 64
LOG2E = 1.4426950408889634


highest = lax.Precision.HIGHEST


def tables(positions):
    half_dim = HD // 2
    frequency = jnp.exp(
        -jnp.log(10000.0) * (2.0 * jnp.arange(half_dim, dtype=jnp.float32) / HD)
    )
    angles = positions.astype(jnp.float32)[:, None] * frequency[None, :]
    cosine, sine = jnp.cos(angles), jnp.sin(angles)
    return (
        jnp.concatenate([cosine] * 4, axis=1),
        jnp.concatenate([-sine, sine, -sine, sine], axis=1),
    )


def full(shape):
    return pl.BlockSpec(shape, lambda step: (0,) * len(shape))


def columns(rows, width, first=0):
    return pl.BlockSpec((rows, width), lambda step: (0, step + first))


def shaped(shape, kind):
    return jax.ShapeDtypeStruct(shape, kind)


def kernel_call(body, steps, in_specs, out_specs, out_shape, scratch, flops, moved):
    return pl.pallas_call(
        body,
        grid=(steps,),
        in_specs=in_specs,
        out_specs=out_specs,
        out_shape=out_shape,
        scratch_shapes=scratch,
        compiler_params=pltpu.CompilerParams(
            dimension_semantics=("arbitrary",), vmem_limit_bytes=36 * 1024 * 1024
        ),
        cost_estimate=pl.CostEstimate(flops=flops, bytes_accessed=moved, transcendentals=0),
    )


def dot(left, right, left_axis=1, right_axis=0):
    return lax.dot_general(
        left,
        right,
        (((left_axis,), (right_axis,)), ((), ())),
        preferred_element_type=jnp.float32,
    )


def normalized(inputs):
    center = inputs - jnp.mean(inputs, axis=-1, keepdims=True)
    inverse = lax.rsqrt(jnp.mean(center * center, axis=-1, keepdims=True) + 1e-05)
    return center * inverse, inverse


def norm_back(back, hat, inverse, factor):
    scaled = back * factor
    return inverse * (
        scaled
        - jnp.mean(scaled, axis=-1, keepdims=True)
        - hat * jnp.mean(scaled * hat, axis=-1, keepdims=True)
    )


def column_sum(values):
    return jnp.sum(values, axis=0, keepdims=True)


SHIFT1, SCALE1, GATE1, SHIFT2, SCALE2, GATE2, GAIN1, GAIN2, COND = range(9)


def row(ref, index):
    return ref[index : index + 1, :]


def rotate_lanes(values, cosine, sine):
    lane = lax.broadcasted_iota(jnp.int32, cosine.shape, 1)
    lower = (lane % HD) < HD // 2
    parts = []
    for start in range(0, values.shape[1], 128):
        part = values[:, start : start + 128]
        other = jnp.where(lower, pltpu.roll(part, 128 - HD // 2, 1), pltpu.roll(part, HD // 2, 1))
        parts.append(part * cosine + other * sine)
    return jnp.concatenate(parts, axis=1)


COLUMNS = 768


def key_value_body(tokens, mods, weight, cosine, sine, normed, out):
    step = pl.program_id(0)
    turned_steps = pl.num_programs(0) // 2

    @pl.when(step == 0)
    def _():
        hat, _ = normalized(tokens[...].astype(jnp.float32))
        value = hat * row(mods, GAIN1) * (1.0 + row(mods, SCALE1)) + row(mods, SHIFT1)
        normed[...] = value.astype(jnp.bfloat16)

    @pl.when(step < turned_steps)
    def _():
        value = dot(normed[...], weight[...])
        out[...] = rotate_lanes(value, cosine[...], sine[...]).astype(jnp.bfloat16)

    @pl.when(step >= turned_steps)
    def _():
        out[...] = dot(normed[...], weight[...]).astype(jnp.bfloat16)


def project_key_value(tokens, mods, weight, cosine, sine):
    rows, width = tokens.shape
    first = width // COLUMNS
    return kernel_call(
        key_value_body,
        2 * first,
        [
            full((rows, width)),
            full((16, width)),
            columns(width, COLUMNS, first),
            full((rows, 128)),
            full((rows, 128)),
        ],
        [full((rows, width)), columns(rows, COLUMNS)],
        [shaped((rows, width), jnp.bfloat16), shaped((rows, 2 * width), jnp.bfloat16)],
        [],
        4 * rows * width * width,
        8 * width * width,
    )(tokens, mods, weight, cosine, sine)


def query_body(normed, weight, cosine, sine, out):
    value = rotate_lanes(dot(normed[...], weight[...]), cosine[...], sine[...])
    out[...] = (value * (LOG2E * HD ** (-0.5))).astype(jnp.bfloat16)


def project_query(normed, weight, cosine, sine):
    rows, width = normed.shape
    return kernel_call(
        query_body,
        width // COLUMNS,
        [full((rows, width)), columns(width, COLUMNS), full((rows, 128)), full((rows, 128))],
        columns(rows, COLUMNS),
        shaped((rows, width), jnp.bfloat16),
        [],
        2 * rows * width * width,
        4 * width * width,
    )(normed, weight, cosine, sine)


def head_mask(shape, head):
    lane = lax.broadcasted_iota(jnp.int32, shape, 1)
    return jnp.where(lane // HD == head, 1.0, 0.0).astype(jnp.bfloat16)


HEADS = 4


def head_lanes(head):
    pair, place = divmod(head, 2)
    return slice(pair * 128, (pair + 1) * 128), place, slice(place * HD, (place + 1) * HD)


def in_turn(count, first, rest):
    results = []
    ahead = first(0)
    for index in range(count):
        now = ahead
        if index + 1 < count:
            ahead = first(index + 1)
        results.append(rest(index, now))
    return results


def attend_body(query, keys1, values1, keys2, values2, out, log_total):
    rows = query.shape[0]

    def first(head):
        lanes, place, _ = head_lanes(head)
        own = query[:, lanes] * head_mask((rows, 128), place)
        return dot(keys1[:, lanes], own, 1, 1), dot(keys2[:, lanes], own, 1, 1)

    def rest(head, scores):
        lanes, place, turned = head_lanes(head)
        scores1, scores2 = scores
        top = jnp.maximum(
            jnp.max(scores1, axis=0, keepdims=True), jnp.max(scores2, axis=0, keepdims=True)
        )
        exps1 = jnp.exp2(scores1 - top)
        exps2 = jnp.exp2(scores2 - top)
        total = column_sum(exps1) + column_sum(exps2)
        mixed = dot(values1[:, lanes].T[turned], exps1.astype(jnp.bfloat16)) + dot(
            values2[:, lanes].T[turned], exps2.astype(jnp.bfloat16)
        )
        log_total[0, head : head + 1, :] = top + jnp.log2(total)
        return mixed * (1.0 / total)

    parts = in_turn(HEADS, first, rest)
    for head in range(0, HEADS, 2):
        lanes = head_lanes(head)[0]
        out[:, lanes] = jnp.concatenate(parts[head : head + 2], axis=0).T.astype(jnp.bfloat16)


def attend(query, own, peer):
    rows, width = query.shape
    lanes = HEADS * HD
    steps = width // lanes
    block = columns(rows, lanes)
    values = columns(rows, lanes, steps)
    return kernel_call(
        attend_body,
        steps,
        [block, block, values, block, values],
        [block, pl.BlockSpec((1, HEADS, rows), lambda step: (step, 0, 0))],
        [shaped((rows, width), jnp.bfloat16), shaped((steps, HEADS, rows), jnp.float32)],
        [],
        16 * rows * rows * width,
        8 * rows * width,
    )(query, own, own, peer, peer)


def attend_back_body(query, keys, values, grad, attended, log_total, *refs):
    if len(refs) == 4:
        before, d_query, d_keys, d_values = refs
    else:
        before, (d_query, d_keys, d_values) = None, refs
    rows = query.shape[0]
    products = {}

    def first(head):
        lanes, place, _ = head_lanes(head)
        if place == 0:
            product = grad[:, lanes].astype(jnp.float32) * attended[:, lanes].astype(jnp.float32)
            products[head] = products[head + 1] = product.T
        own = query[:, lanes] * head_mask((rows, 128), place)
        own_grad = grad[:, lanes] * head_mask((rows, 128), place)
        scores = dot(keys[:, lanes], own, 1, 1)
        d_probs = dot(values[:, lanes], own_grad, 1, 1)
        return own, own_grad, scores, d_probs

    def rest(head, given):
        own, own_grad, scores, d_probs = given
        lanes, place, turned = head_lanes(head)
        delta = column_sum(products[head][turned])
        probs = jnp.exp2(scores - log_total[0, head : head + 1, :])
        d_scores = (probs * (d_probs - delta)).astype(jnp.bfloat16)
        return (
            dot(keys[:, lanes].T[turned], d_scores),
            dot(d_scores, own),
            dot(probs.astype(jnp.bfloat16), own_grad),
        )

    parts = in_turn(HEADS, first, rest)
    for head in range(0, HEADS, 2):
        lanes = head_lanes(head)[0]
        one, two = parts[head : head + 2]
        turned = jnp.concatenate([one[0], two[0]], axis=0).T * HD ** (-0.5)
        d_query[:, lanes] = turned if before is None else turned + before[:, lanes]
        d_keys[:, lanes] = ((one[1] + two[1]) * (1.0 / LOG2E)).astype(d_keys.dtype)
        d_values[:, lanes] = (one[2] + two[2]).astype(d_values.dtype)


def attend_back(query, pair, grad, attended, log_total, before, kind):
    rows, width = query.shape
    lanes = HEADS * HD
    steps = width // lanes
    block = columns(rows, lanes)
    extra = [] if before is None else [before]
    return kernel_call(
        attend_back_body,
        steps,
        [
            block,
            block,
            columns(rows, lanes, steps),
            block,
            block,
            pl.BlockSpec((1, HEADS, rows), lambda step: (step, 0, 0)),
        ]
        + [block] * len(extra),
        [block, block, block],
        [
            shaped((rows, width), jnp.float32),
            shaped((rows, width), kind),
            shaped((rows, width), kind),
        ],
        [],
        20 * rows * rows * width,
        20 * rows * width,
    )(query, pair, pair, grad, attended, log_total, *extra)


def up_body(
    attended, tokens, cotangent, mods, out_weight, up_weight, bias,
    branch, middle, normed, d_ffn, activated, slope, down_grad,
):
    @pl.when(pl.program_id(0) == 0)
    def _():
        mixed = dot(attended[...], out_weight[...])
        branch[...] = mixed
        value = tokens[...].astype(jnp.float32) + row(mods, GATE1) * mixed
        middle[...] = value
        hat, _ = normalized(value)
        value = hat * row(mods, GAIN2) * (1.0 + row(mods, SCALE2)) + row(mods, SHIFT2)
        normed[...] = value.astype(jnp.bfloat16)
        d_ffn[...] = (row(mods, GATE2) * cotangent[...].astype(jnp.float32)).astype(jnp.bfloat16)

    pre = dot(normed[...], up_weight[...]) + bias[...]
    root = 0.7978845608028654
    square = pre * pre
    bent = jnp.tanh(root * pre * (1.0 + 0.044715 * square))
    half = 0.5 + 0.5 * bent
    slope[...] = (
        half + 0.5 * root * pre * (1.0 - bent * bent) * (1.0 + 0.134145 * square)
    ).astype(jnp.bfloat16)
    low = (pre * half).astype(jnp.bfloat16)
    activated[...] = low
    down_grad[...] = dot(low, d_ffn[...], 0, 0).astype(jnp.bfloat16)


def up_layer(attended, tokens, cotangent, mods, out_weight, up_weight, bias):
    rows, width = tokens.shape
    hidden = up_weight.shape[1]
    block = full((rows, width))
    tile = 768
    return kernel_call(
        up_body,
        hidden // tile,
        [
            block,
            block,
            block,
            full((16, width)),
            full((width, width)),
            columns(width, tile),
            columns(1, tile),
        ],
        [
            block,
            block,
            block,
            block,
            columns(rows, tile),
            columns(rows, tile),
            pl.BlockSpec((tile, width), lambda step: (step, 0)),
        ],
        [
            shaped((rows, width), jnp.float32),
            shaped((rows, width), jnp.float32),
            shaped((rows, width), jnp.bfloat16),
            shaped((rows, width), jnp.bfloat16),
            shaped((rows, hidden), jnp.bfloat16),
            shaped((rows, hidden), jnp.bfloat16),
            shaped((hidden, width), jnp.bfloat16),
        ],
        [],
        4 * rows * width * hidden + 2 * rows * width * width,
        8 * rows * hidden + 4 * hidden * width,
    )(attended, tokens, cotangent, mods, out_weight, up_weight, bias)


def up_back_body(d_ffn, normed, down_weight, slope, d_pre, up_grad, bias_grad):
    value = dot(d_ffn[...], down_weight[...], 1, 1) * slope[...].astype(jnp.float32)
    low = value.astype(jnp.bfloat16)
    d_pre[...] = low
    bias_grad[...] = column_sum(value)
    up_grad[...] = dot(normed[...], low, 0, 0).astype(jnp.bfloat16)


def up_back(d_ffn, normed, down_weight, slope):
    rows, width = normed.shape
    hidden = down_weight.shape[0]
    tile = 768
    return kernel_call(
        up_back_body,
        hidden // tile,
        [
            full((rows, width)),
            full((rows, width)),
            pl.BlockSpec((tile, width), lambda step: (step, 0)),
            columns(rows, tile),
        ],
        [columns(rows, tile), columns(width, tile), columns(1, tile)],
        [
            shaped((rows, hidden), jnp.bfloat16),
            shaped((width, hidden), jnp.bfloat16),
            shaped((1, hidden), jnp.float32),
        ],
        [],
        4 * rows * width * hidden,
        8 * rows * hidden + 4 * hidden * width,
    )(d_ffn, normed, down_weight, slope)


def down_body(
    activated, d_pre, down_weight, up_weight, cotangent, d_ffn, middle, branch, attended,
    mods, out_weight, bias,
    mixed, d_middle, d_attended, out_grad, sums, forward, backward,
):
    step = pl.program_id(0)

    @pl.when(step == 0)
    def _():
        forward[...] = dot(activated[...], down_weight[...])
        backward[...] = dot(d_pre[...], up_weight[...], 1, 1)

    @pl.when(step > 0)
    def _():
        forward[...] += dot(activated[...], down_weight[...])
        backward[...] += dot(d_pre[...], up_weight[...], 1, 1)

    @pl.when(step == pl.num_programs(0) - 1)
    def _():
        ffn = forward[...] + bias[...]
        value = middle[...]
        grad = cotangent[...].astype(jnp.float32)
        mixed[...] = (value + row(mods, GATE2) * ffn).astype(jnp.bfloat16)
        back = backward[...]
        hat, inverse = normalized(value)
        d_value = grad + norm_back(
            back, hat, inverse, row(mods, GAIN2) * (1.0 + row(mods, SCALE2))
        )
        d_middle[...] = d_value
        d_branch = (row(mods, GATE1) * d_value).astype(jnp.bfloat16)
        out_grad[...] = dot(attended[...], d_branch, 0, 0).astype(jnp.bfloat16)
        d_attended[...] = dot(d_branch, out_weight[...], 1, 1).astype(jnp.bfloat16)
        sums[0:1, :] = column_sum(back)
        sums[1:2, :] = column_sum(back * hat)
        sums[2:3, :] = column_sum(d_value * branch[...])
        sums[3:4, :] = column_sum(grad * ffn)
        sums[4:5, :] = column_sum(d_ffn[...].astype(jnp.float32))
        sums[5:8, :] = jnp.zeros_like(sums[5:8, :])


def down_layer(
    activated, d_pre, down_weight, up_weight, cotangent, d_ffn, middle, branch, attended,
    mods, out_weight, bias,
):
    rows, width = middle.shape
    hidden = down_weight.shape[0]
    tile = 768
    block = full((rows, width))
    return kernel_call(
        down_body,
        hidden // tile,
        [
            columns(rows, tile),
            columns(rows, tile),
            pl.BlockSpec((tile, width), lambda step: (step, 0)),
            columns(width, tile),
            block,
            block,
            block,
            block,
            block,
            full((16, width)),
            full((width, width)),
            full((1, width)),
        ],
        [block, block, block, full((width, width)), full((8, width))],
        [
            shaped((rows, width), jnp.bfloat16),
            shaped((rows, width), jnp.float32),
            shaped((rows, width), jnp.bfloat16),
            shaped((width, width), jnp.bfloat16),
            shaped((8, width), jnp.float32),
        ],
        [pltpu.VMEM((rows, width), jnp.float32), pltpu.VMEM((rows, width), jnp.float32)],
        4 * rows * width * hidden + 4 * rows * width * width,
        4 * rows * hidden + 4 * hidden * width,
    )(
        activated, d_pre, down_weight, up_weight, cotangent, d_ffn, middle, branch, attended,
        mods, out_weight, bias,
    )


def projected_back_body(
    d_query, d_keys, d_values, peer_keys, peer_values, normed, cosine, sine, out_grad,
    d_projected, grad,
):
    step = pl.program_id(0)

    def finish(low):
        d_projected[...] = low
        grad[...] = dot(normed[...], low, 0, 0).astype(jnp.bfloat16)

    @pl.when(step == 0)
    def _():
        finish(rotate_lanes(d_query[...], cosine[...], -sine[...]).astype(jnp.bfloat16))

    @pl.when(step == 1)
    def _():
        value = d_keys[...] + peer_keys[...].astype(jnp.float32)
        finish(rotate_lanes(value, cosine[...], -sine[...]).astype(jnp.bfloat16))

    @pl.when(step == 2)
    def _():
        value = d_values[...] + peer_values[...].astype(jnp.float32)
        finish(value.astype(jnp.bfloat16))

    @pl.when(step == 3)
    def _():
        grad[...] = out_grad[...]


def projected_back(
    d_query, d_keys, d_values, peer_keys, peer_values, normed, cosine, sine, out_grad
):
    rows, width = normed.shape
    block = full((rows, width))
    return kernel_call(
        projected_back_body,
        4,
        [block] * 6 + [full((rows, 128)), full((rows, 128)), full((width, width))],
        [
            pl.BlockSpec((rows, width), lambda step: (0, jnp.minimum(step, 2))),
            columns(width, width),
        ],
        [shaped((rows, 3 * width), jnp.bfloat16), shaped((width, 4 * width), jnp.bfloat16)],
        [],
        6 * rows * width * width,
        22 * rows * width,
    )(d_query, d_keys, d_values, peer_keys, peer_values, normed, cosine, sine, out_grad)


def tokens_back_body(
    d_projected, weight, tokens, d_middle, mods, sums, bias_grad, out, small, total
):
    step = pl.program_id(0)
    width = tokens.shape[1]

    @pl.when(step == 0)
    def _():
        total[...] = dot(d_projected[...], weight[...], 1, 1)

    @pl.when(step > 0)
    def _():
        total[...] += dot(d_projected[...], weight[...], 1, 1)

    @pl.when(step == pl.num_programs(0) - 1)
    def _():
        back = total[...]
        hat, inverse = normalized(tokens[...].astype(jnp.float32))
        scale1 = 1.0 + row(mods, SCALE1)
        gain1 = row(mods, GAIN1)
        out[...] = (d_middle[...] + norm_back(back, hat, inverse, gain1 * scale1)).astype(
            jnp.bfloat16
        )
        hat_sum1 = column_sum(back * hat)
        hat_sum2 = row(sums, 1)
        rows = [
            column_sum(back),
            hat_sum1 * gain1,
            row(sums, 2),
            row(sums, 0),
            hat_sum2 * row(mods, GAIN2),
            row(sums, 3),
            row(mods, COND) * 0.5,
            jnp.zeros_like(hat_sum1),
            hat_sum1 * scale1,
            hat_sum2 * (1.0 + row(mods, SCALE2)),
            row(sums, 4),
        ]
        for index in range(bias_grad.shape[1] // width):
            rows.append(bias_grad[:, index * width : (index + 1) * width])
        for index, value in enumerate(rows):
            small[index : index + 1, :] = value
        small[len(rows) :, :] = jnp.zeros_like(small[len(rows) :, :])


def tokens_back(d_projected, weight, tokens, d_middle, mods, sums, bias_grad):
    rows, width = tokens.shape
    block = full((rows, width))
    return kernel_call(
        tokens_back_body,
        3 * width // COLUMNS,
        [
            columns(rows, COLUMNS),
            columns(width, COLUMNS),
            block,
            block,
            full((16, width)),
            full((8, width)),
            full(bias_grad.shape),
        ],
        [block, full((16, width))],
        [shaped((rows, width), jnp.bfloat16), shaped((16, width), jnp.float32)],
        [pltpu.VMEM((rows, width), jnp.float32)],
        6 * rows * width * width,
        6 * width * width + 10 * rows * width,
    )(d_projected, weight, tokens, d_middle, mods, sums, bias_grad)


def swap_halves(block):
    count = lax.axis_size("dp") * lax.axis_size("seq")
    target = {1: 2, 2: 1}
    perm = [(i, i - i % 4 + target.get(i % 4, i % 4)) for i in range(count)]
    return lax.ppermute(block, ("dp", "seq"), perm)


def swap_bit(block, bit):
    return lax.ppermute(block, "dp", [(i, i ^ bit) for i in range(lax.axis_size("dp"))])


def swap_cores(block):
    return swap_bit(block, 1)


def swap_seq(block):
    return lax.ppermute(block, "seq", [(0, 1), (1, 0)])


def dp_bits():
    bits, bit = [], 1
    while bit < lax.axis_size("dp"):
        bits.append(bit)
        bit *= 2
    return bits


def pick(block, axis, index):
    return lax.dynamic_index_in_dim(block, index, axis, keepdims=False)


def together(first, second):
    return lax.optimization_barrier((first, second))


class Scatter:
    def __init__(self, matrix, steps):
        dp_size = lax.axis_size("dp")
        rows, width = matrix.shape
        self.block = matrix.reshape(dp_size, rows // dp_size, width)
        self.steps = list(steps)
        self.done = []
        self.sent = self.kept = None

    def prepare(self):
        step = self.steps[0]
        count, rest, width = self.block.shape
        seq_rank = lax.axis_index("seq")
        if step == "half":
            split = self.block.reshape(count, 2, rest // 2, width)
            self.sent = pick(split, 1, 1 - seq_rank)
            self.kept = pick(split, 1, seq_rank)
        elif step in ("whole", "join"):
            self.sent = self.kept = self.block
        else:
            mine = (lax.axis_index("dp") // step) % 2
            inner = 1
            for bit in dp_bits():
                if bit < step and bit not in self.done:
                    inner *= 2
            split = self.block.reshape(count // (2 * inner), 2, inner, rest, width)
            shape = (count // 2, rest, width)
            self.sent = pick(split, 1, 1 - mine).reshape(shape)
            self.kept = pick(split, 1, mine).reshape(shape)
        return self.sent

    def move(self):
        step = self.steps[0]
        if isinstance(step, str):
            self.got = swap_seq(self.sent)
        else:
            self.got = swap_bit(self.sent, step)

    def finish(self):
        step = self.steps.pop(0)
        if step == "join":
            here = lax.axis_index("seq") == 0
            first = jnp.where(here, self.kept, self.got)
            second = jnp.where(here, self.got, self.kept)
            self.block = jnp.concatenate([first, second], axis=1)
            return
        total = self.kept.astype(jnp.float32) + self.got.astype(jnp.float32)
        self.block = total if len(self.steps) == 0 else total.astype(jnp.bfloat16)
        self.done.append(step)

    def slot(self, before, after):
        if self.sent is not None:
            self.got, before = together(self.got, before)
            self.finish()
        if len(self.steps) > 0:
            sent, after = together(self.prepare(), after)
            if self.kept is self.sent:
                self.kept = sent
            self.sent = sent
            self.move()
        return before, after

    def run(self):
        if self.sent is not None:
            self.finish()
        while len(self.steps) > 0:
            self.prepare()
            self.move()
            self.finish()
        return self.block[0].astype(jnp.float32)


def share_small(small):
    small = small + swap_cores(small)

    def double(rows, move):
        got = move(rows)
        return jnp.concatenate([rows[:-8], got[:-8], rows[-8:] + got[-8:]], axis=0)

    small = double(small, swap_seq)
    for bit in dp_bits()[1:]:
        small = double(small, lambda rows, bit=bit: swap_bit(rows, bit))
    return small[:-8].reshape(-1, 8, small.shape[1]), small[-8:]


def per_device(
    tokens,
    cotangent,
    time_index,
    step_table,
    first_gain,
    attn_qkv,
    attn_out,
    second_gain,
    mlp_up,
    up_bias,
    mlp_down,
    down_bias,
    ada_weight,
    ada_bias,
):
    rows, width = tokens.shape[1:]
    dp_rank = lax.axis_index("dp")
    core = dp_rank % 2
    own_cond, silu_back = jax.vjp(
        jax.nn.silu, lax.dynamic_slice_in_dim(step_table, time_index[0], 1, axis=0)
    )
    tokens = swap_halves(tokens[0])
    time_index = swap_halves(time_index)
    cotangent = swap_halves(cotangent[0])
    cond = jax.nn.silu(lax.dynamic_slice_in_dim(step_table, time_index[0], 1, axis=0))
    ada_float = ada_weight.astype(jnp.float32)
    modulation = jnp.dot(cond, ada_float, precision=highest) + ada_bias.astype(jnp.float32)
    gain1 = first_gain.astype(jnp.float32)
    gain2 = second_gain.astype(jnp.float32)
    cond_row = jnp.pad(cond, ((0, 0), (0, width - cond.shape[1])))
    mods = jnp.concatenate(
        [modulation.reshape(6, width), gain1[None], gain2[None], cond_row, jnp.zeros((7, width))]
    )
    positions = core * rows + jnp.arange(rows, dtype=jnp.int32)
    cosine, sine = tables(positions)

    normed1, own_pair = project_key_value(tokens, mods, attn_qkv, cosine, sine)
    peer_pair = swap_cores(own_pair)
    query = project_query(normed1, attn_qkv, cosine, sine)
    attended, log_total = attend(query, own_pair, peer_pair)
    branch, middle, normed2, d_ffn, activated, slope, mlp_down_grad = up_layer(
        attended, tokens, cotangent, mods, attn_out, mlp_up, up_bias.astype(jnp.float32)[None]
    )
    down_rows = lax.psum_scatter(mlp_down_grad, "dp", scatter_dimension=0, tiled=True)
    d_pre, mlp_up_grad, up_bias_grad = up_back(d_ffn, normed2, mlp_down, slope)
    bits = dp_bits()
    up_sum = Scatter(mlp_up_grad, [1, "half"] + bits[1:] + ["join"])
    _, d_pre = up_sum.slot(None, d_pre)
    mixed, d_middle, d_attended, attn_out_grad, sums2 = down_layer(
        activated, d_pre, mlp_down, mlp_up, cotangent, d_ffn, middle, branch, attended,
        mods, attn_out, down_bias.astype(jnp.float32)[None],
    )
    sums2, log_total = up_sum.slot(sums2, log_total)
    d_query, away_keys, away_values = attend_back(
        query, peer_pair, d_attended, attended, log_total, None, jnp.bfloat16
    )
    peer_keys, peer_values = swap_cores(away_keys), swap_cores(away_values)
    d_query, d_keys, d_values = attend_back(
        query, own_pair, d_attended, attended, log_total, d_query, jnp.float32
    )
    d_query, cosine = up_sum.slot(d_query, cosine)
    d_projected, qkv_out_grad = projected_back(
        d_query, d_keys, d_values, peer_keys, peer_values, normed1, cosine, sine, attn_out_grad
    )
    half = qkv_out_grad.shape[1] // 2
    one_sum = Scatter(qkv_out_grad[:, :half], bits + ["whole"])
    two_sum = Scatter(qkv_out_grad[:, half:], [1, "half"] + bits[1:] + ["join"])
    d_projected, sums2 = up_sum.slot(d_projected, sums2)
    _, d_projected = one_sum.slot(None, d_projected)
    _, d_projected = two_sum.slot(None, d_projected)
    tokens_grad, small = tokens_back(
        d_projected, attn_qkv, tokens, d_middle, mods, sums2, up_bias_grad
    )
    per_sequence, sums = share_small(small)
    d_mod_all = per_sequence[:, :6].reshape(per_sequence.shape[0], 6 * width)
    cond_all = per_sequence[:, 6, : cond.shape[1]]
    ada_bias_grad = jnp.sum(d_mod_all, axis=0)
    own_columns = d_mod_all.shape[1] // lax.axis_size("dp")
    mine = lax.dynamic_slice_in_dim(d_mod_all, dp_rank * own_columns, own_columns, axis=1)
    ada_weight_grad = lax.dot_general(
        cond_all, mine, (((0,), (0,)), ((), ())), precision=highest
    )
    d_mod_own = jnp.where(lax.axis_index("seq") == core, d_mod_all[:1], d_mod_all[1:2])
    (cond_grad,) = silu_back(jnp.dot(d_mod_own, ada_float.T, precision=highest))
    one_rows, two_rows = one_sum.run(), two_sum.run()
    qkv_out_rows = jnp.concatenate([one_rows, two_rows], axis=1)
    down_total = down_rows.astype(jnp.float32) + swap_seq(down_rows).astype(jnp.float32)
    return (
        swap_halves(mixed)[None],
        swap_halves(tokens_grad).astype(jnp.float32)[None],
        cond_grad,
        sums[0],
        qkv_out_rows[:, : 3 * width],
        qkv_out_rows[:, 3 * width :],
        sums[1],
        up_sum.run(),
        sums[3:7].reshape(-1),
        down_total,
        sums[2],
        ada_weight_grad,
        ada_bias_grad,
    )


def solution(mesh):
    placed = (
        P("dp", "seq", None),
        P("dp", "seq", None),
        P("dp"),
        P(),
        P(),
        P(),
        P(),
        P(),
        P(),
        P(),
        P(),
        P(),
        P(),
        P(),
    )
    return jax.shard_map(
        per_device,
        mesh=mesh,
        in_specs=placed,
        out_specs=(
            P("dp", "seq", None),
            P("dp", "seq", None),
            P("dp", None),
            P(),
            P("dp", None),
            P("dp", None),
            P(),
            P("dp", None),
            P(),
            P("dp", None),
            P(),
            P(None, "dp"),
            P(),
        ),
        check_vma=False,
    )
```

```python
import functools

import jax
import jax.numpy as jnp
from jax import lax
from jax.experimental import pallas as pl
from jax.experimental.pallas import tpu as pltpu
from jax.sharding import PartitionSpec as P

HD = 64
LOG2E = 1.4426950408889634


highest = lax.Precision.HIGHEST


def tables(positions):
    half_dim = HD // 2
    frequency = jnp.exp(
        -jnp.log(10000.0) * (2.0 * jnp.arange(half_dim, dtype=jnp.float32) / HD)
    )
    angles = positions.astype(jnp.float32)[:, None] * frequency[None, :]
    cosine, sine = jnp.cos(angles), jnp.sin(angles)
    return (
        jnp.concatenate([cosine] * 4, axis=1),
        jnp.concatenate([-sine, sine, -sine, sine], axis=1),
    )


def full(shape):
    return pl.BlockSpec(shape, lambda step: (0,) * len(shape))


def columns(rows, width, first=0):
    return pl.BlockSpec((rows, width), lambda step: (0, step + first))


def shaped(shape, kind):
    return jax.ShapeDtypeStruct(shape, kind)


def far(shape, kind):
    return pltpu.VMEM(shape, kind)


def far(shape, kind):
    return pltpu.HBM(shape, kind)


def store_split(low, core, own, keep, send):
    pairs = low.shape[0] // (2 * own)

    def store(kept):
        for pair in range(pairs):
            rows = slice(pair * own, (pair + 1) * own)
            for parity, target in ((kept, keep), (1 - kept, send)):
                start = (2 * pair + parity) * own
                target[rows, :] = low[start : start + own, :]

    @pl.when(core[0] == 0)
    def _():
        store(0)

    @pl.when(core[0] == 1)
    def _():
        store(1)


def zero_shape():
    return jax.ShapeDtypeStruct((1, 1), jnp.float32)


def scalar_spec():
    return pl.BlockSpec(memory_space=pltpu.SMEM)


def kernel_call(body, steps, in_specs, out_specs, out_shape, scratch, grant):
    call = pl.pallas_call(
        body,
        grid=(steps,),
        in_specs=in_specs,
        out_specs=out_specs,
        out_shape=out_shape,
        scratch_shapes=scratch,
        compiler_params=pltpu.CompilerParams(
            dimension_semantics=("arbitrary",), vmem_limit_bytes=grant * 1024 * 1024
        ),
        cost_estimate=pl.CostEstimate(flops=1, bytes_accessed=1, transcendentals=0),
    )

    def run(*args, free=()):
        placed = []
        for arg in args:
            if arg.size > 4096 and not any(arg is other for other in free):
                arg = pltpu.with_memory_space_constraint(arg, pltpu.HBM)
            placed.append(arg)
        return call(*placed)

    return run


def dot(left, right, left_axis=1, right_axis=0):
    return lax.dot_general(
        left,
        right,
        (((left_axis,), (right_axis,)), ((), ())),
        preferred_element_type=jnp.float32,
    )


def normalized(inputs):
    center = inputs - jnp.mean(inputs, axis=-1, keepdims=True)
    inverse = lax.rsqrt(jnp.mean(center * center, axis=-1, keepdims=True) + 1e-05)
    return center * inverse, inverse


def norm_back(back, hat, inverse, factor):
    scaled = back * factor
    return inverse * (
        scaled
        - jnp.mean(scaled, axis=-1, keepdims=True)
        - hat * jnp.mean(scaled * hat, axis=-1, keepdims=True)
    )


def column_sum(values):
    return jnp.sum(values, axis=0, keepdims=True)


SHIFT1, SCALE1, GATE1, SHIFT2, SCALE2, GATE2, GAIN1, GAIN2, COND = range(9)


def row(ref, index):
    return ref[index : index + 1, :]


def rotate_lanes(values, cosine, sine):
    lane = lax.broadcasted_iota(jnp.int32, cosine.shape, 1)
    lower = (lane % HD) < HD // 2
    parts = []
    for start in range(0, values.shape[1], 128):
        part = values[:, start : start + 128]
        other = jnp.where(lower, pltpu.roll(part, 128 - HD // 2, 1), pltpu.roll(part, HD // 2, 1))
        parts.append(part * cosine + other * sine)
    return jnp.concatenate(parts, axis=1)


COLUMNS = 768


def key_value_body(tokens, mods, weight, cosine, sine, cotangent, normed, out):
    step = pl.program_id(0)
    turned_steps = pl.num_programs(0) // 2

    @pl.when(step == 0)
    def _():
        hat, _ = normalized(tokens[...].astype(jnp.float32))
        value = hat * row(mods, GAIN1) * (1.0 + row(mods, SCALE1)) + row(mods, SHIFT1)
        normed[...] = value.astype(jnp.bfloat16)

    @pl.when(step < turned_steps)
    def _():
        value = dot(normed[...], weight[...])
        out[...] = rotate_lanes(value, cosine[...], sine[...]).astype(jnp.bfloat16)

    @pl.when(step >= turned_steps)
    def _():
        out[...] = dot(normed[...], weight[...]).astype(jnp.bfloat16)


def project_key_value(tokens, mods, weight, cosine, sine, after):
    rows, width = tokens.shape
    first = width // COLUMNS
    return kernel_call(
        key_value_body,
        2 * first,
        [
            full((rows, width)),
            full((16, width)),
            columns(width, COLUMNS, first),
            full((rows, 128)),
            full((rows, 128)),
            pl.BlockSpec(memory_space=pl.ANY),
        ],
        [full((rows, width)), columns(rows, COLUMNS)],
        [far((rows, width), jnp.bfloat16), far((rows, 2 * width), jnp.bfloat16)],
        [],
        18,
    )(tokens, mods, weight, cosine, sine, after, free=(tokens, after))


def head_mask(shape, head):
    lane = lax.broadcasted_iota(jnp.int32, shape, 1)
    return jnp.where(lane // HD == head, 1.0, 0.0).astype(jnp.bfloat16)


HEADS = 4


def head_lanes(head):
    pair, place = divmod(head, 2)
    return slice(pair * 128, (pair + 1) * 128), place, slice(place * HD, (place + 1) * HD)


def in_turn(count, first, rest):
    results = []
    ahead = first(0)
    for index in range(count):
        now = ahead
        if index + 1 < count:
            ahead = first(index + 1)
        results.append(rest(index, now))
    return results


def attend_heads(query, keys1, values1, keys2, values2, log_total):
    rows = query.shape[0]

    def first(head):
        lanes, place, _ = head_lanes(head)
        own = query[:, lanes] * head_mask((rows, 128), place)
        return dot(keys1[:, lanes], own, 1, 1), dot(keys2[:, lanes], own, 1, 1)

    def rest(head, scores):
        lanes, place, turned = head_lanes(head)
        scores1, scores2 = scores
        top = jnp.maximum(
            jnp.max(scores1, axis=0, keepdims=True), jnp.max(scores2, axis=0, keepdims=True)
        )
        exps1 = jnp.exp2(scores1 - top)
        exps2 = jnp.exp2(scores2 - top)
        total = column_sum(exps1) + column_sum(exps2)
        mixed = dot(values1[:, lanes].T[turned], exps1.astype(jnp.bfloat16)) + dot(
            values2[:, lanes].T[turned], exps2.astype(jnp.bfloat16)
        )
        log_total[0, head : head + 1, :] = top + jnp.log2(total)
        return mixed * (1.0 / total)

    parts = in_turn(HEADS, first, rest)
    return jnp.concatenate(
        [
            jnp.concatenate(parts[head : head + 2], axis=0).T.astype(jnp.bfloat16)
            for head in range(0, HEADS, 2)
        ],
        axis=1,
    )


def attend_back_body(second, query, keys, values, grad, attended, log_total, *refs):
    if second:
        before, cosine, sine = refs[:3]
    d_query, d_pair, zero = refs[-3:]
    zero[0, 0] = 0.0
    rows = query.shape[0]
    products = {}

    def first(head):
        lanes, place, _ = head_lanes(head)
        if place == 0:
            product = grad[:, lanes].astype(jnp.float32) * attended[:, lanes].astype(jnp.float32)
            products[head] = products[head + 1] = product.T
        own = query[:, lanes] * head_mask((rows, 128), place)
        own_grad = grad[:, lanes] * head_mask((rows, 128), place)
        scores = dot(keys[:, lanes], own, 1, 1)
        d_probs = dot(values[:, lanes], own_grad, 1, 1)
        return own, own_grad, scores, d_probs

    def rest(head, given):
        own, own_grad, scores, d_probs = given
        lanes, place, turned = head_lanes(head)
        delta = column_sum(products[head][turned])
        probs = jnp.exp2(scores - log_total[0, head : head + 1, :])
        d_scores = (probs * (d_probs - delta)).astype(jnp.bfloat16)
        return (
            dot(keys[:, lanes].T[turned], d_scores),
            dot(d_scores, own),
            dot(probs.astype(jnp.bfloat16), own_grad),
        )

    parts = in_turn(HEADS, first, rest)
    width = HEADS * HD
    for head in range(0, HEADS, 2):
        lanes = head_lanes(head)[0]
        value_lanes = slice(width + lanes.start, width + lanes.stop)
        one, two = parts[head : head + 2]
        turned = jnp.concatenate([one[0], two[0]], axis=0).T * HD ** (-0.5)
        if second:
            turned = rotate_lanes(turned + before[:, lanes], cosine[...], -sine[...])
        d_query[:, lanes] = turned.astype(d_query.dtype)
        d_pair[:, lanes] = ((one[1] + two[1]) * (1.0 / LOG2E)).astype(jnp.bfloat16)
        d_pair[:, value_lanes] = (one[2] + two[2]).astype(jnp.bfloat16)


def attend_back(query, pair, grad, attended, log_total, before=None, after=(), free=()):
    rows, width = query.shape
    lanes = HEADS * HD
    steps = width // lanes
    block = columns(rows, lanes)
    second = before is not None
    extra = list(before) if second else []
    extra_specs = [block, full((rows, 128)), full((rows, 128))] if second else []
    return kernel_call(
        functools.partial(attend_back_body, second),
        steps,
        [
            block,
            block,
            columns(rows, lanes, steps),
            block,
            block,
            pl.BlockSpec((1, HEADS, rows), lambda step: (step, 0, 0)),
        ]
        + extra_specs
        + [pl.BlockSpec(memory_space=pl.ANY)] * len(after),
        [block, columns(rows, 2 * lanes), scalar_spec()],
        [
            far((rows, width), jnp.bfloat16 if second else jnp.float32),
            far((rows, 2 * width), jnp.bfloat16),
            zero_shape(),
        ],
        [],
        28,
    )(query, pair, pair, grad, attended, log_total, *extra, *after, free=(*free, *after))


def block_body(
    own_up, own_down, attend_steps, hidden_steps,
    core, normed1, query_weight, cosine, sine, keys1, values1, keys2, values2, mods,
    up_bias, down_bias, tokens_far, cotangent_far, out_far, up_far, down_far,
    query, attended, log_total, mixed, d_middle, d_attended, up_keep, up_send,
    down_keep, down_send, bias_grad, sums,
    tokens, cotangent, out_weight, up_weight, down_weight, arrived,
    all_attended, normed, d_ffn, branch, middle, forward, back,
):
    step = pl.program_id(0)
    tile = up_bias.shape[1]
    arrivals = [
        pltpu.make_async_copy(source, target, arrived.at[index])
        for index, (source, target) in enumerate(
            (
                (tokens_far, tokens),
                (cotangent_far, cotangent),
                (out_far, out_weight),
                (up_far, up_weight),
                (down_far, down_weight),
            )
        )
    ]

    @pl.when(step == 0)
    def _():
        for arrival in arrivals:
            arrival.start()

    @pl.when(step < attend_steps)
    def _():
        value = rotate_lanes(dot(normed1[...], query_weight[...]), cosine[...], sine[...])
        query[...] = (value * (LOG2E * HD ** (-0.5))).astype(jnp.bfloat16)
        found = attend_heads(query, keys1, values1, keys2, values2, log_total)
        attended[...] = found
        for index in range(attend_steps):

            @pl.when(step == index)
            def _(index=index):
                lanes = HEADS * HD
                all_attended[:, index * lanes : (index + 1) * lanes] = found

    @pl.when(step == attend_steps)
    def _():
        for arrival in arrivals:
            arrival.wait()
        turned = dot(all_attended[...], out_weight[...])
        branch[...] = turned.astype(jnp.bfloat16)
        value = tokens[...].astype(jnp.float32) + row(mods, GATE1) * turned
        middle[...] = value
        hat, _ = normalized(value)
        value = hat * row(mods, GAIN2) * (1.0 + row(mods, SCALE2)) + row(mods, SHIFT2)
        normed[...] = value.astype(jnp.bfloat16)
        low = (row(mods, GATE2) * cotangent[...].astype(jnp.float32)).astype(jnp.bfloat16)
        d_ffn[...] = low
        sums[4:5, :] = column_sum(low.astype(jnp.float32))
        forward[...] = jnp.zeros_like(forward)
        back[...] = jnp.zeros_like(back)

    @pl.when((step >= attend_steps) & (step < attend_steps + hidden_steps))
    def _():
        place = pl.ds(pl.multiple_of((step - attend_steps) * tile, tile), tile)
        pre = dot(normed[...], up_weight[:, place]) + up_bias[...]
        d_activated = dot(d_ffn[...], down_weight[place, :], 1, 1)
        root = 0.7978845608028654
        square = pre * pre
        bent = jnp.tanh(root * pre * (1.0 + 0.044715 * square))
        half = 0.5 + 0.5 * bent
        slope = half + (0.5 * root) * pre * (1.0 - bent * bent) * (1.0 + 0.134145 * square)
        low = (pre * half).astype(jnp.bfloat16)
        d_pre = d_activated * slope
        d_low = d_pre.astype(jnp.bfloat16)
        bias_grad[...] = column_sum(d_pre)
        down_grad = dot(low, d_ffn[...], 0, 0).astype(jnp.bfloat16)
        store_split(down_grad, core, own_down, down_keep, down_send)
        up_grad = dot(normed[...], d_low, 0, 0).astype(jnp.bfloat16)
        store_split(up_grad, core, own_up, up_keep, up_send)
        forward[...] += dot(low, down_weight[place, :])
        back[...] += dot(d_low, up_weight[:, place], 1, 1)

    @pl.when(step == attend_steps + hidden_steps)
    def _():
        grad = cotangent[...].astype(jnp.float32)
        held = middle[...]
        hat, inverse = normalized(held)
        factor = row(mods, GAIN2) * (1.0 + row(mods, SCALE2))
        value = back[...]
        d_value = grad + norm_back(value, hat, inverse, factor)
        d_middle[...] = d_value
        d_branch = (row(mods, GATE1) * d_value).astype(jnp.bfloat16)
        d_attended[...] = dot(d_branch, out_weight[...], 1, 1).astype(jnp.bfloat16)
        out_grad = dot(all_attended[...], d_branch, 0, 0).astype(jnp.bfloat16)
        store_split(out_grad, core, own_up, up_keep, up_send)
        ffn = forward[...] + down_bias[...]
        mixed[...] = (held + row(mods, GATE2) * ffn).astype(jnp.bfloat16)
        sums[0:1, :] = column_sum(value)
        sums[1:2, :] = column_sum(value * hat)
        sums[2:3, :] = column_sum(d_value * branch[...].astype(jnp.float32))
        sums[3:4, :] = column_sum(grad * ffn)
        sums[5:8, :] = jnp.zeros_like(sums[5:8, :])


def split_rows(rows):
    own = rows // lax.axis_size("dp")
    return own if own % 16 == 0 else rows // 2


def block_layer(
    core, normed1, qkv_weight, cosine, sine, own, peer, mods, up_bias, down_bias,
    tokens, cotangent, out_weight, up_weight, down_weight,
):
    rows, width = tokens.shape
    hidden = up_weight.shape[1]
    tile = width
    lanes = HEADS * HD
    attend_steps = width // lanes
    hidden_steps = hidden // tile
    own_down = hidden // lax.axis_size("dp")
    if own_down % 16 > 0:
        own_down = tile // 2

    def heads(first=0):
        return pl.BlockSpec(
            (rows, lanes), lambda step: (0, jnp.minimum(step, attend_steps - 1) + first)
        )

    def tiles(step):
        return jnp.clip(step - attend_steps, 0, hidden_steps - 1)

    def up_tiles(step):
        return jnp.clip(step - attend_steps, 0, hidden_steps)

    block = full((rows, width))
    far_spec = pl.BlockSpec(memory_space=pl.ANY)
    low = jnp.bfloat16
    up_spec = pl.BlockSpec((width // 2, tile), lambda step: (0, up_tiles(step)))
    down_spec = pl.BlockSpec((tile // 2, width), lambda step: (tiles(step), 0))
    return kernel_call(
        functools.partial(
            block_body, split_rows(width), own_down, attend_steps, hidden_steps
        ),
        attend_steps + hidden_steps + 1,
        [
            scalar_spec(),
            block,
            pl.BlockSpec((width, lanes), lambda step: (0, jnp.minimum(step, attend_steps - 1))),
            full((rows, 128)),
            full((rows, 128)),
            heads(),
            heads(attend_steps),
            heads(),
            heads(attend_steps),
            full((16, width)),
            pl.BlockSpec((1, tile), lambda step: (0, tiles(step))),
            full((1, width)),
        ]
        + [far_spec] * 5,
        [
            heads(),
            heads(),
            pl.BlockSpec(
                (1, HEADS, rows), lambda step: (jnp.minimum(step, attend_steps - 1), 0, 0)
            ),
            block,
            block,
            block,
            up_spec,
            up_spec,
            down_spec,
            down_spec,
            pl.BlockSpec((1, tile), lambda step: (0, tiles(step))),
            full((8, width)),
        ],
        [
            far((rows, width), low),
            far((rows, width), low),
            far((attend_steps, HEADS, rows), jnp.float32),
            far((rows, width), low),
            far((rows, width), jnp.float32),
            far((rows, width), low),
            far((width // 2, hidden + width), low),
            far((width // 2, hidden + width), low),
            far((hidden // 2, width), low),
            far((hidden // 2, width), low),
            far((1, hidden), jnp.float32),
            far((8, width), jnp.float32),
        ],
        [
            pltpu.VMEM((rows, width), low),
            pltpu.VMEM((rows, width), low),
            pltpu.VMEM((width, width), low),
            pltpu.VMEM((width, hidden), low),
            pltpu.VMEM((hidden, width), low),
            pltpu.SemaphoreType.DMA((5,)),
            pltpu.VMEM((rows, width), low),
            pltpu.VMEM((rows, width), low),
            pltpu.VMEM((rows, width), low),
            pltpu.VMEM((rows, width), low),
            pltpu.VMEM((rows, width), jnp.float32),
            pltpu.VMEM((rows, width), jnp.float32),
            pltpu.VMEM((rows, width), jnp.float32),
        ],
        58,
    )(
        core, normed1, qkv_weight, cosine, sine, own, own, peer, peer, mods, up_bias, down_bias,
        tokens, cotangent, out_weight, up_weight, down_weight, free=(peer, cotangent, tokens),
    )


def projected_back_body(
    own, core, d_query, d_pair, peer_pair, normed, cosine, sine, d_projected, keep, send, zero
):
    zero[0, 0] = 0.0
    lanes = HEADS * HD
    pair = d_pair[...].astype(jnp.float32) + peer_pair[...].astype(jnp.float32)
    keys = rotate_lanes(pair[:, :lanes], cosine[...], -sine[...]).astype(jnp.bfloat16)
    low = jnp.concatenate([d_query[...], keys, pair[:, lanes:].astype(jnp.bfloat16)], axis=1)
    d_projected[...] = low
    store_split(dot(normed[...], low, 0, 0).astype(jnp.bfloat16), core, own, keep, send)


def projected_back(core, d_query, d_pair, peer_pair, normed, cosine, sine):
    rows, width = normed.shape
    lanes = HEADS * HD
    return kernel_call(
        functools.partial(projected_back_body, split_rows(width)),
        width // lanes,
        [
            scalar_spec(),
            columns(rows, lanes),
            columns(rows, 2 * lanes),
            columns(rows, 2 * lanes),
            full((rows, width)),
            full((rows, 128)),
            full((rows, 128)),
        ],
        [
            columns(rows, 3 * lanes),
            columns(width // 2, 3 * lanes),
            columns(width // 2, 3 * lanes),
            scalar_spec(),
        ],
        [
            far((rows, 3 * width), jnp.bfloat16),
            far((width // 2, 3 * width), jnp.bfloat16),
            far((width // 2, 3 * width), jnp.bfloat16),
            zero_shape(),
        ],
        [],
        32,
    )(core, d_query, d_pair, peer_pair, normed, cosine, sine, free=(peer_pair,))


def tokens_back_body(
    d_projected, weight1, weight2, weight3, tokens, d_middle, mods, sums, bias_grad, *refs
):
    out, small, zero, total = refs[-4:]
    zero[0, 0] = 0.0
    step = pl.program_id(0)
    width = tokens.shape[1]
    lanes = HEADS * HD
    part = sum(
        dot(d_projected[:, index * lanes : (index + 1) * lanes], weight[...], 1, 1)
        for index, weight in enumerate((weight1, weight2, weight3))
    )

    @pl.when(step == 0)
    def _():
        total[...] = part

    @pl.when(step > 0)
    def _():
        total[...] += part

    @pl.when(step == pl.num_programs(0) - 1)
    def _():
        back = total[...]
        hat, inverse = normalized(tokens[...].astype(jnp.float32))
        scale1 = 1.0 + row(mods, SCALE1)
        gain1 = row(mods, GAIN1)
        out[...] = (d_middle[...] + norm_back(back, hat, inverse, gain1 * scale1)).astype(
            jnp.bfloat16
        )
        hat_sum1 = column_sum(back * hat)
        hat_sum2 = row(sums, 1)
        rows = [
            column_sum(back),
            hat_sum1 * gain1,
            row(sums, 2),
            row(sums, 0),
            hat_sum2 * row(mods, GAIN2),
            row(sums, 3),
            row(mods, COND) * 0.5,
            jnp.zeros_like(hat_sum1),
            hat_sum1 * scale1,
            hat_sum2 * (1.0 + row(mods, SCALE2)),
            row(sums, 4),
        ]
        for index in range(bias_grad.shape[1] // width):
            rows.append(bias_grad[:, index * width : (index + 1) * width])
        for index, value in enumerate(rows):
            small[index : index + 1, :] = value
        small[len(rows) :, :] = jnp.zeros_like(small[len(rows) :, :])


def tokens_back(d_projected, weight, tokens, d_middle, mods, sums, bias_grad, after):
    rows, width = tokens.shape
    block = full((rows, width))
    lanes = HEADS * HD
    steps = width // lanes
    return kernel_call(
        tokens_back_body,
        steps,
        [
            columns(rows, 3 * lanes),
            columns(width, lanes),
            columns(width, lanes, steps),
            columns(width, lanes, 2 * steps),
            block,
            block,
            full((16, width)),
            full((8, width)),
            full(bias_grad.shape),
        ]
        + [pl.BlockSpec(memory_space=pl.ANY)] * len(after),
        [block, full((16, width)), scalar_spec()],
        [far((rows, width), jnp.bfloat16), far((16, width), jnp.float32), zero_shape()],
        [pltpu.VMEM((rows, width), jnp.float32)],
        32,
    )(d_projected, weight, weight, weight, tokens, d_middle, mods, sums, bias_grad, *after, free=after)


def swap_halves(block):
    count = lax.axis_size("dp") * lax.axis_size("seq")
    target = {1: 2, 2: 1}
    perm = [(i, i - i % 4 + target.get(i % 4, i % 4)) for i in range(count)]
    return lax.ppermute(block, ("dp", "seq"), perm)


def swap_bit(block, bit):
    return lax.ppermute(block, "dp", [(i, i ^ bit) for i in range(lax.axis_size("dp"))])


def swap_cores(block):
    return swap_bit(block, 1)


def swap_seq(block):
    return lax.ppermute(block, "seq", [(0, 1), (1, 0)])


def dp_bits():
    bits, bit = [], 1
    while bit < lax.axis_size("dp"):
        bits.append(bit)
        bit *= 2
    return bits


def pick(block, axis, index):
    return lax.dynamic_index_in_dim(block, index, axis, keepdims=False)


class Flow:
    def __init__(self, got, kept, lanes=None):
        self.got, self.kept = got, kept
        self.lanes = lanes or (0, kept.shape[2])
        self.count, self.rest = kept.shape[:2]
        self.width = self.lanes[1] - self.lanes[0]


def stage_body(jobs, counts, mine, *refs):
    inputs = refs[: counts[0]]
    outputs = refs[counts[0] + counts[1] :]
    for place, (half, sources, target) in enumerate(jobs):
        sent, kept = outputs[target], outputs[target + 1]

        def store(out, which, half=half, sources=sources):
            at = 0
            for one, two, start, stop, rows in sources:
                if half:
                    middle = (start + stop) // 2
                    lanes = slice(middle, stop) if which else slice(start, middle)
                    total = inputs[one][:, :, lanes].astype(jnp.float32)
                    total = total + inputs[two][:, :, lanes].astype(jnp.float32)
                    out[...] = total.astype(jnp.bfloat16)
                    continue
                for pair in range(out.shape[0]):
                    block = 2 * pair + which
                    total = inputs[one][block, :, start:stop].astype(jnp.float32)
                    total = total + inputs[two][block, :, start:stop].astype(jnp.float32)
                    total = total.astype(jnp.bfloat16)
                    column = at
                    for first in range(0, total.shape[0], rows):
                        out[pair, :, column : column + stop - start] = total[first : first + rows]
                        column += stop - start
                at = column

        for which in range(2):

            @pl.when(mine[place] == which)
            def _(which=which, sent=sent, kept=kept, store=store):
                store(kept, which)
                store(sent, 1 - which)


def small_body(steps, first, one, two, out):
    rows = one.shape[0] - 8

    @pl.when(pl.program_id(0) == 0)
    def _():
        if first:
            out[...] = one[...] + two[...]
        else:
            out[:rows, :] = one[:rows, :]
            out[rows : 2 * rows, :] = two[:rows, :]
            out[2 * rows :, :] = one[rows:, :] + two[rows:, :]


def stage(steps, jobs, after=(), small=None):
    seq_rank, dp_rank = lax.axis_index("seq"), lax.axis_index("dp")
    inputs, in_specs, specs, out_specs, out_shape, mine = [], [], [], [], [], []

    def place_of(array):
        for index, other in enumerate(inputs):
            if other is array:
                return index
        inputs.append(array)
        each = array.shape[0] // steps
        in_specs.append(pl.BlockSpec((each,) + array.shape[1:], lambda at: (at, 0, 0)))
        return len(inputs) - 1

    for flows, step in jobs:
        half = step == "half"
        rest, count = flows[0].rest, flows[0].count
        sources = [
            (place_of(flow.got), place_of(flow.kept), *flow.lanes, rest) for flow in flows
        ]
        if half:
            shape = (count, rest, flows[0].width // 2)
            mine.append(seq_rank)
        else:
            width = sum(flow.width * flow.rest // rest for flow in flows)
            shape = (count // 2, rest, width)
            mine.append((dp_rank // step) % 2)
        specs.append((half, sources, len(out_shape)))
        out_shape += [far(shape, jnp.bfloat16)] * 2
        block = (shape[0] // steps,) + shape[1:]
        out_specs += [pl.BlockSpec(block, lambda at: (at, 0, 0))] * 2
    counts = (len(inputs), len(after))
    extra = []
    if small is not None:
        got, kept, first = small
        extra = [kept, got]
        rows = kept.shape[0] if first else 2 * kept.shape[0] - 8
        out_shape.append(far((rows, kept.shape[1]), jnp.float32))
        out_specs.append(full((rows, kept.shape[1])))

    def body(mine, *refs):
        if small is None:
            stage_body(specs, counts, mine, *refs)
            return
        main, ends = refs[: sum(counts)], refs[sum(counts) :]
        small_body(steps, first, ends[0], ends[1], ends[-1])
        stage_body(specs, counts, mine, *main, *ends[2:-1])

    results = kernel_call(
        body,
        steps,
        [scalar_spec()]
        + in_specs
        + [pl.BlockSpec(memory_space=pl.ANY)] * len(after)
        + [full(array.shape) for array in extra],
        out_specs,
        out_shape,
        [],
        40,
    )(jnp.stack(mine), *inputs, *after, *extra, free=(*inputs, *after, *extra))
    new = []
    for (flows, step), (_, _, target) in zip(jobs, specs):
        sent = results[target]
        got = swap_seq(sent) if step == "half" else swap_bit(sent, step)
        new.append(Flow(got, results[target + 1]))
    if small is not None:
        new.append(results[-1])
    return new, results[0]


def from_tiles(kept, sent, tile):
    rows, width = 2 * kept.shape[0], kept.shape[1]
    core = lax.axis_index("dp") % 2
    first = jnp.where(core == 0, kept, sent).reshape(rows // tile, 1, tile // 2, width)
    second = jnp.where(core == 0, sent, kept).reshape(rows // tile, 1, tile // 2, width)
    return jnp.concatenate([first, second], axis=1).reshape(rows, width)


def plain_sum(kept, sent, tile):
    matrix = from_tiles(kept, sent, tile)
    return lax.psum(
        lax.psum_scatter(matrix, "dp", scatter_dimension=0, tiled=True).astype(jnp.float32), "seq"
    )


def joined(terms, size, widths):
    block = terms.got[0].astype(jnp.float32) + terms.kept[0].astype(jnp.float32)
    got = swap_seq(block.astype(jnp.bfloat16)).astype(jnp.float32)
    here = lax.axis_index("seq") == 0
    first, second = jnp.where(here, block, got), jnp.where(here, got, block)
    parts, at = [], 0
    for index, width in enumerate(widths):
        rows = []
        for _ in range(size if index == len(widths) - 1 else 1):
            rows.append(
                jnp.concatenate([first[:, at : at + width], second[:, at : at + width]], axis=1)
            )
            at += width
        parts.append(jnp.concatenate(rows, axis=0))
    return parts


def per_device(
    tokens,
    cotangent,
    time_index,
    step_table,
    first_gain,
    attn_qkv,
    attn_out,
    second_gain,
    mlp_up,
    up_bias,
    mlp_down,
    down_bias,
    ada_weight,
    ada_bias,
):
    rows, width = tokens.shape[1:]
    dp_rank = lax.axis_index("dp")
    core = dp_rank % 2
    own_cond, silu_back = jax.vjp(
        jax.nn.silu, lax.dynamic_slice_in_dim(step_table, time_index[0], 1, axis=0)
    )
    positions = core * rows + jnp.arange(rows, dtype=jnp.int32)
    cosine, sine = tables(positions)
    tokens = swap_halves(tokens[0])
    time_index = swap_halves(time_index)
    cotangent = swap_halves(cotangent[0])
    cond = jax.nn.silu(lax.dynamic_slice_in_dim(step_table, time_index[0], 1, axis=0))
    ada_float = ada_weight.astype(jnp.float32)
    modulation = jnp.dot(cond, ada_float, precision=highest) + ada_bias.astype(jnp.float32)
    gain1 = first_gain.astype(jnp.float32)
    gain2 = second_gain.astype(jnp.float32)
    cond_row = jnp.pad(cond, ((0, 0), (0, width - cond.shape[1])))
    mods = jnp.concatenate(
        [modulation.reshape(6, width), gain1[None], gain2[None], cond_row, jnp.zeros((7, width))]
    )
    normed1, own_pair = project_key_value(tokens, mods, attn_qkv, cosine, sine, cotangent)
    peer_pair = swap_cores(own_pair)
    core_ref = core[None]
    (
        query, attended, log_total, mixed, d_middle, d_attended, up_keep, up_send,
        down_keep, down_send, up_bias_grad, sums2,
    ) = block_layer(
        core_ref, normed1, attn_qkv, cosine, sine, own_pair, peer_pair, mods,
        up_bias.astype(jnp.float32)[None], down_bias.astype(jnp.float32)[None],
        tokens, cotangent, attn_out, mlp_up, mlp_down,
    )
    hidden = mlp_up.shape[1]
    dp_size = lax.axis_size("dp")
    bits = dp_bits()
    by_steps = split_rows(width) == width // dp_size
    mixed = swap_halves(mixed)

    def blocks(part):
        return part.reshape(dp_size // 2, -1, part.shape[1])

    if by_steps:
        up = Flow(swap_cores(blocks(up_send)), blocks(up_keep))
        down = Flow(swap_cores(blocks(down_send)), blocks(down_keep))
    d_query, away_pair, _ = attend_back(
        query, peer_pair, d_attended, attended, log_total, free=(peer_pair,)
    )
    after = (mixed,)
    if by_steps:
        (down, up), sent = stage(4, [([down], "half"), ([up], bits[1])], (away_pair,))
        after = (sent, mixed)
    back_pair = swap_cores(away_pair)
    d_query, d_pair, _ = attend_back(
        query, own_pair, d_attended, attended, log_total, (d_query, cosine, sine), after
    )
    d_projected, qkv_keep, qkv_send, _ = projected_back(
        core_ref, d_query, d_pair, back_pair, normed1, cosine, sine
    )
    after = ()
    cut = (3 * width // 256 - 1) // 2 * 256
    if by_steps:
        got, kept = swap_cores(blocks(qkv_send)), blocks(qkv_keep)
        one, two = Flow(got, kept, (0, cut)), Flow(got, kept, (cut, 3 * width))
        (one, two), sent = stage(4, [([one], "half"), ([two], bits[1])])
        after = (sent,)
    tokens_grad, small, _ = tokens_back(
        d_projected, attn_qkv, tokens, d_middle, mods, sums2, up_bias_grad, after
    )
    got = swap_cores(small)
    if by_steps:
        (down, up, small), sent = stage(
            4, [([down], bits[1]), ([up], "half")], (), (got, small, True)
        )
        got = swap_seq(small)
        (one, two, small), sent = stage(
            4, [([one], bits[1]), ([two], "half")], (sent,), (got, small, False)
        )
        early, late = [up, down], [one, two]
        for bit, small_bit in zip(bits[2:], bits[1:]):
            early, sent = stage(early[0].count // 2, [(early, bit)], (sent,))
            got = swap_bit(small, small_bit)
            (*late, small), sent = stage(
                late[0].count // 2, [(late, bit)], (sent,), (got, small, False)
            )
        got = swap_bit(small, bits[-1])
        small = jnp.concatenate([small[:-8], got[:-8], small[-8:] + got[-8:]], axis=0)
        up_half, down_half = (hidden + width) // 2, width // 2
        up_rows, down_rows = joined(early[0], hidden // width, (up_half, down_half))
        grouped = jnp.concatenate(joined(late[0], 1, (cut // 2, (3 * width - cut) // 2)), axis=1)
    else:
        small = small + got
        moves = [swap_seq] + [functools.partial(swap_bit, bit=bit) for bit in bits[1:]]
        for move in moves:
            got = move(small)
            small = jnp.concatenate([small[:-8], got[:-8], small[-8:] + got[-8:]], axis=0)
        up_rows = plain_sum(up_keep, up_send, width)
        down_rows = plain_sum(down_keep, down_send, width)
        grouped = plain_sum(qkv_keep, qkv_send, width)
    per_sequence, sums = small[:-8].reshape(-1, 8, width), small[-8:]
    d_mod_all = per_sequence[:, :6].reshape(per_sequence.shape[0], 6 * width)
    cond_all = per_sequence[:, 6, : cond.shape[1]]
    ada_bias_grad = jnp.sum(d_mod_all, axis=0)
    own_columns = d_mod_all.shape[1] // lax.axis_size("dp")
    mine = lax.dynamic_slice_in_dim(d_mod_all, dp_rank * own_columns, own_columns, axis=1)
    ada_weight_grad = lax.dot_general(
        cond_all, mine, (((0,), (0,)), ((), ())), precision=highest
    )
    d_mod_own = jnp.where(lax.axis_index("seq") == core, d_mod_all[:1], d_mod_all[1:2])
    (cond_grad,) = silu_back(jnp.dot(d_mod_own, ada_float.T, precision=highest))
    parts = []
    for index in range(3):
        for start in range(index * HEADS * HD, 3 * width, 3 * HEADS * HD):
            parts.append(grouped[:, start : start + HEADS * HD])
    qkv_rows = jnp.concatenate(parts, axis=1)
    return (
        mixed[None],
        swap_halves(tokens_grad).astype(jnp.float32)[None],
        cond_grad,
        sums[0],
        qkv_rows,
        up_rows[:, hidden:],
        sums[1],
        up_rows[:, :hidden],
        sums[3:7].reshape(-1),
        down_rows,
        sums[2],
        ada_weight_grad,
        ada_bias_grad,
    )


def solution(mesh):
    placed = (
        P("dp", "seq", None),
        P("dp", "seq", None),
        P("dp"),
        P(),
        P(),
        P(),
        P(),
        P(),
        P(),
        P(),
        P(),
        P(),
        P(),
        P(),
    )
    return jax.shard_map(
        per_device,
        mesh=mesh,
        in_specs=placed,
        out_specs=(
            P("dp", "seq", None),
            P("dp", "seq", None),
            P("dp", None),
            P(),
            P("dp", None),
            P("dp", None),
            P(),
            P("dp", None),
            P(),
            P("dp", None),
            P(),
            P(None, "dp"),
            P(),
        ),
        check_vma=False,
    )
```

```python
import functools

import jax
import jax.numpy as jnp
from jax import lax
from jax.experimental import pallas as pl
from jax.experimental.pallas import tpu as pltpu
from jax.sharding import PartitionSpec as P

HD = 64
LOG2E = 1.4426950408889634


highest = lax.Precision.HIGHEST


def tables(positions):
    half_dim = HD // 2
    frequency = jnp.exp(
        -jnp.log(10000.0) * (2.0 * jnp.arange(half_dim, dtype=jnp.float32) / HD)
    )
    angles = positions.astype(jnp.float32)[:, None] * frequency[None, :]
    cosine, sine = jnp.cos(angles), jnp.sin(angles)
    return (
        jnp.concatenate([cosine] * 4, axis=1),
        jnp.concatenate([-sine, sine, -sine, sine], axis=1),
    )


def full(shape):
    return pl.BlockSpec(shape, lambda step: (0,) * len(shape))


def columns(rows, width, first=0):
    return pl.BlockSpec((rows, width), lambda step: (0, step + first))


def shaped(shape, kind):
    return jax.ShapeDtypeStruct(shape, kind)


def far(shape, kind):
    return pltpu.VMEM(shape, kind)


def far(shape, kind):
    return pltpu.HBM(shape, kind)


def store_split(low, core, own, keep, send):
    pairs = low.shape[0] // (2 * own)

    def store(kept):
        for pair in range(pairs):
            rows = slice(pair * own, (pair + 1) * own)
            for parity, target in ((kept, keep), (1 - kept, send)):
                start = (2 * pair + parity) * own
                target[rows, :] = low[start : start + own, :]

    @pl.when(core[0] == 0)
    def _():
        store(0)

    @pl.when(core[0] == 1)
    def _():
        store(1)


def zero_shape():
    return jax.ShapeDtypeStruct((1, 1), jnp.float32)


def scalar_spec():
    return pl.BlockSpec(memory_space=pltpu.SMEM)


def kernel_call(body, steps, in_specs, out_specs, out_shape, scratch, grant):
    call = pl.pallas_call(
        body,
        grid=(steps,),
        in_specs=in_specs,
        out_specs=out_specs,
        out_shape=out_shape,
        scratch_shapes=scratch,
        compiler_params=pltpu.CompilerParams(
            dimension_semantics=("arbitrary",), vmem_limit_bytes=grant * 1024 * 1024
        ),
        cost_estimate=pl.CostEstimate(flops=1, bytes_accessed=1, transcendentals=0),
    )

    def run(*args, free=()):
        placed = []
        for arg in args:
            if arg.size > 4096 and not any(arg is other for other in free):
                arg = pltpu.with_memory_space_constraint(arg, pltpu.HBM)
            placed.append(arg)
        return call(*placed)

    return run


def dot(left, right, left_axis=1, right_axis=0):
    return lax.dot_general(
        left,
        right,
        (((left_axis,), (right_axis,)), ((), ())),
        preferred_element_type=jnp.float32,
    )


def normalized(inputs):
    center = inputs - jnp.mean(inputs, axis=-1, keepdims=True)
    inverse = lax.rsqrt(jnp.mean(center * center, axis=-1, keepdims=True) + 1e-05)
    return center * inverse, inverse


def norm_back(back, hat, inverse, factor):
    scaled = back * factor
    return inverse * (
        scaled
        - jnp.mean(scaled, axis=-1, keepdims=True)
        - hat * jnp.mean(scaled * hat, axis=-1, keepdims=True)
    )


def column_sum(values):
    return jnp.sum(values, axis=0, keepdims=True)


SHIFT1, SCALE1, GATE1, SHIFT2, SCALE2, GATE2, GAIN1, GAIN2, COND = range(9)


def row(ref, index):
    return ref[index : index + 1, :]


def rotate_lanes(values, cosine, sine):
    lane = lax.broadcasted_iota(jnp.int32, cosine.shape, 1)
    lower = (lane % HD) < HD // 2
    parts = []
    for start in range(0, values.shape[1], 128):
        part = values[:, start : start + 128]
        other = jnp.where(lower, pltpu.roll(part, 128 - HD // 2, 1), pltpu.roll(part, HD // 2, 1))
        parts.append(part * cosine + other * sine)
    return jnp.concatenate(parts, axis=1)


HEADS = 4


def key_value_body(
    tokens, mods, key_weight, value_weight, cosine, sine, normed, every, *parts
):
    step = pl.program_id(0)

    @pl.when(step == 0)
    def _():
        hat, _ = normalized(tokens[...].astype(jnp.float32))
        value = hat * row(mods, GAIN1) * (1.0 + row(mods, SCALE1)) + row(mods, SHIFT1)
        normed[...] = value.astype(jnp.bfloat16)

    keys = rotate_lanes(dot(normed[...], key_weight[...]), cosine[...], sine[...])
    values = dot(normed[...], value_weight[...])
    both = jnp.concatenate([keys, values], axis=1).astype(jnp.bfloat16)
    every[...] = both
    for index, part in enumerate(parts):

        @pl.when(step == index)
        def _(part=part):
            part[...] = both


def project_key_value(tokens, mods, weight, cosine, sine):
    rows, width = tokens.shape
    lanes = HEADS * HD
    steps = width // lanes
    low = jnp.bfloat16
    return kernel_call(
        key_value_body,
        steps,
        [
            full((rows, width)),
            full((16, width)),
            columns(width, lanes, steps),
            columns(width, lanes, 2 * steps),
            full((rows, 128)),
            full((rows, 128)),
        ],
        [full((rows, width)), columns(rows, 2 * lanes)] + [full((rows, 2 * lanes))] * steps,
        [far((rows, width), low), far((rows, 2 * width), low)]
        + [far((rows, 2 * lanes), low)] * steps,
        [],
        24,
    )(tokens, mods, weight, weight, cosine, sine, free=(tokens,))


def head_mask(shape, head):
    lane = lax.broadcasted_iota(jnp.int32, shape, 1)
    return jnp.where(lane // HD == head, 1.0, 0.0).astype(jnp.bfloat16)


def head_lanes(head):
    pair, place = divmod(head, 2)
    return slice(pair * 128, (pair + 1) * 128), place, slice(place * HD, (place + 1) * HD)


def value_lanes(lanes):
    return slice(HEADS * HD + lanes.start, HEADS * HD + lanes.stop)


def in_turn(count, first, rest):
    results = []
    ahead = first(0)
    for index in range(count):
        now = ahead
        if index + 1 < count:
            ahead = first(index + 1)
        results.append(rest(index, now))
    return results


def attend_heads(query, pair1, pair2, log_total):
    rows = query.shape[0]

    def first(head):
        lanes, place, _ = head_lanes(head)
        own = query[:, lanes] * head_mask((rows, 128), place)
        return dot(pair1[:, lanes], own, 1, 1), dot(pair2[:, lanes], own, 1, 1)

    def rest(head, scores):
        lanes, place, turned = head_lanes(head)
        scores1, scores2 = scores
        top = jnp.maximum(
            jnp.max(scores1, axis=0, keepdims=True), jnp.max(scores2, axis=0, keepdims=True)
        )
        exps1 = jnp.exp2(scores1 - top)
        exps2 = jnp.exp2(scores2 - top)
        total = column_sum(exps1) + column_sum(exps2)
        lanes = value_lanes(lanes)
        mixed = dot(pair1[:, lanes].T[turned], exps1.astype(jnp.bfloat16)) + dot(
            pair2[:, lanes].T[turned], exps2.astype(jnp.bfloat16)
        )
        log_total[0, head : head + 1, :] = top + jnp.log2(total)
        return mixed * (1.0 / total)

    parts = in_turn(HEADS, first, rest)
    return jnp.concatenate(
        [
            jnp.concatenate(parts[head : head + 2], axis=0).T.astype(jnp.bfloat16)
            for head in range(0, HEADS, 2)
        ],
        axis=1,
    )


def attend_back_body(second, query, pair, grad, attended, log_total, *refs):
    if second:
        before, cosine, sine = refs[:3]
    d_query, d_pair, zero = refs[-3:]
    zero[0, 0] = 0.0
    rows = query.shape[0]
    products = {}

    def first(head):
        lanes, place, _ = head_lanes(head)
        if place == 0:
            product = grad[:, lanes].astype(jnp.float32) * attended[:, lanes].astype(jnp.float32)
            products[head] = products[head + 1] = product.T
        own = query[:, lanes] * head_mask((rows, 128), place)
        own_grad = grad[:, lanes] * head_mask((rows, 128), place)
        scores = dot(pair[:, lanes], own, 1, 1)
        d_probs = dot(pair[:, value_lanes(lanes)], own_grad, 1, 1)
        return own, own_grad, scores, d_probs

    def rest(head, given):
        own, own_grad, scores, d_probs = given
        lanes, place, turned = head_lanes(head)
        delta = column_sum(products[head][turned])
        probs = jnp.exp2(scores - log_total[0, head : head + 1, :])
        d_scores = (probs * (d_probs - delta)).astype(jnp.bfloat16)
        return (
            dot(pair[:, lanes].T[turned], d_scores),
            dot(d_scores, own),
            dot(probs.astype(jnp.bfloat16), own_grad),
        )

    parts = in_turn(HEADS, first, rest)
    for head in range(0, HEADS, 2):
        lanes = head_lanes(head)[0]
        one, two = parts[head : head + 2]
        turned = jnp.concatenate([one[0], two[0]], axis=0).T * HD ** (-0.5)
        if second:
            turned = rotate_lanes(turned + before[:, lanes], cosine[...], -sine[...])
        d_query[:, lanes] = turned.astype(d_query.dtype)
        d_pair[:, lanes] = ((one[1] + two[1]) * (1.0 / LOG2E)).astype(jnp.bfloat16)
        d_pair[:, value_lanes(lanes)] = (one[2] + two[2]).astype(jnp.bfloat16)


def attend_back(query, pair, grad, attended, log_total, before=None, after=(), free=()):
    rows, width = query.shape
    lanes = HEADS * HD
    steps = width // lanes
    block = columns(rows, lanes)
    second = before is not None
    extra = list(before) if second else []
    extra_specs = [block, full((rows, 128)), full((rows, 128))] if second else []
    return kernel_call(
        functools.partial(attend_back_body, second),
        steps,
        [
            block,
            columns(rows, 2 * lanes),
            block,
            block,
            pl.BlockSpec((1, HEADS, rows), lambda step: (step, 0, 0)),
        ]
        + extra_specs
        + [pl.BlockSpec(memory_space=pl.ANY)] * len(after),
        [block, columns(rows, 2 * lanes), scalar_spec()],
        [
            far((rows, width), jnp.bfloat16 if second else jnp.float32),
            far((rows, 2 * width), jnp.bfloat16),
            zero_shape(),
        ],
        [],
        28,
    )(query, pair, grad, attended, log_total, *extra, *after, free=free)


def block_body(
    own_up, own_down, attend_steps, hidden_steps,
    core, normed1, query_weight, cosine, sine, mods, up_bias, down_bias, *refs,
):
    pairs_far, refs = refs[: 2 * attend_steps], refs[2 * attend_steps :]
    (
        tokens_far, cotangent_far, out_far, up_far, down_far,
        query, attended, log_total, mixed, d_middle, d_attended, up_keep, up_send,
        down_keep, down_send, bias_grad, sums, peer_far,
        tokens, cotangent, out_weight, up_weight, down_weight, arrived,
        own_pairs, peer_pairs, pair_arrived, left,
        all_attended, normed, d_ffn, branch, middle, forward, back,
    ) = refs
    step = pl.program_id(0)
    tile = up_bias.shape[1]
    lanes = 2 * HEADS * HD
    own_arrivals, peer_arrivals, departures = [], [], []
    for index in range(attend_steps):
        own_arrivals.append(
            pltpu.make_async_copy(
                pairs_far[index], own_pairs.at[index], pair_arrived.at[0, index]
            )
        )
        peer_arrivals.append(
            pltpu.make_async_copy(
                pairs_far[attend_steps + index], peer_pairs.at[index], pair_arrived.at[1, index]
            )
        )
        departures.append(
            pltpu.make_async_copy(
                peer_pairs.at[index],
                peer_far.at[:, pl.ds(index * lanes, lanes)],
                left.at[index],
            )
        )
    arrivals = [
        pltpu.make_async_copy(source, target, arrived.at[index])
        for index, (source, target) in enumerate(
            (
                (tokens_far, tokens),
                (cotangent_far, cotangent),
                (out_far, out_weight),
                (up_far, up_weight),
                (down_far, down_weight),
            )
        )
    ]

    @pl.when(step == 0)
    def _():
        for index in range(attend_steps):
            own_arrivals[index].start()
            peer_arrivals[index].start()
        for arrival in arrivals:
            arrival.start()

    for index in range(attend_steps):

        @pl.when(step == index)
        def _(index=index):
            own_arrivals[index].wait()
            peer_arrivals[index].wait()
            departures[index].start()

    @pl.when(step < attend_steps)
    def _():
        value = rotate_lanes(dot(normed1[...], query_weight[...]), cosine[...], sine[...])
        query[...] = (value * (LOG2E * HD ** (-0.5))).astype(jnp.bfloat16)
        found = attend_heads(query, own_pairs.at[step], peer_pairs.at[step], log_total)
        attended[...] = found
        for index in range(attend_steps):

            @pl.when(step == index)
            def _(index=index):
                heads = HEADS * HD
                all_attended[:, index * heads : (index + 1) * heads] = found

    @pl.when(step == attend_steps)
    def _():
        for arrival in arrivals:
            arrival.wait()
        for departure in departures:
            departure.wait()
        turned = dot(all_attended[...], out_weight[...])
        branch[...] = turned.astype(jnp.bfloat16)
        value = tokens[...].astype(jnp.float32) + row(mods, GATE1) * turned
        middle[...] = value
        hat, _ = normalized(value)
        value = hat * row(mods, GAIN2) * (1.0 + row(mods, SCALE2)) + row(mods, SHIFT2)
        normed[...] = value.astype(jnp.bfloat16)
        low = (row(mods, GATE2) * cotangent[...].astype(jnp.float32)).astype(jnp.bfloat16)
        d_ffn[...] = low
        sums[4:5, :] = column_sum(low.astype(jnp.float32))
        forward[...] = jnp.zeros_like(forward)
        back[...] = jnp.zeros_like(back)

    @pl.when((step >= attend_steps) & (step < attend_steps + hidden_steps))
    def _():
        place = pl.ds(pl.multiple_of((step - attend_steps) * tile, tile), tile)
        pre = dot(normed[...], up_weight[:, place]) + up_bias[...]
        d_activated = dot(d_ffn[...], down_weight[place, :], 1, 1)
        root = 0.7978845608028654
        square = pre * pre
        bent = jnp.tanh(root * pre * (1.0 + 0.044715 * square))
        half = 0.5 + 0.5 * bent
        slope = half + (0.5 * root) * pre * (1.0 - bent * bent) * (1.0 + 0.134145 * square)
        low = (pre * half).astype(jnp.bfloat16)
        d_pre = d_activated * slope
        d_low = d_pre.astype(jnp.bfloat16)
        bias_grad[...] = column_sum(d_pre)
        down_grad = dot(low, d_ffn[...], 0, 0).astype(jnp.bfloat16)
        store_split(down_grad, core, own_down, down_keep, down_send)
        up_grad = dot(normed[...], d_low, 0, 0).astype(jnp.bfloat16)
        store_split(up_grad, core, own_up, up_keep, up_send)
        forward[...] += dot(low, down_weight[place, :])
        back[...] += dot(d_low, up_weight[:, place], 1, 1)

    @pl.when(step == attend_steps + hidden_steps)
    def _():
        grad = cotangent[...].astype(jnp.float32)
        held = middle[...]
        hat, inverse = normalized(held)
        factor = row(mods, GAIN2) * (1.0 + row(mods, SCALE2))
        value = back[...]
        d_value = grad + norm_back(value, hat, inverse, factor)
        d_middle[...] = d_value
        d_branch = (row(mods, GATE1) * d_value).astype(jnp.bfloat16)
        d_attended[...] = dot(d_branch, out_weight[...], 1, 1).astype(jnp.bfloat16)
        out_grad = dot(all_attended[...], d_branch, 0, 0).astype(jnp.bfloat16)
        store_split(out_grad, core, own_up, up_keep, up_send)
        ffn = forward[...] + down_bias[...]
        mixed[...] = (held + row(mods, GATE2) * ffn).astype(jnp.bfloat16)
        sums[0:1, :] = column_sum(value)
        sums[1:2, :] = column_sum(value * hat)
        sums[2:3, :] = column_sum(d_value * branch[...].astype(jnp.float32))
        sums[3:4, :] = column_sum(grad * ffn)
        sums[5:8, :] = jnp.zeros_like(sums[5:8, :])


def split_rows(rows):
    own = rows // lax.axis_size("dp")
    return own if own % 16 == 0 else rows // 2


def block_layer(
    core, normed1, qkv_weight, cosine, sine, mods, up_bias, down_bias, own, peer,
    tokens, cotangent, out_weight, up_weight, down_weight,
):
    rows, width = tokens.shape
    hidden = up_weight.shape[1]
    tile = width
    lanes = HEADS * HD
    attend_steps = width // lanes
    hidden_steps = hidden // tile
    own_down = hidden // lax.axis_size("dp")
    if own_down % 16 > 0:
        own_down = tile // 2

    def heads(first=0):
        return pl.BlockSpec(
            (rows, lanes), lambda step: (0, jnp.minimum(step, attend_steps - 1) + first)
        )

    def tiles(step):
        return jnp.clip(step - attend_steps, 0, hidden_steps - 1)

    def up_tiles(step):
        return jnp.clip(step - attend_steps, 0, hidden_steps)

    block = full((rows, width))
    far_spec = pl.BlockSpec(memory_space=pl.ANY)
    low = jnp.bfloat16
    up_spec = pl.BlockSpec((width // 2, tile), lambda step: (0, up_tiles(step)))
    down_spec = pl.BlockSpec((tile // 2, width), lambda step: (tiles(step), 0))
    return kernel_call(
        functools.partial(
            block_body, split_rows(width), own_down, attend_steps, hidden_steps
        ),
        attend_steps + hidden_steps + 1,
        [
            scalar_spec(),
            block,
            pl.BlockSpec((width, lanes), lambda step: (0, jnp.minimum(step, attend_steps - 1))),
            full((rows, 128)),
            full((rows, 128)),
            full((16, width)),
            pl.BlockSpec((1, tile), lambda step: (0, tiles(step))),
            full((1, width)),
        ]
        + [far_spec] * (2 * attend_steps + 5),
        [
            heads(),
            heads(),
            pl.BlockSpec(
                (1, HEADS, rows), lambda step: (jnp.minimum(step, attend_steps - 1), 0, 0)
            ),
            block,
            block,
            block,
            up_spec,
            up_spec,
            down_spec,
            down_spec,
            pl.BlockSpec((1, tile), lambda step: (0, tiles(step))),
            full((8, width)),
            far_spec,
        ],
        [
            far((rows, width), low),
            far((rows, width), low),
            far((attend_steps, HEADS, rows), jnp.float32),
            far((rows, width), low),
            far((rows, width), jnp.float32),
            far((rows, width), low),
            far((width // 2, hidden + width), low),
            far((width // 2, hidden + width), low),
            far((hidden // 2, width), low),
            far((hidden // 2, width), low),
            far((1, hidden), jnp.float32),
            far((8, width), jnp.float32),
            far((rows, 2 * width), low),
        ],
        [
            pltpu.VMEM((rows, width), low),
            pltpu.VMEM((rows, width), low),
            pltpu.VMEM((width, width), low),
            pltpu.VMEM((width, hidden), low),
            pltpu.VMEM((hidden, width), low),
            pltpu.SemaphoreType.DMA((5,)),
            pltpu.VMEM((attend_steps, rows, 2 * lanes), low),
            pltpu.VMEM((attend_steps, rows, 2 * lanes), low),
            pltpu.SemaphoreType.DMA((2, attend_steps)),
            pltpu.SemaphoreType.DMA((attend_steps,)),
            pltpu.VMEM((rows, width), low),
            pltpu.VMEM((rows, width), low),
            pltpu.VMEM((rows, width), low),
            pltpu.VMEM((rows, width), low),
            pltpu.VMEM((rows, width), jnp.float32),
            pltpu.VMEM((rows, width), jnp.float32),
            pltpu.VMEM((rows, width), jnp.float32),
        ],
        58,
    )(
        core, normed1, qkv_weight, cosine, sine, mods, up_bias, down_bias, *own, *peer,
        tokens, cotangent, out_weight, up_weight, down_weight,
        free=(*peer, cotangent, tokens),
    )


def projected_back_body(
    own, core, d_query, d_pair, peer_pair, normed, cosine, sine, d_projected, zero, *parts
):
    zero[0, 0] = 0.0
    lanes = HEADS * HD
    pair = d_pair[...].astype(jnp.float32) + peer_pair[...].astype(jnp.float32)
    keys = rotate_lanes(pair[:, :lanes], cosine[...], -sine[...]).astype(jnp.bfloat16)
    low = jnp.concatenate([d_query[...], keys, pair[:, lanes:].astype(jnp.bfloat16)], axis=1)
    d_projected[...] = low
    grad = dot(normed[...], low, 0, 0).astype(jnp.bfloat16)
    for index in range(3):
        part = grad[:, index * lanes : (index + 1) * lanes]
        store_split(part, core, own, parts[2 * index], parts[2 * index + 1])


def projected_back(core, d_query, d_pair, peer_pair, normed, cosine, sine):
    rows, width = normed.shape
    lanes = HEADS * HD
    return kernel_call(
        functools.partial(projected_back_body, split_rows(width)),
        width // lanes,
        [
            scalar_spec(),
            columns(rows, lanes),
            columns(rows, 2 * lanes),
            columns(rows, 2 * lanes),
            full((rows, width)),
            full((rows, 128)),
            full((rows, 128)),
        ],
        [columns(rows, 3 * lanes), scalar_spec()] + [columns(width // 2, lanes)] * 6,
        [far((rows, 3 * width), jnp.bfloat16), zero_shape()]
        + [far((width // 2, width), jnp.bfloat16)] * 6,
        [],
        32,
    )(core, d_query, d_pair, peer_pair, normed, cosine, sine, free=(peer_pair,))


def tokens_back_body(
    d_projected, weight1, weight2, weight3, tokens, d_middle, mods, sums, bias_grad, *refs
):
    out, small, zero, total = refs[-4:]
    zero[0, 0] = 0.0
    step = pl.program_id(0)
    width = tokens.shape[1]
    lanes = HEADS * HD
    part = sum(
        dot(d_projected[:, index * lanes : (index + 1) * lanes], weight[...], 1, 1)
        for index, weight in enumerate((weight1, weight2, weight3))
    )

    @pl.when(step == 0)
    def _():
        total[...] = part

    @pl.when(step > 0)
    def _():
        total[...] += part

    @pl.when(step == pl.num_programs(0) - 1)
    def _():
        back = total[...]
        hat, inverse = normalized(tokens[...].astype(jnp.float32))
        scale1 = 1.0 + row(mods, SCALE1)
        gain1 = row(mods, GAIN1)
        out[...] = (d_middle[...] + norm_back(back, hat, inverse, gain1 * scale1)).astype(
            jnp.bfloat16
        )
        hat_sum1 = column_sum(back * hat)
        hat_sum2 = row(sums, 1)
        rows = [
            column_sum(back),
            hat_sum1 * gain1,
            row(sums, 2),
            row(sums, 0),
            hat_sum2 * row(mods, GAIN2),
            row(sums, 3),
            row(mods, COND) * 0.5,
            jnp.zeros_like(hat_sum1),
            hat_sum1 * scale1,
            hat_sum2 * (1.0 + row(mods, SCALE2)),
            row(sums, 4),
        ]
        for index in range(bias_grad.shape[1] // width):
            rows.append(bias_grad[:, index * width : (index + 1) * width])
        for index, value in enumerate(rows):
            small[index : index + 1, :] = value
        small[len(rows) :, :] = jnp.zeros_like(small[len(rows) :, :])


def tokens_back(d_projected, weight, tokens, d_middle, mods, sums, bias_grad):
    rows, width = tokens.shape
    block = full((rows, width))
    lanes = HEADS * HD
    steps = width // lanes
    return kernel_call(
        tokens_back_body,
        steps,
        [
            columns(rows, 3 * lanes),
            columns(width, lanes),
            columns(width, lanes, steps),
            columns(width, lanes, 2 * steps),
            block,
            block,
            full((16, width)),
            full((8, width)),
            full(bias_grad.shape),
        ],
        [block, full((16, width)), scalar_spec()],
        [far((rows, width), jnp.bfloat16), far((16, width), jnp.float32), zero_shape()],
        [pltpu.VMEM((rows, width), jnp.float32)],
        32,
    )(d_projected, weight, weight, weight, tokens, d_middle, mods, sums, bias_grad)


def swap_halves(block):
    count = lax.axis_size("dp") * lax.axis_size("seq")
    target = {1: 2, 2: 1}
    perm = [(i, i - i % 4 + target.get(i % 4, i % 4)) for i in range(count)]
    return lax.ppermute(block, ("dp", "seq"), perm)


def swap_bit(block, bit):
    return lax.ppermute(block, "dp", [(i, i ^ bit) for i in range(lax.axis_size("dp"))])


def swap_cores(block):
    return swap_bit(block, 1)


def swap_seq(block):
    return lax.ppermute(block, "seq", [(0, 1), (1, 0)])


def dp_bits():
    bits, bit = [], 1
    while bit < lax.axis_size("dp"):
        bits.append(bit)
        bit *= 2
    return bits


def pick(block, axis, index):
    return lax.dynamic_index_in_dim(block, index, axis, keepdims=False)


class Flow:
    def __init__(self, got, kept, lanes=None):
        self.got, self.kept = got, kept
        self.lanes = lanes or (0, kept.shape[2])
        self.count, self.rest = kept.shape[:2]
        self.width = self.lanes[1] - self.lanes[0]


def stage_body(jobs, counts, mine, *refs):
    inputs = refs[: counts[0]]
    outputs = refs[counts[0] + counts[1] :]
    for place, (half, sources, target) in enumerate(jobs):
        if half is None:
            total = sum(inputs[place][...].astype(jnp.float32) for place in sources[0][:2])
            outputs[target][...] = total.astype(jnp.bfloat16)
            continue
        sent, kept = outputs[target], outputs[target + 1]

        def store(out, which, half=half, sources=sources):
            at = 0
            for one, two, start, stop, rows in sources:
                if half:
                    middle = (start + stop) // 2
                    lanes = slice(middle, stop) if which else slice(start, middle)
                    total = inputs[one][:, :, lanes].astype(jnp.float32)
                    total = total + inputs[two][:, :, lanes].astype(jnp.float32)
                    out[:, :, at : at + stop - middle] = total.astype(jnp.bfloat16)
                    at += stop - middle
                    continue
                for pair in range(out.shape[0]):
                    block = 2 * pair + which
                    total = inputs[one][block, :, start:stop].astype(jnp.float32)
                    total = total + inputs[two][block, :, start:stop].astype(jnp.float32)
                    total = total.astype(jnp.bfloat16)
                    column = at
                    for first in range(0, total.shape[0], rows):
                        out[pair, :, column : column + stop - start] = total[first : first + rows]
                        column += stop - start
                at = column

        for which in range(2):

            @pl.when(mine[place] == which)
            def _(which=which, sent=sent, kept=kept, store=store):
                store(kept, which)
                store(sent, 1 - which)


def small_body(steps, first, one, two, out):
    rows = one.shape[0] - 8

    @pl.when(pl.program_id(0) == 0)
    def _():
        if first:
            out[...] = one[...] + two[...]
        else:
            out[:rows, :] = one[:rows, :]
            out[rows : 2 * rows, :] = two[:rows, :]
            out[2 * rows :, :] = one[rows:, :] + two[rows:, :]


def stage(steps, jobs, after=(), small=None, free=()):
    seq_rank, dp_rank = lax.axis_index("seq"), lax.axis_index("dp")
    inputs, in_specs, specs, out_specs, out_shape, mine = [], [], [], [], [], []
    free = [*free] + [flow.got for flows, _ in jobs for flow in flows]

    def place_of(array):
        for index, other in enumerate(inputs):
            if other is array:
                return index
        inputs.append(array)
        each = array.shape[0] // steps
        in_specs.append(pl.BlockSpec((each,) + array.shape[1:], lambda at: (at, 0, 0)))
        return len(inputs) - 1

    for flows, step in jobs:
        half = None if step == "sum" else step == "half"
        rest, count = flows[0].rest, flows[0].count
        sources = [
            (place_of(flow.got), place_of(flow.kept), *flow.lanes, rest) for flow in flows
        ]
        if half is None:
            shape = flows[0].kept.shape
            mine.append(seq_rank)
        elif half:
            shape = (count, rest, sum(flow.width for flow in flows) // 2)
            mine.append(seq_rank)
        else:
            width = sum(flow.width * flow.rest // rest for flow in flows)
            shape = (count // 2, rest, width)
            mine.append((dp_rank // step) % 2)
        specs.append((half, sources, len(out_shape)))
        results = 1 if half is None else 2
        out_shape += [far(shape, jnp.bfloat16)] * results
        block = (shape[0] // steps,) + shape[1:]
        out_specs += [pl.BlockSpec(block, lambda at: (at, 0, 0))] * results
    counts = (len(inputs), len(after))
    extra = []
    if small is not None:
        got, kept, first = small
        extra = [kept, got]
        rows = kept.shape[0] if first else 2 * kept.shape[0] - 8
        out_shape.append(far((rows, kept.shape[1]), jnp.float32))
        out_specs.append(full((rows, kept.shape[1])))

    def body(mine, *refs):
        if small is None:
            stage_body(specs, counts, mine, *refs)
            return
        main, ends = refs[: sum(counts)], refs[sum(counts) :]
        small_body(steps, first, ends[0], ends[1], ends[-1])
        stage_body(specs, counts, mine, *main, *ends[2:-1])

    results = kernel_call(
        body,
        steps,
        [scalar_spec()]
        + in_specs
        + [pl.BlockSpec(memory_space=pl.ANY)] * len(after)
        + [full(array.shape) for array in extra],
        out_specs,
        out_shape,
        [],
        40,
    )(jnp.stack(mine), *inputs, *after, *extra, free=(*free, *extra))
    new = []
    for (flows, step), (_, _, target) in zip(jobs, specs):
        sent = results[target]
        got = swap_seq(sent) if isinstance(step, str) else swap_bit(sent, step)
        new.append(Flow(got, sent if step == "sum" else results[target + 1]))
    if small is not None:
        new.append(results[-1])
    return new, results[0]


def from_tiles(kept, sent, tile):
    rows, width = 2 * kept.shape[0], kept.shape[1]
    core = lax.axis_index("dp") % 2
    first = jnp.where(core == 0, kept, sent).reshape(rows // tile, 1, tile // 2, width)
    second = jnp.where(core == 0, sent, kept).reshape(rows // tile, 1, tile // 2, width)
    return jnp.concatenate([first, second], axis=1).reshape(rows, width)


def plain_sum(kept, sent, tile):
    matrix = from_tiles(kept, sent, tile)
    return lax.psum(
        lax.psum_scatter(matrix, "dp", scatter_dimension=0, tiled=True).astype(jnp.float32), "seq"
    )


def joined(terms, size, widths):
    block, got = terms.kept[0].astype(jnp.float32), terms.got[0].astype(jnp.float32)
    here = lax.axis_index("seq") == 0
    first, second = jnp.where(here, block, got), jnp.where(here, got, block)
    parts, at = [], 0
    for index, width in enumerate(widths):
        rows = []
        for _ in range(size if index == len(widths) - 1 else 1):
            rows.append(
                jnp.concatenate([first[:, at : at + width], second[:, at : at + width]], axis=1)
            )
            at += width
        parts.append(jnp.concatenate(rows, axis=0))
    return parts


def per_device(
    tokens,
    cotangent,
    time_index,
    step_table,
    first_gain,
    attn_qkv,
    attn_out,
    second_gain,
    mlp_up,
    up_bias,
    mlp_down,
    down_bias,
    ada_weight,
    ada_bias,
):
    rows, width = tokens.shape[1:]
    dp_rank = lax.axis_index("dp")
    core = dp_rank % 2
    own_cond, silu_back = jax.vjp(
        jax.nn.silu, lax.dynamic_slice_in_dim(step_table, time_index[0], 1, axis=0)
    )
    positions = core * rows + jnp.arange(rows, dtype=jnp.int32)
    cosine, sine = tables(positions)
    tokens = swap_halves(tokens[0])
    time_index = swap_halves(time_index)
    cotangent = swap_halves(cotangent[0])
    cond = jax.nn.silu(lax.dynamic_slice_in_dim(step_table, time_index[0], 1, axis=0))
    ada_float = ada_weight.astype(jnp.float32)
    modulation = jnp.dot(cond, ada_float, precision=highest) + ada_bias.astype(jnp.float32)
    gain1 = first_gain.astype(jnp.float32)
    gain2 = second_gain.astype(jnp.float32)
    cond_row = jnp.pad(cond, ((0, 0), (0, width - cond.shape[1])))
    mods = jnp.concatenate(
        [modulation.reshape(6, width), gain1[None], gain2[None], cond_row, jnp.zeros((7, width))]
    )
    normed1, own_pair, *own_parts = project_key_value(tokens, mods, attn_qkv, cosine, sine)
    peer_parts = [swap_cores(part) for part in own_parts]
    core_ref = core[None]
    (
        query, attended, log_total, mixed, d_middle, d_attended, up_keep, up_send,
        down_keep, down_send, up_bias_grad, sums2, peer_pair,
    ) = block_layer(
        core_ref, normed1, attn_qkv, cosine, sine, mods,
        up_bias.astype(jnp.float32)[None], down_bias.astype(jnp.float32)[None],
        own_parts, peer_parts,
        tokens, cotangent, attn_out, mlp_up, mlp_down,
    )
    hidden = mlp_up.shape[1]
    dp_size = lax.axis_size("dp")
    bits = dp_bits()
    by_steps = split_rows(width) == width // dp_size
    mixed = swap_halves(mixed)

    def blocks(part):
        return part.reshape(dp_size // 2, -1, part.shape[1])

    if by_steps:
        up = Flow(swap_cores(blocks(up_send)), blocks(up_keep))
        down = Flow(swap_cores(blocks(down_send)), blocks(down_keep))
    d_query, away_pair, _ = attend_back(query, peer_pair, d_attended, attended, log_total)
    after = ()
    if by_steps:
        (down, up), sent = stage(
            4, [([down], "half"), ([up], bits[1])], (away_pair, mixed), free=(mixed,)
        )
        after = (sent,)
    back_pair = swap_cores(away_pair)
    d_query, d_pair, _ = attend_back(
        query, own_pair, d_attended, attended, log_total, (d_query, cosine, sine), after
    )
    d_projected, _, *qkv_parts = projected_back(
        core_ref, d_query, d_pair, back_pair, normed1, cosine, sine
    )
    third = HEADS * HD
    if by_steps:
        queries, keys, values = [
            (swap_cores(blocks(send)), blocks(keep))
            for keep, send in zip(qkv_parts[::2], qkv_parts[1::2])
        ]
        one = [Flow(*queries), Flow(*values, (0, third))]
        two = [Flow(*keys), Flow(*values, (third, width))]
    tokens_grad, small, _ = tokens_back(
        d_projected, attn_qkv, tokens, d_middle, mods, sums2, up_bias_grad
    )
    got = swap_cores(small)
    def doubled(small, got):
        return jnp.concatenate([small[:-8], got[:-8], small[-8:] + got[-8:]], axis=0)

    if by_steps:
        (down, up, one, two, small), sent = stage(
            4,
            [([down], bits[1]), ([up], "half"), (one, "half"), (two, bits[1])],
            (),
            (got, small, True),
        )
        early = [up, down]
        two = [Flow(two.got, two.kept, lanes) for lanes in ((0, width), (width, two.width))]
        late = [one, two]
        moves = [functools.partial(swap_bit, bit=bit) for bit in bits[2:] + bits[1:2]]
        moves.append(swap_seq)

        def next_stage(jobs, count):
            nonlocal small, sent
            extra = (moves.pop(0)(small), small, False) if len(moves) > 0 else None
            flows, sent = stage(count, jobs, (sent,), extra)
            if extra is not None:
                small = flows.pop()
            return flows

        early = next_stage([(early, bits[2])], early[0].count // 2)
        late = next_stage([([one], bits[1]), (two, "half")], 4)
        for index, bit in enumerate(bits[3:]):
            early = next_stage([(early, bit)], early[0].count // 2)
            late = next_stage([(late, bits[2 + index])], late[0].count // 2)
        early = next_stage([(early, "sum")], 1)
        late = next_stage([(late, bits[-1])], late[0].count // 2)
        late = next_stage([(late, "sum")], 1)
        while len(moves) > 0:
            small = doubled(small, moves.pop(0)(small))
        up_half, down_half = (hidden + width) // 2, width // 2
        up_rows, down_rows = joined(early[0], hidden // width, (up_half, down_half))
        query_rows, value_rows1, key_rows, value_rows2 = joined(
            late[0], 1, (width // 2, third // 2, width // 2, (width - third) // 2)
        )
        qkv_rows = jnp.concatenate([query_rows, key_rows, value_rows1, value_rows2], axis=1)
    else:
        small = small + got
        moves = [functools.partial(swap_bit, bit=bit) for bit in bits[2:] + bits[1:2]]
        for move in moves + [swap_seq]:
            small = doubled(small, move(small))
        up_rows = plain_sum(up_keep, up_send, width)
        down_rows = plain_sum(down_keep, down_send, width)
        qkv_rows = jnp.concatenate(
            [
                plain_sum(keep, send, width)
                for keep, send in zip(qkv_parts[::2], qkv_parts[1::2])
            ],
            axis=1,
        )
    per_sequence, sums = small[:-8].reshape(-1, 8, width), small[-8:]
    d_mod_all = per_sequence[:, :6].reshape(per_sequence.shape[0], 6 * width)
    cond_all = per_sequence[:, 6, : cond.shape[1]]
    ada_bias_grad = jnp.sum(d_mod_all, axis=0)
    own_columns = d_mod_all.shape[1] // lax.axis_size("dp")
    mine = lax.dynamic_slice_in_dim(d_mod_all, dp_rank * own_columns, own_columns, axis=1)
    ada_weight_grad = lax.dot_general(
        cond_all, mine, (((0,), (0,)), ((), ())), precision=highest
    )
    other = d_mod_all.shape[0] // 2
    d_mod_own = jnp.where(
        lax.axis_index("seq") == core, d_mod_all[:1], d_mod_all[other : other + 1]
    )
    (cond_grad,) = silu_back(jnp.dot(d_mod_own, ada_float.T, precision=highest))
    return (
        mixed[None],
        swap_halves(tokens_grad).astype(jnp.float32)[None],
        cond_grad,
        sums[0],
        qkv_rows,
        up_rows[:, hidden:],
        sums[1],
        up_rows[:, :hidden],
        sums[3:7].reshape(-1),
        down_rows,
        sums[2],
        ada_weight_grad,
        ada_bias_grad,
    )


def solution(mesh):
    placed = (
        P("dp", "seq", None),
        P("dp", "seq", None),
        P("dp"),
        P(),
        P(),
        P(),
        P(),
        P(),
        P(),
        P(),
        P(),
        P(),
        P(),
        P(),
    )
    return jax.shard_map(
        per_device,
        mesh=mesh,
        in_specs=placed,
        out_specs=(
            P("dp", "seq", None),
            P("dp", "seq", None),
            P("dp", None),
            P(),
            P("dp", None),
            P("dp", None),
            P(),
            P("dp", None),
            P(),
            P("dp", None),
            P(),
            P(None, "dp"),
            P(),
        ),
        check_vma=False,
    )
```

```python
import functools

import jax
import jax.numpy as jnp
from jax import lax
from jax.experimental import pallas as pl
from jax.experimental.pallas import tpu as pltpu
from jax.sharding import PartitionSpec as P

HD = 64
LOG2E = 1.4426950408889634


highest = lax.Precision.HIGHEST


def tables(positions):
    half_dim = HD // 2
    frequency = jnp.exp(
        -jnp.log(10000.0) * (2.0 * jnp.arange(half_dim, dtype=jnp.float32) / HD)
    )
    angles = positions.astype(jnp.float32)[:, None] * frequency[None, :]
    cosine, sine = jnp.cos(angles), jnp.sin(angles)
    return (
        jnp.concatenate([cosine] * 4, axis=1),
        jnp.concatenate([-sine, sine, -sine, sine], axis=1),
    )


def full(shape):
    return pl.BlockSpec(shape, lambda step: (0,) * len(shape))


def columns(rows, width, first=0):
    return pl.BlockSpec((rows, width), lambda step: (0, step + first))


def shaped(shape, kind):
    return jax.ShapeDtypeStruct(shape, kind)


def far(shape, kind):
    return pltpu.VMEM(shape, kind)


def far(shape, kind):
    return pltpu.HBM(shape, kind)


def store_split(low, core, own, keep, send):
    pairs = low.shape[0] // (2 * own)

    def store(kept):
        for pair in range(pairs):
            rows = slice(pair * own, (pair + 1) * own)
            for parity, target in ((kept, keep), (1 - kept, send)):
                start = (2 * pair + parity) * own
                target[rows, :] = low[start : start + own, :]

    @pl.when(core[0] == 0)
    def _():
        store(0)

    @pl.when(core[0] == 1)
    def _():
        store(1)


def zero_shape():
    return jax.ShapeDtypeStruct((1, 1), jnp.float32)


def scalar_spec():
    return pl.BlockSpec(memory_space=pltpu.SMEM)


def kernel_call(body, steps, in_specs, out_specs, out_shape, scratch, grant):
    call = pl.pallas_call(
        body,
        grid=(steps,),
        in_specs=in_specs,
        out_specs=out_specs,
        out_shape=out_shape,
        scratch_shapes=scratch,
        compiler_params=pltpu.CompilerParams(
            dimension_semantics=("arbitrary",), vmem_limit_bytes=grant * 1024 * 1024
        ),
        cost_estimate=pl.CostEstimate(flops=1, bytes_accessed=1, transcendentals=0),
    )

    def run(*args, free=()):
        placed = []
        for arg in args:
            if arg.size > 4096 and not any(arg is other for other in free):
                arg = pltpu.with_memory_space_constraint(arg, pltpu.HBM)
            placed.append(arg)
        return call(*placed)

    return run


def dot(left, right, left_axis=1, right_axis=0):
    return lax.dot_general(
        left,
        right,
        (((left_axis,), (right_axis,)), ((), ())),
        preferred_element_type=jnp.float32,
    )


def normalized(inputs):
    center = inputs - jnp.mean(inputs, axis=-1, keepdims=True)
    inverse = lax.rsqrt(jnp.mean(center * center, axis=-1, keepdims=True) + 1e-05)
    return center * inverse, inverse


def norm_back(back, hat, inverse, factor):
    scaled = back * factor
    return inverse * (
        scaled
        - jnp.mean(scaled, axis=-1, keepdims=True)
        - hat * jnp.mean(scaled * hat, axis=-1, keepdims=True)
    )


def column_sum(values):
    return jnp.sum(values, axis=0, keepdims=True)


SHIFT1, SCALE1, GATE1, SHIFT2, SCALE2, GATE2, GAIN1, GAIN2, COND = range(9)


def row(ref, index):
    return ref[index : index + 1, :]


def rotate_lanes(values, cosine, sine):
    lane = lax.broadcasted_iota(jnp.int32, cosine.shape, 1)
    lower = (lane % HD) < HD // 2
    parts = []
    for start in range(0, values.shape[1], 128):
        part = values[:, start : start + 128]
        other = jnp.where(lower, pltpu.roll(part, 128 - HD // 2, 1), pltpu.roll(part, HD // 2, 1))
        parts.append(part * cosine + other * sine)
    return jnp.concatenate(parts, axis=1)


HEADS = 4


def key_value_body(
    tokens, mods, key_weight, value_weight, cosine, sine, normed, every, *parts
):
    step = pl.program_id(0)

    @pl.when(step == 0)
    def _():
        hat, _ = normalized(tokens[...].astype(jnp.float32))
        value = hat * row(mods, GAIN1) * (1.0 + row(mods, SCALE1)) + row(mods, SHIFT1)
        normed[...] = value.astype(jnp.bfloat16)

    keys = rotate_lanes(dot(normed[...], key_weight[...]), cosine[...], sine[...])
    values = dot(normed[...], value_weight[...])
    both = jnp.concatenate([keys, values], axis=1).astype(jnp.bfloat16)
    every[...] = both
    for index, part in enumerate(parts):

        @pl.when(step == index)
        def _(part=part):
            part[...] = both


def project_key_value(tokens, mods, weight, cosine, sine):
    rows, width = tokens.shape
    lanes = HEADS * HD
    steps = width // lanes
    low = jnp.bfloat16
    return kernel_call(
        key_value_body,
        steps,
        [
            full((rows, width)),
            full((16, width)),
            columns(width, lanes, steps),
            columns(width, lanes, 2 * steps),
            full((rows, 128)),
            full((rows, 128)),
        ],
        [full((rows, width)), columns(rows, 2 * lanes)] + [full((rows, 2 * lanes))] * steps,
        [far((rows, width), low), far((rows, 2 * width), low)]
        + [far((rows, 2 * lanes), low)] * steps,
        [],
        24,
    )(tokens, mods, weight, weight, cosine, sine, free=(tokens,))


def head_mask(shape, head):
    lane = lax.broadcasted_iota(jnp.int32, shape, 1)
    return jnp.where(lane // HD == head, 1.0, 0.0).astype(jnp.bfloat16)


def head_lanes(head):
    pair, place = divmod(head, 2)
    return slice(pair * 128, (pair + 1) * 128), place, slice(place * HD, (place + 1) * HD)


def value_lanes(lanes):
    return slice(HEADS * HD + lanes.start, HEADS * HD + lanes.stop)


def in_turn(count, first, rest):
    results = []
    ahead = first(0)
    for index in range(count):
        now = ahead
        if index + 1 < count:
            ahead = first(index + 1)
        results.append(rest(index, now))
    return results


def attend_heads(query, pair1, pair2, log_total):
    rows = query.shape[0]

    def first(head):
        lanes, place, _ = head_lanes(head)
        own = query[:, lanes] * head_mask((rows, 128), place)
        return dot(pair1[:, lanes], own, 1, 1), dot(pair2[:, lanes], own, 1, 1)

    def rest(head, scores):
        lanes, place, turned = head_lanes(head)
        scores1, scores2 = scores
        top = jnp.maximum(
            jnp.max(scores1, axis=0, keepdims=True), jnp.max(scores2, axis=0, keepdims=True)
        )
        exps1 = jnp.exp2(scores1 - top)
        exps2 = jnp.exp2(scores2 - top)
        total = column_sum(exps1) + column_sum(exps2)
        lanes = value_lanes(lanes)
        mixed = dot(pair1[:, lanes].T[turned], exps1.astype(jnp.bfloat16)) + dot(
            pair2[:, lanes].T[turned], exps2.astype(jnp.bfloat16)
        )
        log_total[0, head : head + 1, :] = top + jnp.log2(total)
        return mixed * (1.0 / total)

    parts = in_turn(HEADS, first, rest)
    return jnp.concatenate(
        [
            jnp.concatenate(parts[head : head + 2], axis=0).T.astype(jnp.bfloat16)
            for head in range(0, HEADS, 2)
        ],
        axis=1,
    )


def attend_back_body(second, query, pair, grad, attended, log_total, *refs):
    if second:
        before, cosine, sine = refs[:3]
    d_query, d_keys, d_values = refs[-3:]
    rows = query.shape[0]
    products = {}

    def first(head):
        lanes, place, _ = head_lanes(head)
        if place == 0:
            product = grad[:, lanes].astype(jnp.float32) * attended[:, lanes].astype(jnp.float32)
            products[head] = products[head + 1] = product.T
        own = query[:, lanes] * head_mask((rows, 128), place)
        own_grad = grad[:, lanes] * head_mask((rows, 128), place)
        scores = dot(pair[:, lanes], own, 1, 1)
        d_probs = dot(pair[:, value_lanes(lanes)], own_grad, 1, 1)
        return own, own_grad, scores, d_probs

    def rest(head, given):
        own, own_grad, scores, d_probs = given
        lanes, place, turned = head_lanes(head)
        delta = column_sum(products[head][turned])
        probs = jnp.exp2(scores - log_total[0, head : head + 1, :])
        d_scores = (probs * (d_probs - delta)).astype(jnp.bfloat16)
        return (
            dot(pair[:, lanes].T[turned], d_scores),
            dot(d_scores, own),
            dot(probs.astype(jnp.bfloat16), own_grad),
        )

    parts = in_turn(HEADS, first, rest)
    for head in range(0, HEADS, 2):
        lanes = head_lanes(head)[0]
        one, two = parts[head : head + 2]
        turned = jnp.concatenate([one[0], two[0]], axis=0).T * HD ** (-0.5)
        if second:
            turned = rotate_lanes(turned + before[:, lanes], cosine[...], -sine[...])
        d_query[:, lanes] = turned.astype(d_query.dtype)
        d_keys[:, lanes] = ((one[1] + two[1]) * (1.0 / LOG2E)).astype(jnp.bfloat16)
        d_values[:, lanes] = (one[2] + two[2]).astype(jnp.bfloat16)


def attend_back(query, pair, grad, attended, log_total, before=None, after=(), free=()):
    rows, width = query.shape
    lanes = HEADS * HD
    steps = width // lanes
    block = columns(rows, lanes)
    second = before is not None
    extra = list(before) if second else []
    extra_specs = [block, full((rows, 128)), full((rows, 128))] if second else []
    return kernel_call(
        functools.partial(attend_back_body, second),
        steps,
        [
            block,
            columns(rows, 2 * lanes),
            block,
            block,
            pl.BlockSpec((1, HEADS, rows), lambda step: (step, 0, 0)),
        ]
        + extra_specs
        + [pl.BlockSpec(memory_space=pl.ANY)] * len(after),
        [block, block, block],
        [
            far((rows, width), jnp.bfloat16 if second else jnp.float32),
            far((rows, width), jnp.bfloat16),
            far((rows, width), jnp.bfloat16),
        ],
        [],
        28,
    )(query, pair, grad, attended, log_total, *extra, *after, free=free)


def block_body(
    own_down, attend_steps, hidden_steps,
    core, normed1, query_weight, cosine, sine, mods, up_bias, down_bias, *refs,
):
    pairs_far, refs = refs[: 2 * attend_steps], refs[2 * attend_steps :]
    (
        tokens_far, cotangent_far, out_far, up_far, down_far,
        query, attended, log_total, mixed, d_middle, d_attended, up_grad,
        down_keep, down_send, bias_grad, sums, peer_far,
        tokens, cotangent, out_weight, up_weight, down_weight, arrived,
        own_pairs, peer_pairs, pair_arrived, left,
        all_attended, normed, d_ffn, branch, middle, forward, back,
    ) = refs
    step = pl.program_id(0)
    tile = up_bias.shape[1]
    lanes = 2 * HEADS * HD
    own_arrivals, peer_arrivals, departures = [], [], []
    for index in range(attend_steps):
        own_arrivals.append(
            pltpu.make_async_copy(
                pairs_far[index], own_pairs.at[index], pair_arrived.at[0, index]
            )
        )
        peer_arrivals.append(
            pltpu.make_async_copy(
                pairs_far[attend_steps + index], peer_pairs.at[index], pair_arrived.at[1, index]
            )
        )
        departures.append(
            pltpu.make_async_copy(
                peer_pairs.at[index],
                peer_far.at[:, pl.ds(index * lanes, lanes)],
                left.at[index],
            )
        )
    arrivals = [
        pltpu.make_async_copy(source, target, arrived.at[index])
        for index, (source, target) in enumerate(
            (
                (tokens_far, tokens),
                (cotangent_far, cotangent),
                (out_far, out_weight),
                (up_far, up_weight),
                (down_far, down_weight),
            )
        )
    ]

    @pl.when(step == 0)
    def _():
        for index in range(attend_steps):
            own_arrivals[index].start()
            peer_arrivals[index].start()
        for arrival in arrivals:
            arrival.start()

    for index in range(attend_steps):

        @pl.when(step == index)
        def _(index=index):
            own_arrivals[index].wait()
            peer_arrivals[index].wait()
            departures[index].start()

    @pl.when(step < attend_steps)
    def _():
        value = rotate_lanes(dot(normed1[...], query_weight[...]), cosine[...], sine[...])
        query[...] = (value * (LOG2E * HD ** (-0.5))).astype(jnp.bfloat16)
        found = attend_heads(query, own_pairs.at[step], peer_pairs.at[step], log_total)
        attended[...] = found
        for index in range(attend_steps):

            @pl.when(step == index)
            def _(index=index):
                heads = HEADS * HD
                all_attended[:, index * heads : (index + 1) * heads] = found

    @pl.when(step == attend_steps)
    def _():
        for arrival in arrivals:
            arrival.wait()
        for departure in departures:
            departure.wait()
        turned = dot(all_attended[...], out_weight[...])
        branch[...] = turned.astype(jnp.bfloat16)
        value = tokens[...].astype(jnp.float32) + row(mods, GATE1) * turned
        middle[...] = value
        hat, _ = normalized(value)
        value = hat * row(mods, GAIN2) * (1.0 + row(mods, SCALE2)) + row(mods, SHIFT2)
        normed[...] = value.astype(jnp.bfloat16)
        low = (row(mods, GATE2) * cotangent[...].astype(jnp.float32)).astype(jnp.bfloat16)
        d_ffn[...] = low
        sums[4:5, :] = column_sum(low.astype(jnp.float32))
        forward[...] = jnp.zeros_like(forward)
        back[...] = jnp.zeros_like(back)

    @pl.when((step >= attend_steps) & (step < attend_steps + hidden_steps))
    def _():
        place = pl.ds(pl.multiple_of((step - attend_steps) * tile, tile), tile)
        pre = dot(normed[...], up_weight[:, place]) + up_bias[...]
        d_activated = dot(d_ffn[...], down_weight[place, :], 1, 1)
        root = 0.7978845608028654
        square = pre * pre
        bent = jnp.tanh(root * pre * (1.0 + 0.044715 * square))
        half = 0.5 + 0.5 * bent
        slope = half + (0.5 * root) * pre * (1.0 - bent * bent) * (1.0 + 0.134145 * square)
        low = (pre * half).astype(jnp.bfloat16)
        d_pre = d_activated * slope
        d_low = d_pre.astype(jnp.bfloat16)
        bias_grad[...] = column_sum(d_pre)
        down_grad = dot(low, d_ffn[...], 0, 0).astype(jnp.bfloat16)
        store_split(down_grad, core, own_down, down_keep, down_send)
        up_grad[...] = dot(normed[...], d_low, 0, 0).astype(jnp.bfloat16)
        forward[...] += dot(low, down_weight[place, :])
        back[...] += dot(d_low, up_weight[:, place], 1, 1)

    @pl.when(step == attend_steps + hidden_steps)
    def _():
        grad = cotangent[...].astype(jnp.float32)
        held = middle[...]
        hat, inverse = normalized(held)
        factor = row(mods, GAIN2) * (1.0 + row(mods, SCALE2))
        value = back[...]
        d_value = grad + norm_back(value, hat, inverse, factor)
        d_middle[...] = d_value
        d_branch = (row(mods, GATE1) * d_value).astype(jnp.bfloat16)
        d_attended[...] = dot(d_branch, out_weight[...], 1, 1).astype(jnp.bfloat16)
        up_grad[...] = dot(all_attended[...], d_branch, 0, 0).astype(jnp.bfloat16)
        ffn = forward[...] + down_bias[...]
        mixed[...] = (held + row(mods, GATE2) * ffn).astype(jnp.bfloat16)
        sums[0:1, :] = column_sum(value)
        sums[1:2, :] = column_sum(value * hat)
        sums[2:3, :] = column_sum(d_value * branch[...].astype(jnp.float32))
        sums[3:4, :] = column_sum(grad * ffn)
        sums[5:8, :] = jnp.zeros_like(sums[5:8, :])


def split_rows(rows):
    own = rows // lax.axis_size("dp")
    return own if own % 16 == 0 else rows // 2


def block_layer(
    core, normed1, qkv_weight, cosine, sine, mods, up_bias, down_bias, own, peer,
    tokens, cotangent, out_weight, up_weight, down_weight,
):
    rows, width = tokens.shape
    hidden = up_weight.shape[1]
    tile = width
    lanes = HEADS * HD
    attend_steps = width // lanes
    hidden_steps = hidden // tile
    own_down = hidden // lax.axis_size("dp")
    if own_down % 16 > 0:
        own_down = tile // 2

    def heads(first=0):
        return pl.BlockSpec(
            (rows, lanes), lambda step: (0, jnp.minimum(step, attend_steps - 1) + first)
        )

    def tiles(step):
        return jnp.clip(step - attend_steps, 0, hidden_steps - 1)

    def up_tiles(step):
        return jnp.clip(step - attend_steps, 0, hidden_steps)

    block = full((rows, width))
    far_spec = pl.BlockSpec(memory_space=pl.ANY)
    low = jnp.bfloat16
    up_spec = pl.BlockSpec((width, tile), lambda step: (0, up_tiles(step)))
    down_spec = pl.BlockSpec((tile // 2, width), lambda step: (tiles(step), 0))
    return kernel_call(
        functools.partial(block_body, own_down, attend_steps, hidden_steps),
        attend_steps + hidden_steps + 1,
        [
            scalar_spec(),
            block,
            pl.BlockSpec((width, lanes), lambda step: (0, jnp.minimum(step, attend_steps - 1))),
            full((rows, 128)),
            full((rows, 128)),
            full((16, width)),
            pl.BlockSpec((1, tile), lambda step: (0, tiles(step))),
            full((1, width)),
        ]
        + [far_spec] * (2 * attend_steps + 5),
        [
            heads(),
            heads(),
            pl.BlockSpec(
                (1, HEADS, rows), lambda step: (jnp.minimum(step, attend_steps - 1), 0, 0)
            ),
            block,
            block,
            block,
            up_spec,
            down_spec,
            down_spec,
            pl.BlockSpec((1, tile), lambda step: (0, tiles(step))),
            full((8, width)),
            far_spec,
        ],
        [
            far((rows, width), low),
            far((rows, width), low),
            far((attend_steps, HEADS, rows), jnp.float32),
            far((rows, width), low),
            far((rows, width), jnp.float32),
            far((rows, width), low),
            far((width, hidden + width), low),
            far((hidden // 2, width), low),
            far((hidden // 2, width), low),
            far((1, hidden), jnp.float32),
            far((8, width), jnp.float32),
            far((rows, 2 * width), low),
        ],
        [
            pltpu.VMEM((rows, width), low),
            pltpu.VMEM((rows, width), low),
            pltpu.VMEM((width, width), low),
            pltpu.VMEM((width, hidden), low),
            pltpu.VMEM((hidden, width), low),
            pltpu.SemaphoreType.DMA((5,)),
            pltpu.VMEM((attend_steps, rows, 2 * lanes), low),
            pltpu.VMEM((attend_steps, rows, 2 * lanes), low),
            pltpu.SemaphoreType.DMA((2, attend_steps)),
            pltpu.SemaphoreType.DMA((attend_steps,)),
            pltpu.VMEM((rows, width), low),
            pltpu.VMEM((rows, width), low),
            pltpu.VMEM((rows, width), low),
            pltpu.VMEM((rows, width), low),
            pltpu.VMEM((rows, width), jnp.float32),
            pltpu.VMEM((rows, width), jnp.float32),
            pltpu.VMEM((rows, width), jnp.float32),
        ],
        58,
    )(
        core, normed1, qkv_weight, cosine, sine, mods, up_bias, down_bias, *own, *peer,
        tokens, cotangent, out_weight, up_weight, down_weight,
        free=(*peer, cotangent, tokens),
    )


def tokens_back_body(
    own, core, d_query, d_keys, d_values, peer_keys, peer_values, normed, cosine, sine,
    weight1, weight2, weight3, tokens, d_middle, mods, sums, bias_grad, *refs,
):
    parts, (out, small, total) = refs[:6], refs[6:]
    step = pl.program_id(0)
    width = tokens.shape[1]
    lanes = HEADS * HD
    keys = d_keys[...].astype(jnp.float32) + peer_keys[...].astype(jnp.float32)
    keys = rotate_lanes(keys, cosine[...], -sine[...]).astype(jnp.bfloat16)
    values = d_values[...].astype(jnp.float32) + peer_values[...].astype(jnp.float32)
    values = values.astype(jnp.bfloat16)
    low = jnp.concatenate([d_query[...], keys, values], axis=1)
    grad = dot(normed[...], low, 0, 0).astype(jnp.bfloat16)
    for index in range(3):
        third = grad[:, index * lanes : (index + 1) * lanes]
        store_split(third, core, own, parts[2 * index], parts[2 * index + 1])
    part = (
        dot(d_query[...], weight1[...], 1, 1)
        + dot(keys, weight2[...], 1, 1)
        + dot(values, weight3[...], 1, 1)
    )

    @pl.when(step == 0)
    def _():
        total[...] = part

    @pl.when(step > 0)
    def _():
        total[...] += part

    @pl.when(step == pl.num_programs(0) - 1)
    def _():
        back = total[...]
        hat, inverse = normalized(tokens[...].astype(jnp.float32))
        scale1 = 1.0 + row(mods, SCALE1)
        gain1 = row(mods, GAIN1)
        out[...] = (d_middle[...] + norm_back(back, hat, inverse, gain1 * scale1)).astype(
            jnp.bfloat16
        )
        hat_sum1 = column_sum(back * hat)
        hat_sum2 = row(sums, 1)
        rows = [
            column_sum(back),
            hat_sum1 * gain1,
            row(sums, 2),
            row(sums, 0),
            hat_sum2 * row(mods, GAIN2),
            row(sums, 3),
            row(mods, COND) * 0.5,
            jnp.zeros_like(hat_sum1),
            hat_sum1 * scale1,
            hat_sum2 * (1.0 + row(mods, SCALE2)),
            row(sums, 4),
        ]
        for index in range(bias_grad.shape[1] // width):
            rows.append(bias_grad[:, index * width : (index + 1) * width])
        for index, value in enumerate(rows):
            small[index : index + 1, :] = value
        small[len(rows) :, :] = jnp.zeros_like(small[len(rows) :, :])


def tokens_back(
    core, d_query, d_keys, d_values, peer_keys, peer_values, normed, cosine, sine, weight,
    tokens, d_middle, mods, sums, bias_grad,
):
    rows, width = normed.shape
    lanes = HEADS * HD
    steps = width // lanes
    block = full((rows, width))
    return kernel_call(
        functools.partial(tokens_back_body, split_rows(width)),
        steps,
        [
            scalar_spec(),
            columns(rows, lanes),
            columns(rows, lanes),
            columns(rows, lanes),
            columns(rows, lanes),
            columns(rows, lanes),
            block,
            full((rows, 128)),
            full((rows, 128)),
            columns(width, lanes),
            columns(width, lanes, steps),
            columns(width, lanes, 2 * steps),
            block,
            block,
            full((16, width)),
            full((8, width)),
            full(bias_grad.shape),
        ],
        [columns(width // 2, lanes)] * 6 + [block, full((16, width))],
        [far((width // 2, width), jnp.bfloat16)] * 6
        + [
            far((rows, width), jnp.bfloat16),
            far((16, width), jnp.float32),
        ],
        [pltpu.VMEM((rows, width), jnp.float32)],
        40,
    )(
        core, d_query, d_keys, d_values, peer_keys, peer_values, normed, cosine, sine,
        weight, weight, weight, tokens, d_middle, mods, sums, bias_grad,
        free=(peer_keys, peer_values),
    )


def swap_halves(block):
    count = lax.axis_size("dp") * lax.axis_size("seq")
    target = {1: 2, 2: 1}
    perm = [(i, i - i % 4 + target.get(i % 4, i % 4)) for i in range(count)]
    return lax.ppermute(block, ("dp", "seq"), perm)


def swap_bit(block, bit):
    return lax.ppermute(block, "dp", [(i, i ^ bit) for i in range(lax.axis_size("dp"))])


def swap_cores(block):
    return swap_bit(block, 1)


def swap_seq(block):
    return lax.ppermute(block, "seq", [(0, 1), (1, 0)])


def dp_bits():
    bits, bit = [], 1
    while bit < lax.axis_size("dp"):
        bits.append(bit)
        bit *= 2
    return bits


def pick(block, axis, index):
    return lax.dynamic_index_in_dim(block, index, axis, keepdims=False)


class Flow:
    def __init__(self, got, kept, lanes=None):
        self.got, self.kept = got, kept
        self.lanes = lanes or (0, kept.shape[2])
        self.count, self.rest = kept.shape[:2]
        self.width = self.lanes[1] - self.lanes[0]


def stage_body(jobs, counts, mine, *refs):
    inputs = refs[: counts[0]]
    outputs = refs[counts[0] + counts[1] :]

    def terms(sources, place):
        for one, two, lanes, rows in sources:
            total = inputs[one][place + (slice(None), lanes)].astype(jnp.float32)
            total = total + inputs[two][place + (slice(None), lanes)].astype(jnp.float32)
            total = total.astype(jnp.bfloat16)
            height = total.shape[-2]
            for start in range(0, height, rows):
                yield total if height == rows else total[..., start : start + rows, :]

    def store(out, place, values):
        at = 0
        for value in values:
            width = value.shape[-1]
            out[place + (slice(None), slice(at, at + width))] = value
            at += width

    def run(index, kind, stride, sources, target):
        if kind == "sum":
            store(outputs[target], (slice(None),), terms(sources, (slice(None),)))
            return

        def part(out, which):
            if kind == "half":
                halves = []
                for one, two, lanes, rows in sources:
                    middle = (lanes.start + lanes.stop) // 2
                    first, second = slice(lanes.start, middle), slice(middle, lanes.stop)
                    halves.append((one, two, second if which else first, rows))
                store(out, (slice(None),), terms(halves, (slice(None),)))
                return
            for block in range(out.shape[0]):
                high, low = divmod(block, stride)
                place = (2 * high + which) * stride + low
                store(out, (block,), terms(sources, (place,)))

        for which in range(2):

            @pl.when(mine[index] == which)
            def _(which=which):
                part(outputs[target + 1], which)
                part(outputs[target], 1 - which)

    for index, (kind, stride, sources, target, whole) in enumerate(jobs):
        if whole:

            @pl.when(pl.program_id(0) == 0)
            def _(args=(index, kind, stride, sources, target)):
                run(*args)

        else:
            run(index, kind, stride, sources, target)


def small_body(first, one, two, out):
    rows = one.shape[0] - 8

    @pl.when(pl.program_id(0) == 0)
    def _():
        if first:
            out[...] = one[...] + two[...]
        else:
            out[:rows, :] = one[:rows, :]
            out[rows : 2 * rows, :] = two[:rows, :]
            out[2 * rows :, :] = one[rows:, :] + two[rows:, :]


def stage(steps, jobs, after=(), small=None, free=()):
    seq_rank, dp_rank = lax.axis_index("seq"), lax.axis_index("dp")
    inputs, in_specs, specs, out_specs, out_shape, mine = [], [], [], [], [], []
    free = [*free] + [flow.got for flows, _ in jobs for flow in flows]

    def spec(shape, whole):
        if whole:
            return full(shape)
        return pl.BlockSpec((shape[0] // steps,) + shape[1:], lambda at: (at, 0, 0))

    def place_of(array, whole):
        for index, other in enumerate(inputs):
            if other is array:
                return index
        inputs.append(array)
        in_specs.append(spec(array.shape, whole))
        return len(inputs) - 1

    for flows, step in jobs:
        bit, stride = step if isinstance(step, tuple) else (None, 1)
        rest, count = flows[0].rest, flows[0].count
        smallest = 1 if bit is None else 2 * stride
        whole = count % steps > 0 or (count // steps) % smallest > 0
        sources = [
            (place_of(flow.got, whole), place_of(flow.kept, whole), slice(*flow.lanes), rest)
            for flow in flows
        ]
        width = sum(flow.width * flow.rest // rest for flow in flows)
        if bit is not None:
            shape = (count // 2, rest, width)
            mine.append((dp_rank // bit) % 2)
        else:
            shape = (count, rest, width // 2 if step == "half" else width)
            mine.append(seq_rank)
        specs.append((step if bit is None else "bit", stride, sources, len(out_shape), whole))
        results = 1 if step == "sum" else 2
        out_shape += [far(shape, jnp.bfloat16)] * results
        out_specs += [spec(shape, whole)] * results
    counts = (len(inputs), len(after))
    extra = []
    if small is not None:
        got, kept, first = small
        extra = [kept, got]
        rows = kept.shape[0] if first else 2 * kept.shape[0] - 8
        out_shape.append(far((rows, kept.shape[1]), jnp.float32))
        out_specs.append(full((rows, kept.shape[1])))

    def body(mine, *refs):
        if small is None:
            stage_body(specs, counts, mine, *refs)
            return
        main, ends = refs[: sum(counts)], refs[sum(counts) :]
        small_body(first, ends[0], ends[1], ends[-1])
        stage_body(specs, counts, mine, *main, *ends[2:-1])

    results = kernel_call(
        body,
        steps,
        [scalar_spec()]
        + in_specs
        + [pl.BlockSpec(memory_space=pl.ANY)] * len(after)
        + [full(array.shape) for array in extra],
        out_specs,
        out_shape,
        [],
        40,
    )(jnp.stack(mine), *inputs, *after, *extra, free=(*free, *extra[1:]))
    new = []
    for (flows, step), (_, _, _, target, _) in zip(jobs, specs):
        sent = results[target]
        got = swap_seq(sent) if isinstance(step, str) else swap_bit(sent, step[0])
        new.append(Flow(got, sent if step == "sum" else results[target + 1]))
    if small is not None:
        new.append(results[-1])
    return new, results[0]


def from_tiles(kept, sent, tile):
    rows, width = 2 * kept.shape[0], kept.shape[1]
    core = lax.axis_index("dp") % 2
    first = jnp.where(core == 0, kept, sent).reshape(rows // tile, 1, tile // 2, width)
    second = jnp.where(core == 0, sent, kept).reshape(rows // tile, 1, tile // 2, width)
    return jnp.concatenate([first, second], axis=1).reshape(rows, width)


def plain_sum(kept, sent, tile):
    matrix = from_tiles(kept, sent, tile)
    return lax.psum(
        lax.psum_scatter(matrix, "dp", scatter_dimension=0, tiled=True).astype(jnp.float32), "seq"
    )


def joined(flow, widths):
    block, got = flow.kept[0].astype(jnp.float32), flow.got[0].astype(jnp.float32)
    here = lax.axis_index("seq") == 0
    first, second = jnp.where(here, block, got), jnp.where(here, got, block)
    parts, at = [], 0
    for width in widths:
        parts.append(
            jnp.concatenate([first[:, at : at + width], second[:, at : at + width]], axis=1)
        )
        at += width
    return parts


def per_device(
    tokens,
    cotangent,
    time_index,
    step_table,
    first_gain,
    attn_qkv,
    attn_out,
    second_gain,
    mlp_up,
    up_bias,
    mlp_down,
    down_bias,
    ada_weight,
    ada_bias,
):
    rows, width = tokens.shape[1:]
    dp_rank = lax.axis_index("dp")
    core = dp_rank % 2
    own_cond, silu_back = jax.vjp(
        jax.nn.silu, lax.dynamic_slice_in_dim(step_table, time_index[0], 1, axis=0)
    )
    positions = core * rows + jnp.arange(rows, dtype=jnp.int32)
    cosine, sine = tables(positions)
    tokens = swap_halves(tokens[0])
    time_index = swap_halves(time_index)
    cotangent = swap_halves(cotangent[0])
    cond = jax.nn.silu(lax.dynamic_slice_in_dim(step_table, time_index[0], 1, axis=0))
    ada_float = ada_weight.astype(jnp.float32)
    modulation = jnp.dot(cond, ada_float, precision=highest) + ada_bias.astype(jnp.float32)
    gain1 = first_gain.astype(jnp.float32)
    gain2 = second_gain.astype(jnp.float32)
    cond_row = jnp.pad(cond, ((0, 0), (0, width - cond.shape[1])))
    mods = jnp.concatenate(
        [modulation.reshape(6, width), gain1[None], gain2[None], cond_row, jnp.zeros((7, width))]
    )
    normed1, own_pair, *own_parts = project_key_value(tokens, mods, attn_qkv, cosine, sine)
    peer_parts = [swap_cores(part) for part in own_parts]
    core_ref = core[None]
    (
        query, attended, log_total, mixed, d_middle, d_attended, up_grad,
        down_keep, down_send, up_bias_grad, sums2, peer_pair,
    ) = block_layer(
        core_ref, normed1, attn_qkv, cosine, sine, mods,
        up_bias.astype(jnp.float32)[None], down_bias.astype(jnp.float32)[None],
        own_parts, peer_parts,
        tokens, cotangent, attn_out, mlp_up, mlp_down,
    )
    hidden = mlp_up.shape[1]
    dp_size = lax.axis_size("dp")
    bits = dp_bits()
    by_steps = split_rows(width) == width // dp_size and len(bits) == 4
    mixed = swap_halves(mixed)
    up_rows = lax.psum_scatter(up_grad, "dp", scatter_dimension=0, tiled=True)
    up_got = swap_seq(up_rows)

    def blocks(part):
        return part.reshape(dp_size // 2, -1, part.shape[1])

    if by_steps:
        down = Flow(swap_cores(blocks(down_send)), blocks(down_keep))
    d_query, away_keys, away_values = attend_back(query, peer_pair, d_attended, attended, log_total)
    after = ()
    if by_steps:
        (down,), sent = stage(4, [([down], "half")], (away_keys, mixed), free=(mixed,))
        after = (sent,)
    peer_keys, peer_values = swap_cores(away_keys), swap_cores(away_values)
    d_query, d_keys, d_values = attend_back(
        query, own_pair, d_attended, attended, log_total, (d_query, cosine, sine), after
    )
    *qkv_parts, tokens_grad, small = tokens_back(
        core_ref, d_query, d_keys, d_values, peer_keys, peer_values, normed1, cosine, sine, attn_qkv, tokens,
        d_middle, mods, sums2, up_bias_grad,
    )
    got = swap_cores(small)
    def doubled(small, got):
        return jnp.concatenate([small[:-8], got[:-8], small[-8:] + got[-8:]], axis=0)

    if by_steps:
        late = [
            Flow(swap_cores(blocks(send)), blocks(keep))
            for keep, send in zip(qkv_parts[::2], qkv_parts[1::2])
        ]
        moves = [functools.partial(swap_bit, bit=bit) for bit in bits[2:] + bits[1:2]]
        moves.append(swap_seq)
        (down, late, small), sent = stage(
            4, [([down], (bits[1], 1)), (late, "half")], (), (got, small, True)
        )

        small = doubled(small, moves.pop(0)(small))

        def next_stage(jobs, count, after=()):
            nonlocal small, sent
            extra = (moves.pop(0)(small), small, False) if len(moves) > 0 else None
            flows, sent = stage(count, jobs, (sent, *after), extra, after)
            if extra is not None:
                small = flows.pop()
            return flows

        down, late = next_stage([([down], (bits[2], 1)), ([late], (bits[1], 1))], 2)
        down, late = next_stage([([down], (bits[3], 1)), ([late], (bits[2], 1))], 2)
        down, late = next_stage([([down], "sum"), ([late], (bits[3], 1))], 1, (up_got,))
        (late,) = next_stage([([late], "sum")], 1)
        while len(moves) > 0:
            small = doubled(small, moves.pop(0)(small))
        (down_rows,) = joined(down, (width // 2,))
        qkv_rows = jnp.concatenate(joined(late, (width // 2,) * 3), axis=1)
    else:
        small = small + got
        moves = [functools.partial(swap_bit, bit=bit) for bit in bits[1:]] + [swap_seq]
        for move in moves:
            small = doubled(small, move(small))
        down_rows = plain_sum(down_keep, down_send, width)
        qkv_rows = jnp.concatenate(
            [
                plain_sum(keep, send, width)
                for keep, send in zip(qkv_parts[::2], qkv_parts[1::2])
            ],
            axis=1,
        )
    up_rows = up_rows.astype(jnp.float32) + up_got.astype(jnp.float32)
    per_sequence, sums = small[:-8].reshape(-1, 8, width), small[-8:]
    d_mod_all = per_sequence[:, :6].reshape(per_sequence.shape[0], 6 * width)
    cond_all = per_sequence[:, 6, : cond.shape[1]]
    ada_bias_grad = jnp.sum(d_mod_all, axis=0)
    own_columns = d_mod_all.shape[1] // lax.axis_size("dp")
    mine = lax.dynamic_slice_in_dim(d_mod_all, dp_rank * own_columns, own_columns, axis=1)
    ada_weight_grad = lax.dot_general(
        cond_all, mine, (((0,), (0,)), ((), ())), precision=highest
    )
    other = d_mod_all.shape[0] // 2
    d_mod_own = jnp.where(
        lax.axis_index("seq") == core, d_mod_all[:1], d_mod_all[other : other + 1]
    )
    (cond_grad,) = silu_back(jnp.dot(d_mod_own, ada_float.T, precision=highest))
    return (
        mixed[None],
        swap_halves(tokens_grad).astype(jnp.float32)[None],
        cond_grad,
        sums[0],
        qkv_rows,
        up_rows[:, hidden:],
        sums[1],
        up_rows[:, :hidden],
        sums[3:7].reshape(-1),
        down_rows,
        sums[2],
        ada_weight_grad,
        ada_bias_grad,
    )


def solution(mesh):
    placed = (
        P("dp", "seq", None),
        P("dp", "seq", None),
        P("dp"),
        P(),
        P(),
        P(),
        P(),
        P(),
        P(),
        P(),
        P(),
        P(),
        P(),
        P(),
    )
    return jax.shard_map(
        per_device,
        mesh=mesh,
        in_specs=placed,
        out_specs=(
            P("dp", "seq", None),
            P("dp", "seq", None),
            P("dp", None),
            P(),
            P("dp", None),
            P("dp", None),
            P(),
            P("dp", None),
            P(),
            P("dp", None),
            P(),
            P(None, "dp"),
            P(),
        ),
        check_vma=False,
    )
```

```python
import functools

import jax
import jax.numpy as jnp
from jax import lax
from jax.experimental import pallas as pl
from jax.experimental.pallas import tpu as pltpu
from jax.sharding import PartitionSpec as P

HD = 64
LOG2E = 1.4426950408889634


highest = lax.Precision.HIGHEST


def tables(positions):
    half_dim = HD // 2
    frequency = jnp.exp(
        -jnp.log(10000.0) * (2.0 * jnp.arange(half_dim, dtype=jnp.float32) / HD)
    )
    angles = positions.astype(jnp.float32)[:, None] * frequency[None, :]
    cosine, sine = jnp.cos(angles), jnp.sin(angles)
    return (
        jnp.concatenate([cosine] * 4, axis=1),
        jnp.concatenate([-sine, sine, -sine, sine], axis=1),
    )


def full(shape):
    return pl.BlockSpec(shape, lambda step: (0,) * len(shape))


def columns(rows, width, first=0):
    return pl.BlockSpec((rows, width), lambda step: (0, step + first))


def shaped(shape, kind):
    return jax.ShapeDtypeStruct(shape, kind)


def far(shape, kind):
    return pltpu.VMEM(shape, kind)


def far(shape, kind):
    return pltpu.HBM(shape, kind)


def store_split(low, core, own, keep, send):
    pairs = low.shape[0] // (2 * own)

    def store(kept):
        for pair in range(pairs):
            rows = slice(pair * own, (pair + 1) * own)
            for parity, target in ((kept, keep), (1 - kept, send)):
                start = (2 * pair + parity) * own
                target[rows, :] = low[start : start + own, :]

    @pl.when(core[0] == 0)
    def _():
        store(0)

    @pl.when(core[0] == 1)
    def _():
        store(1)


def zero_shape():
    return jax.ShapeDtypeStruct((1, 1), jnp.float32)


def scalar_spec():
    return pl.BlockSpec(memory_space=pltpu.SMEM)


def kernel_call(body, steps, in_specs, out_specs, out_shape, scratch, grant):
    call = pl.pallas_call(
        body,
        grid=(steps,),
        in_specs=in_specs,
        out_specs=out_specs,
        out_shape=out_shape,
        scratch_shapes=scratch,
        compiler_params=pltpu.CompilerParams(
            dimension_semantics=("arbitrary",), vmem_limit_bytes=grant * 1024 * 1024
        ),
        cost_estimate=pl.CostEstimate(flops=1, bytes_accessed=1, transcendentals=0),
    )

    def run(*args, free=()):
        placed = []
        for arg in args:
            if arg.size > 4096 and not any(arg is other for other in free):
                arg = pltpu.with_memory_space_constraint(arg, pltpu.HBM)
            placed.append(arg)
        return call(*placed)

    return run


def dot(left, right, left_axis=1, right_axis=0):
    return lax.dot_general(
        left,
        right,
        (((left_axis,), (right_axis,)), ((), ())),
        preferred_element_type=jnp.float32,
    )


def normalized(inputs):
    center = inputs - jnp.mean(inputs, axis=-1, keepdims=True)
    inverse = lax.rsqrt(jnp.mean(center * center, axis=-1, keepdims=True) + 1e-05)
    return center * inverse, inverse


def norm_back(back, hat, inverse, factor):
    scaled = back * factor
    return inverse * (
        scaled
        - jnp.mean(scaled, axis=-1, keepdims=True)
        - hat * jnp.mean(scaled * hat, axis=-1, keepdims=True)
    )


def column_sum(values):
    return jnp.sum(values, axis=0, keepdims=True)


SHIFT1, SCALE1, GATE1, SHIFT2, SCALE2, GATE2, GAIN1, GAIN2, COND = range(9)


def row(ref, index):
    return ref[index : index + 1, :]


def rotate_lanes(values, cosine, sine):
    lane = lax.broadcasted_iota(jnp.int32, cosine.shape, 1)
    lower = (lane % HD) < HD // 2
    parts = []
    for start in range(0, values.shape[1], 128):
        part = values[:, start : start + 128]
        other = jnp.where(lower, pltpu.roll(part, 128 - HD // 2, 1), pltpu.roll(part, HD // 2, 1))
        parts.append(part * cosine + other * sine)
    return jnp.concatenate(parts, axis=1)


HEADS = 4


def key_value_body(
    tokens, mods, key_weight, value_weight, cosine, sine, normed, every, *parts
):
    step = pl.program_id(0)

    @pl.when(step == 0)
    def _():
        hat, _ = normalized(tokens[...].astype(jnp.float32))
        value = hat * row(mods, GAIN1) * (1.0 + row(mods, SCALE1)) + row(mods, SHIFT1)
        normed[...] = value.astype(jnp.bfloat16)

    keys = rotate_lanes(dot(normed[...], key_weight[...]), cosine[...], sine[...])
    values = dot(normed[...], value_weight[...])
    both = jnp.concatenate([keys, values], axis=1).astype(jnp.bfloat16)
    every[...] = both
    for index, part in enumerate(parts):

        @pl.when(step == index)
        def _(part=part):
            part[...] = both


def project_key_value(tokens, mods, weight, cosine, sine):
    rows, width = tokens.shape
    lanes = HEADS * HD
    steps = width // lanes
    low = jnp.bfloat16
    return kernel_call(
        key_value_body,
        steps,
        [
            full((rows, width)),
            full((16, width)),
            columns(width, lanes, steps),
            columns(width, lanes, 2 * steps),
            full((rows, 128)),
            full((rows, 128)),
        ],
        [full((rows, width)), columns(rows, 2 * lanes)] + [full((rows, 2 * lanes))] * steps,
        [far((rows, width), low), far((rows, 2 * width), low)]
        + [far((rows, 2 * lanes), low)] * steps,
        [],
        24,
    )(tokens, mods, weight, weight, cosine, sine, free=(tokens,))


def head_mask(shape, head):
    lane = lax.broadcasted_iota(jnp.int32, shape, 1)
    return jnp.where(lane // HD == head, 1.0, 0.0).astype(jnp.bfloat16)


def head_lanes(head):
    pair, place = divmod(head, 2)
    return slice(pair * 128, (pair + 1) * 128), place, slice(place * HD, (place + 1) * HD)


def value_lanes(lanes):
    return slice(HEADS * HD + lanes.start, HEADS * HD + lanes.stop)


def in_turn(count, first, rest):
    results = []
    ahead = first(0)
    for index in range(count):
        now = ahead
        if index + 1 < count:
            ahead = first(index + 1)
        results.append(rest(index, now))
    return results


def attend_heads(query, pair1, pair2, log_total):
    rows = query.shape[0]

    def first(head):
        lanes, place, _ = head_lanes(head)
        own = query[:, lanes] * head_mask((rows, 128), place)
        return dot(pair1[:, lanes], own, 1, 1), dot(pair2[:, lanes], own, 1, 1)

    def rest(head, scores):
        lanes, place, turned = head_lanes(head)
        scores1, scores2 = scores
        top = jnp.maximum(
            jnp.max(scores1, axis=0, keepdims=True), jnp.max(scores2, axis=0, keepdims=True)
        )
        exps1 = jnp.exp2(scores1 - top)
        exps2 = jnp.exp2(scores2 - top)
        total = column_sum(exps1) + column_sum(exps2)
        lanes = value_lanes(lanes)
        mixed = dot(pair1[:, lanes].T[turned], exps1.astype(jnp.bfloat16)) + dot(
            pair2[:, lanes].T[turned], exps2.astype(jnp.bfloat16)
        )
        log_total[0, head : head + 1, :] = top + jnp.log2(total)
        return mixed * (1.0 / total)

    parts = in_turn(HEADS, first, rest)
    return jnp.concatenate(
        [
            jnp.concatenate(parts[head : head + 2], axis=0).T.astype(jnp.bfloat16)
            for head in range(0, HEADS, 2)
        ],
        axis=1,
    )


def attend_back_body(second, query, pair, grad, attended, log_total, *refs):
    if second:
        before, cosine, sine = refs[:3]
    d_query, d_keys, d_values = refs[-3:]
    rows = query.shape[0]
    products = {}

    def first(head):
        lanes, place, _ = head_lanes(head)
        if place == 0:
            product = grad[:, lanes].astype(jnp.float32) * attended[:, lanes].astype(jnp.float32)
            products[head] = products[head + 1] = product.T
        own = query[:, lanes] * head_mask((rows, 128), place)
        own_grad = grad[:, lanes] * head_mask((rows, 128), place)
        scores = dot(pair[:, lanes], own, 1, 1)
        d_probs = dot(pair[:, value_lanes(lanes)], own_grad, 1, 1)
        return own, own_grad, scores, d_probs

    def rest(head, given):
        own, own_grad, scores, d_probs = given
        lanes, place, turned = head_lanes(head)
        delta = column_sum(products[head][turned])
        probs = jnp.exp2(scores - log_total[0, head : head + 1, :])
        d_scores = (probs * (d_probs - delta)).astype(jnp.bfloat16)
        return (
            dot(pair[:, lanes].T[turned], d_scores),
            dot(d_scores, own),
            dot(probs.astype(jnp.bfloat16), own_grad),
        )

    parts = in_turn(HEADS, first, rest)
    for head in range(0, HEADS, 2):
        lanes = head_lanes(head)[0]
        one, two = parts[head : head + 2]
        turned = jnp.concatenate([one[0], two[0]], axis=0).T * HD ** (-0.5)
        if second:
            turned = rotate_lanes(turned + before[:, lanes], cosine[...], -sine[...])
        d_query[:, lanes] = turned.astype(d_query.dtype)
        d_keys[:, lanes] = ((one[1] + two[1]) * (1.0 / LOG2E)).astype(jnp.bfloat16)
        d_values[:, lanes] = (one[2] + two[2]).astype(jnp.bfloat16)


def attend_back(query, pair, grad, attended, log_total, before=None, after=(), free=()):
    rows, width = query.shape
    lanes = HEADS * HD
    steps = width // lanes
    block = columns(rows, lanes)
    second = before is not None
    extra = list(before) if second else []
    extra_specs = [block, full((rows, 128)), full((rows, 128))] if second else []
    return kernel_call(
        functools.partial(attend_back_body, second),
        steps,
        [
            block,
            columns(rows, 2 * lanes),
            block,
            block,
            pl.BlockSpec((1, HEADS, rows), lambda step: (step, 0, 0)),
        ]
        + extra_specs
        + [pl.BlockSpec(memory_space=pl.ANY)] * len(after),
        [block, block, block],
        [
            far((rows, width), jnp.bfloat16 if second else jnp.float32),
            far((rows, width), jnp.bfloat16),
            far((rows, width), jnp.bfloat16),
        ],
        [],
        28,
    )(query, pair, grad, attended, log_total, *extra, *after, free=free)


def block_body(
    own_down, attend_steps, hidden_steps,
    core, normed1, query_weight, cosine, sine, mods, up_bias, down_bias, *refs,
):
    pairs_far, refs = refs[: 2 * attend_steps], refs[2 * attend_steps :]
    (
        tokens_far, cotangent_far, out_far, up_far, down_far,
        query, attended, log_total, mixed, d_middle, d_attended, up_grad,
        down_keep, down_send, bias_grad, sums, peer_far,
        tokens, cotangent, out_weight, up_weight, down_weight, arrived,
        own_pairs, peer_pairs, pair_arrived, left,
        all_attended, normed, d_ffn, branch, middle, forward, back,
    ) = refs
    step = pl.program_id(0)
    tile = up_bias.shape[1]
    lanes = 2 * HEADS * HD
    own_arrivals, peer_arrivals, departures = [], [], []
    for index in range(attend_steps):
        own_arrivals.append(
            pltpu.make_async_copy(
                pairs_far[index], own_pairs.at[index], pair_arrived.at[0, index]
            )
        )
        peer_arrivals.append(
            pltpu.make_async_copy(
                pairs_far[attend_steps + index], peer_pairs.at[index], pair_arrived.at[1, index]
            )
        )
        departures.append(
            pltpu.make_async_copy(
                peer_pairs.at[index],
                peer_far.at[:, pl.ds(index * lanes, lanes)],
                left.at[index],
            )
        )
    arrivals = [
        pltpu.make_async_copy(source, target, arrived.at[index])
        for index, (source, target) in enumerate(
            (
                (tokens_far, tokens),
                (cotangent_far, cotangent),
                (out_far, out_weight),
                (up_far, up_weight),
                (down_far, down_weight),
            )
        )
    ]

    @pl.when(step == 0)
    def _():
        for index in range(attend_steps):
            own_arrivals[index].start()
            peer_arrivals[index].start()
        for arrival in arrivals:
            arrival.start()

    for index in range(attend_steps):

        @pl.when(step == index)
        def _(index=index):
            own_arrivals[index].wait()
            peer_arrivals[index].wait()
            departures[index].start()

    @pl.when(step < attend_steps)
    def _():
        value = rotate_lanes(dot(normed1[...], query_weight[...]), cosine[...], sine[...])
        query[...] = (value * (LOG2E * HD ** (-0.5))).astype(jnp.bfloat16)
        found = attend_heads(query, own_pairs.at[step], peer_pairs.at[step], log_total)
        attended[...] = found
        for index in range(attend_steps):

            @pl.when(step == index)
            def _(index=index):
                heads = HEADS * HD
                all_attended[:, index * heads : (index + 1) * heads] = found

    @pl.when(step == attend_steps)
    def _():
        for arrival in arrivals:
            arrival.wait()
        for departure in departures:
            departure.wait()
        turned = dot(all_attended[...], out_weight[...])
        branch[...] = turned.astype(jnp.bfloat16)
        value = tokens[...].astype(jnp.float32) + row(mods, GATE1) * turned
        middle[...] = value
        hat, _ = normalized(value)
        value = hat * row(mods, GAIN2) * (1.0 + row(mods, SCALE2)) + row(mods, SHIFT2)
        normed[...] = value.astype(jnp.bfloat16)
        low = (row(mods, GATE2) * cotangent[...].astype(jnp.float32)).astype(jnp.bfloat16)
        d_ffn[...] = low
        sums[4:5, :] = column_sum(low.astype(jnp.float32))
        forward[...] = jnp.zeros_like(forward)
        back[...] = jnp.zeros_like(back)

    @pl.when((step >= attend_steps) & (step < attend_steps + hidden_steps))
    def _():
        place = pl.ds(pl.multiple_of((step - attend_steps) * tile, tile), tile)
        pre = dot(normed[...], up_weight[:, place]) + up_bias[...]
        d_activated = dot(d_ffn[...], down_weight[place, :], 1, 1)
        root = 0.7978845608028654
        square = pre * pre
        bent = jnp.tanh(root * pre * (1.0 + 0.044715 * square))
        half = 0.5 + 0.5 * bent
        slope = half + (0.5 * root) * pre * (1.0 - bent * bent) * (1.0 + 0.134145 * square)
        low = (pre * half).astype(jnp.bfloat16)
        d_pre = d_activated * slope
        d_low = d_pre.astype(jnp.bfloat16)
        bias_grad[...] = column_sum(d_pre)
        down_grad = dot(low, d_ffn[...], 0, 0).astype(jnp.bfloat16)
        store_split(down_grad, core, own_down, down_keep, down_send)
        up_grad[...] = dot(normed[...], d_low, 0, 0).astype(jnp.bfloat16)
        forward[...] += dot(low, down_weight[place, :])
        back[...] += dot(d_low, up_weight[:, place], 1, 1)

    @pl.when(step == attend_steps + hidden_steps)
    def _():
        grad = cotangent[...].astype(jnp.float32)
        held = middle[...]
        hat, inverse = normalized(held)
        factor = row(mods, GAIN2) * (1.0 + row(mods, SCALE2))
        value = back[...]
        d_value = grad + norm_back(value, hat, inverse, factor)
        d_middle[...] = d_value
        d_branch = (row(mods, GATE1) * d_value).astype(jnp.bfloat16)
        d_attended[...] = dot(d_branch, out_weight[...], 1, 1).astype(jnp.bfloat16)
        up_grad[...] = dot(all_attended[...], d_branch, 0, 0).astype(jnp.bfloat16)
        ffn = forward[...] + down_bias[...]
        mixed[...] = (held + row(mods, GATE2) * ffn).astype(jnp.bfloat16)
        sums[0:1, :] = column_sum(value)
        sums[1:2, :] = column_sum(value * hat)
        sums[2:3, :] = column_sum(d_value * branch[...].astype(jnp.float32))
        sums[3:4, :] = column_sum(grad * ffn)
        sums[5:8, :] = jnp.zeros_like(sums[5:8, :])


def split_rows(rows):
    own = rows // lax.axis_size("dp")
    return own if own % 16 == 0 else rows // 2


def block_layer(
    core, normed1, qkv_weight, cosine, sine, mods, up_bias, down_bias, own, peer,
    tokens, cotangent, out_weight, up_weight, down_weight,
):
    rows, width = tokens.shape
    hidden = up_weight.shape[1]
    tile = width
    lanes = HEADS * HD
    attend_steps = width // lanes
    hidden_steps = hidden // tile
    own_down = hidden // lax.axis_size("dp")
    if own_down % 16 > 0:
        own_down = tile // 2

    def heads(first=0):
        return pl.BlockSpec(
            (rows, lanes), lambda step: (0, jnp.minimum(step, attend_steps - 1) + first)
        )

    def tiles(step):
        return jnp.clip(step - attend_steps, 0, hidden_steps - 1)

    def up_tiles(step):
        return jnp.clip(step - attend_steps, 0, hidden_steps)

    block = full((rows, width))
    far_spec = pl.BlockSpec(memory_space=pl.ANY)
    low = jnp.bfloat16
    up_spec = pl.BlockSpec((width, tile), lambda step: (0, up_tiles(step)))
    down_spec = pl.BlockSpec((tile // 2, width), lambda step: (tiles(step), 0))
    return kernel_call(
        functools.partial(block_body, own_down, attend_steps, hidden_steps),
        attend_steps + hidden_steps + 1,
        [
            scalar_spec(),
            block,
            pl.BlockSpec((width, lanes), lambda step: (0, jnp.minimum(step, attend_steps - 1))),
            full((rows, 128)),
            full((rows, 128)),
            full((16, width)),
            pl.BlockSpec((1, tile), lambda step: (0, tiles(step))),
            full((1, width)),
        ]
        + [far_spec] * (2 * attend_steps + 5),
        [
            heads(),
            heads(),
            pl.BlockSpec(
                (1, HEADS, rows), lambda step: (jnp.minimum(step, attend_steps - 1), 0, 0)
            ),
            block,
            block,
            block,
            up_spec,
            down_spec,
            down_spec,
            pl.BlockSpec((1, tile), lambda step: (0, tiles(step))),
            full((8, width)),
            far_spec,
        ],
        [
            far((rows, width), low),
            far((rows, width), low),
            far((attend_steps, HEADS, rows), jnp.float32),
            far((rows, width), low),
            far((rows, width), jnp.float32),
            far((rows, width), low),
            far((width, hidden + width), low),
            far((hidden // 2, width), low),
            far((hidden // 2, width), low),
            far((1, hidden), jnp.float32),
            far((8, width), jnp.float32),
            far((rows, 2 * width), low),
        ],
        [
            pltpu.VMEM((rows, width), low),
            pltpu.VMEM((rows, width), low),
            pltpu.VMEM((width, width), low),
            pltpu.VMEM((width, hidden), low),
            pltpu.VMEM((hidden, width), low),
            pltpu.SemaphoreType.DMA((5,)),
            pltpu.VMEM((attend_steps, rows, 2 * lanes), low),
            pltpu.VMEM((attend_steps, rows, 2 * lanes), low),
            pltpu.SemaphoreType.DMA((2, attend_steps)),
            pltpu.SemaphoreType.DMA((attend_steps,)),
            pltpu.VMEM((rows, width), low),
            pltpu.VMEM((rows, width), low),
            pltpu.VMEM((rows, width), low),
            pltpu.VMEM((rows, width), low),
            pltpu.VMEM((rows, width), jnp.float32),
            pltpu.VMEM((rows, width), jnp.float32),
            pltpu.VMEM((rows, width), jnp.float32),
        ],
        58,
    )(
        core, normed1, qkv_weight, cosine, sine, mods, up_bias, down_bias, *own, *peer,
        tokens, cotangent, out_weight, up_weight, down_weight,
        free=(*peer, cotangent, tokens),
    )


def projected_back_body(
    own, core, d_query, d_keys, d_values, peer_keys, peer_values, normed, cosine, sine,
    d_projected, *parts,
):
    lanes = HEADS * HD
    keys = d_keys[...].astype(jnp.float32) + peer_keys[...].astype(jnp.float32)
    keys = rotate_lanes(keys, cosine[...], -sine[...]).astype(jnp.bfloat16)
    values = d_values[...].astype(jnp.float32) + peer_values[...].astype(jnp.float32)
    low = jnp.concatenate([d_query[...], keys, values.astype(jnp.bfloat16)], axis=1)
    d_projected[...] = low
    grad = dot(normed[...], low, 0, 0).astype(jnp.bfloat16)
    for index in range(3):
        third = grad[:, index * lanes : (index + 1) * lanes]
        store_split(third, core, own, parts[2 * index], parts[2 * index + 1])


def projected_back(core, d_query, d_keys, d_values, peer_keys, peer_values, normed, cosine, sine):
    rows, width = normed.shape
    lanes = HEADS * HD
    block = columns(rows, lanes)
    return kernel_call(
        functools.partial(projected_back_body, split_rows(width)),
        width // lanes,
        [
            scalar_spec(),
            block,
            block,
            block,
            block,
            block,
            full((rows, width)),
            full((rows, 128)),
            full((rows, 128)),
        ],
        [columns(rows, 3 * lanes)] + [columns(width // 2, lanes)] * 6,
        [far((rows, 3 * width), jnp.bfloat16)] + [far((width // 2, width), jnp.bfloat16)] * 6,
        [],
        32,
    )(
        core, d_query, d_keys, d_values, peer_keys, peer_values, normed, cosine, sine,
        free=(peer_keys, peer_values),
    )


def tokens_back_body(
    d_projected, weight1, weight2, weight3, tokens, d_middle, mods, sums, bias_grad, *refs
):
    out, small, total = refs[-3:]
    step = pl.program_id(0)
    width = tokens.shape[1]
    lanes = HEADS * HD
    part = sum(
        dot(d_projected[:, index * lanes : (index + 1) * lanes], weight[...], 1, 1)
        for index, weight in enumerate((weight1, weight2, weight3))
    )

    @pl.when(step == 0)
    def _():
        total[...] = part

    @pl.when(step > 0)
    def _():
        total[...] += part

    @pl.when(step == pl.num_programs(0) - 1)
    def _():
        back = total[...]
        hat, inverse = normalized(tokens[...].astype(jnp.float32))
        scale1 = 1.0 + row(mods, SCALE1)
        gain1 = row(mods, GAIN1)
        out[...] = (d_middle[...] + norm_back(back, hat, inverse, gain1 * scale1)).astype(
            jnp.bfloat16
        )
        hat_sum1 = column_sum(back * hat)
        hat_sum2 = row(sums, 1)
        rows = [
            column_sum(back),
            hat_sum1 * gain1,
            row(sums, 2),
            row(sums, 0),
            hat_sum2 * row(mods, GAIN2),
            row(sums, 3),
            row(mods, COND) * 0.5,
            jnp.zeros_like(hat_sum1),
            hat_sum1 * scale1,
            hat_sum2 * (1.0 + row(mods, SCALE2)),
            row(sums, 4),
        ]
        for index in range(bias_grad.shape[1] // width):
            rows.append(bias_grad[:, index * width : (index + 1) * width])
        for index, value in enumerate(rows):
            small[index : index + 1, :] = value
        small[len(rows) :, :] = jnp.zeros_like(small[len(rows) :, :])


def tokens_back(d_projected, weight, tokens, d_middle, mods, sums, bias_grad, after):
    rows, width = tokens.shape
    lanes = HEADS * HD
    steps = width // lanes
    block = full((rows, width))
    return kernel_call(
        tokens_back_body,
        steps,
        [
            columns(rows, 3 * lanes),
            columns(width, lanes),
            columns(width, lanes, steps),
            columns(width, lanes, 2 * steps),
            block,
            block,
            full((16, width)),
            full((8, width)),
            full(bias_grad.shape),
        ]
        + [pl.BlockSpec(memory_space=pl.ANY)] * len(after),
        [block, full((16, width))],
        [far((rows, width), jnp.bfloat16), far((16, width), jnp.float32)],
        [pltpu.VMEM((rows, width), jnp.float32)],
        36,
    )(d_projected, weight, weight, weight, tokens, d_middle, mods, sums, bias_grad, *after)


def finish_body(
    places, here, there, embedded, ada_weight,
    first_gain, second_gain, up_bias, down_bias, ada_bias, ada_grad, cond_grad, every,
):
    width = here.shape[1]
    sequences = (here.shape[0] - 8) // 8
    own_columns = ada_grad.shape[1]
    sums = here[8 * sequences :, :] + there[8 * sequences :, :]
    first_gain[...] = sums[0, :]
    second_gain[...] = sums[1, :]
    down_bias[...] = sums[2, :]
    for index in range(up_bias.shape[0] // width):
        up_bias[index * width : (index + 1) * width] = sums[3 + index, :]
    total = here[:8, :] + there[:8, :]
    for index in range(1, sequences):
        rows = slice(8 * index, 8 * index + 8)
        total = total + here[rows, :] + there[rows, :]
    conds = []
    for side, block in enumerate((here, there)):
        for index in range(sequences):
            conds.append(block[8 * index + 6 : 8 * index + 7, : embedded.shape[1]])
            for part in range(6):
                every[
                    side * sequences + index : side * sequences + index + 1,
                    part * width : (part + 1) * width,
                ] = block[8 * index + part : 8 * index + part + 1, :]
    for part in range(6):
        ada_bias[part * width : (part + 1) * width] = total[part, :]
    turned = pltpu.roll(every[...], places[0], 1)[:, : -(-own_columns // 128) * 128]
    grad = lax.dot_general(
        jnp.concatenate(conds, axis=0),
        turned,
        (((0,), (0,)), ((), ())),
        precision=highest,
        preferred_element_type=jnp.float32,
    )
    ada_grad[...] = grad[:, :own_columns]
    own = jnp.where(places[1] == 1, here[:8, :], there[:8, :])
    products = ada_weight[:, :width].astype(jnp.float32) * own[0:1, :]
    for part in range(1, 6):
        columns_here = ada_weight[:, part * width : (part + 1) * width].astype(jnp.float32)
        products = products + columns_here * own[part : part + 1, :]
    summed = jnp.sum(products, axis=1, keepdims=True)
    turned_sum = jnp.broadcast_to(summed, (summed.shape[0], 128)).T[0:1, :]
    value = embedded[...]
    sigmoid = 1.0 / (1.0 + jnp.exp(-value))
    cond_grad[...] = turned_sum * (sigmoid * (1.0 + value * (1.0 - sigmoid)))


def finish(here, there, embedded, ada_weight, hidden):
    width = here.shape[1]
    sequences = (here.shape[0] - 8) // 8
    dp_size, dp_rank = lax.axis_size("dp"), lax.axis_index("dp")
    all_columns = ada_weight.shape[1]
    own_columns = all_columns // dp_size
    turn = (all_columns - dp_rank * own_columns) % all_columns
    same = (lax.axis_index("seq") == dp_rank % 2).astype(jnp.int32)
    kind = jnp.float32
    whole = pl.BlockSpec(memory_space=pltpu.VMEM)
    return pl.pallas_call(
        finish_body,
        in_specs=[scalar_spec(), whole, whole, whole, whole],
        out_specs=[whole] * 7,
        out_shape=[
            shaped((width,), kind),
            shaped((width,), kind),
            shaped((hidden,), kind),
            shaped((width,), kind),
            shaped((all_columns,), kind),
            shaped((ada_weight.shape[0], own_columns), kind),
            shaped((1, ada_weight.shape[0]), kind),
        ],
        scratch_shapes=[pltpu.VMEM((2 * sequences, all_columns), kind)],
        compiler_params=pltpu.CompilerParams(vmem_limit_bytes=24 * 1024 * 1024),
        cost_estimate=pl.CostEstimate(flops=1, bytes_accessed=1, transcendentals=0),
    )(jnp.stack([turn, same]), here, there, embedded, ada_weight)


def swap_halves(block):
    count = lax.axis_size("dp") * lax.axis_size("seq")
    target = {1: 2, 2: 1}
    perm = [(i, i - i % 4 + target.get(i % 4, i % 4)) for i in range(count)]
    return lax.ppermute(block, ("dp", "seq"), perm)


def swap_bit(block, bit):
    return lax.ppermute(block, "dp", [(i, i ^ bit) for i in range(lax.axis_size("dp"))])


def swap_cores(block):
    return swap_bit(block, 1)


def swap_seq(block):
    return lax.ppermute(block, "seq", [(0, 1), (1, 0)])


def dp_bits():
    bits, bit = [], 1
    while bit < lax.axis_size("dp"):
        bits.append(bit)
        bit *= 2
    return bits


def pick(block, axis, index):
    return lax.dynamic_index_in_dim(block, index, axis, keepdims=False)


class Flow:
    def __init__(self, got, kept, lanes=None):
        self.got, self.kept = got, kept
        self.lanes = lanes or (0, kept.shape[2])
        self.count, self.rest = kept.shape[:2]
        self.width = self.lanes[1] - self.lanes[0]


def stage_body(jobs, counts, mine, *refs):
    inputs = refs[: counts[0]]
    outputs = refs[counts[0] + counts[1] :]

    def terms(sources, place):
        for one, two, lanes, rows in sources:
            total = inputs[one][place + (slice(None), lanes)].astype(jnp.float32)
            total = total + inputs[two][place + (slice(None), lanes)].astype(jnp.float32)
            total = total.astype(jnp.bfloat16)
            height = total.shape[-2]
            for start in range(0, height, rows):
                yield total if height == rows else total[..., start : start + rows, :]

    def store(out, place, values):
        at = 0
        for value in values:
            width = value.shape[-1]
            out[place + (slice(None), slice(at, at + width))] = value
            at += width

    def run(index, kind, stride, sources, target):
        if kind == "sum":
            store(outputs[target], (slice(None),), terms(sources, (slice(None),)))
            return

        def part(out, which):
            if kind == "half":
                halves = []
                for one, two, lanes, rows in sources:
                    middle = (lanes.start + lanes.stop) // 2
                    first, second = slice(lanes.start, middle), slice(middle, lanes.stop)
                    halves.append((one, two, second if which else first, rows))
                store(out, (slice(None),), terms(halves, (slice(None),)))
                return
            for block in range(out.shape[0]):
                high, low = divmod(block, stride)
                place = (2 * high + which) * stride + low
                store(out, (block,), terms(sources, (place,)))

        for which in range(2):

            @pl.when(mine[index] == which)
            def _(which=which):
                part(outputs[target + 1], which)
                part(outputs[target], 1 - which)

    for index, (kind, stride, sources, target, whole) in enumerate(jobs):
        if whole:

            @pl.when(pl.program_id(0) == 0)
            def _(args=(index, kind, stride, sources, target)):
                run(*args)

        else:
            run(index, kind, stride, sources, target)


def small_body(first, one, two, out):
    rows = one.shape[0] - 8

    @pl.when(pl.program_id(0) == 0)
    def _():
        if first:
            out[...] = one[...] + two[...]
        else:
            out[:rows, :] = one[:rows, :]
            out[rows : 2 * rows, :] = two[:rows, :]
            out[2 * rows :, :] = one[rows:, :] + two[rows:, :]


def stage(steps, jobs, after=(), small=None, free=(), relay=None):
    seq_rank, dp_rank = lax.axis_index("seq"), lax.axis_index("dp")
    inputs, in_specs, specs, out_specs, out_shape, mine = [], [], [], [], [], []
    free = [*free] + [flow.got for flows, _ in jobs for flow in flows]

    def spec(shape, whole):
        if whole:
            return full(shape)
        return pl.BlockSpec((shape[0] // steps,) + shape[1:], lambda at: (at, 0, 0))

    def place_of(array, whole):
        for index, other in enumerate(inputs):
            if other is array:
                return index
        inputs.append(array)
        in_specs.append(spec(array.shape, whole))
        return len(inputs) - 1

    for flows, step in jobs:
        bit, stride = step if isinstance(step, tuple) else (None, 1)
        rest, count = flows[0].rest, flows[0].count
        smallest = 1 if bit is None else 2 * stride
        whole = count % steps > 0 or (count // steps) % smallest > 0
        sources = [
            (place_of(flow.got, whole), place_of(flow.kept, whole), slice(*flow.lanes), rest)
            for flow in flows
        ]
        width = sum(flow.width * flow.rest // rest for flow in flows)
        if bit is not None:
            shape = (count // 2, rest, width)
            mine.append((dp_rank // bit) % 2)
        else:
            shape = (count, rest, width // 2 if step == "half" else width)
            mine.append(seq_rank)
        specs.append((step if bit is None else "bit", stride, sources, len(out_shape), whole))
        results = 1 if step == "sum" else 2
        out_shape += [far(shape, jnp.bfloat16)] * results
        out_specs += [spec(shape, whole)] * results
    counts = (len(inputs), len(after))
    extra = []
    if small is not None:
        got, kept, first = small
        extra = [kept, got]
        rows = kept.shape[0] if first else 2 * kept.shape[0] - 8
        out_shape.append(far((rows, kept.shape[1]), jnp.float32))
        out_specs.append(full((rows, kept.shape[1])))

    if relay is not None:
        extra.append(relay)
        out_shape.append(far(relay.shape, relay.dtype))
        out_specs.append(full(relay.shape))

    def body(mine, *refs):
        if relay is not None:
            place = sum(counts) + len(extra) - 1
            refs[-1][...] = refs[place][...]
            refs = (*refs[:place], *refs[place + 1 : -1])
        if small is None:
            stage_body(specs, counts, mine, *refs)
            return
        main, ends = refs[: sum(counts)], refs[sum(counts) :]
        small_body(first, ends[0], ends[1], ends[-1])
        stage_body(specs, counts, mine, *main, *ends[2:-1])

    results = kernel_call(
        body,
        steps,
        [scalar_spec()]
        + in_specs
        + [pl.BlockSpec(memory_space=pl.ANY)] * len(after)
        + [full(array.shape) for array in extra],
        out_specs,
        out_shape,
        [],
        40,
    )(jnp.stack(mine), *inputs, *after, *extra, free=(*free, *extra[1:2]))
    new = []
    for (flows, step), (_, _, _, target, _) in zip(jobs, specs):
        sent = results[target]
        got = swap_seq(sent) if isinstance(step, str) else swap_bit(sent, step[0])
        new.append(Flow(got, sent if step == "sum" else results[target + 1]))
    if small is not None:
        new.append(results[-1 if relay is None else -2])
    if relay is not None:
        new.append(results[-1])
    return new, results[0]


def from_tiles(kept, sent, tile):
    rows, width = 2 * kept.shape[0], kept.shape[1]
    core = lax.axis_index("dp") % 2
    first = jnp.where(core == 0, kept, sent).reshape(rows // tile, 1, tile // 2, width)
    second = jnp.where(core == 0, sent, kept).reshape(rows // tile, 1, tile // 2, width)
    return jnp.concatenate([first, second], axis=1).reshape(rows, width)


def plain_sum(kept, sent, tile):
    matrix = from_tiles(kept, sent, tile)
    return lax.psum(
        lax.psum_scatter(matrix, "dp", scatter_dimension=0, tiled=True).astype(jnp.float32), "seq"
    )


def joined(flow, widths):
    block, got = flow.kept[0].astype(jnp.float32), flow.got[0].astype(jnp.float32)
    here = lax.axis_index("seq") == 0
    first, second = jnp.where(here, block, got), jnp.where(here, got, block)
    parts, at = [], 0
    for width in widths:
        parts.append(
            jnp.concatenate([first[:, at : at + width], second[:, at : at + width]], axis=1)
        )
        at += width
    return parts


def per_device(
    tokens,
    cotangent,
    time_index,
    step_table,
    first_gain,
    attn_qkv,
    attn_out,
    second_gain,
    mlp_up,
    up_bias,
    mlp_down,
    down_bias,
    ada_weight,
    ada_bias,
):
    rows, width = tokens.shape[1:]
    dp_rank = lax.axis_index("dp")
    core = dp_rank % 2
    own_embedded = lax.dynamic_slice_in_dim(step_table, time_index[0], 1, axis=0)
    positions = core * rows + jnp.arange(rows, dtype=jnp.int32)
    cosine, sine = tables(positions)
    tokens = swap_halves(tokens[0])
    time_index = swap_halves(time_index)
    cotangent = swap_halves(cotangent[0])
    cond = jax.nn.silu(lax.dynamic_slice_in_dim(step_table, time_index[0], 1, axis=0))
    ada_float = ada_weight.astype(jnp.float32)
    modulation = jnp.dot(cond, ada_float, precision=highest) + ada_bias.astype(jnp.float32)
    gain1 = first_gain.astype(jnp.float32)
    gain2 = second_gain.astype(jnp.float32)
    cond_row = jnp.pad(cond, ((0, 0), (0, width - cond.shape[1])))
    mods = jnp.concatenate(
        [modulation.reshape(6, width), gain1[None], gain2[None], cond_row, jnp.zeros((7, width))]
    )
    normed1, own_pair, *own_parts = project_key_value(tokens, mods, attn_qkv, cosine, sine)
    peer_parts = [swap_cores(part) for part in own_parts]
    core_ref = core[None]
    (
        query, attended, log_total, mixed, d_middle, d_attended, up_grad,
        down_keep, down_send, up_bias_grad, sums2, peer_pair,
    ) = block_layer(
        core_ref, normed1, attn_qkv, cosine, sine, mods,
        up_bias.astype(jnp.float32)[None], down_bias.astype(jnp.float32)[None],
        own_parts, peer_parts,
        tokens, cotangent, attn_out, mlp_up, mlp_down,
    )
    hidden = mlp_up.shape[1]
    dp_size = lax.axis_size("dp")
    bits = dp_bits()
    by_steps = split_rows(width) == width // dp_size and len(bits) == 4
    mixed = swap_halves(mixed)
    up_rows = lax.psum_scatter(up_grad, "dp", scatter_dimension=0, tiled=True)
    up_got = swap_seq(up_rows)

    def blocks(part):
        return part.reshape(dp_size // 2, -1, part.shape[1])

    if by_steps:
        down = Flow(swap_cores(blocks(down_send)), blocks(down_keep))
    d_query, away_keys, away_values = attend_back(query, peer_pair, d_attended, attended, log_total)
    after = ()
    if by_steps:
        (down,), sent = stage(4, [([down], "half")], (away_keys, mixed), free=(mixed,))
        after = (sent,)
    peer_keys, peer_values = swap_cores(away_keys), swap_cores(away_values)
    d_query, d_keys, d_values = attend_back(
        query, own_pair, d_attended, attended, log_total, (d_query, cosine, sine), after
    )
    d_projected, *qkv_parts = projected_back(
        core_ref, d_query, d_keys, d_values, peer_keys, peer_values, normed1, cosine, sine
    )
    sent = ()
    if by_steps:
        late = [
            Flow(swap_cores(blocks(send)), blocks(keep))
            for keep, send in zip(qkv_parts[::2], qkv_parts[1::2])
        ]
        (late,), *sent = stage(4, [(late, "half")])
        (down,), *sent = stage(4, [([down], (bits[1], 1))], sent)
    tokens_grad, small = tokens_back(
        d_projected, attn_qkv, tokens, d_middle, mods, sums2, up_bias_grad, sent
    )
    small = small + swap_cores(small)
    moves = [functools.partial(swap_bit, bit=bit) for bit in bits[2:] + bits[1:2]] + [swap_seq]

    def doubled(small, got):
        return jnp.concatenate([small[:-8], got[:-8], small[-8:] + got[-8:]], axis=0)

    if by_steps:

        def next_stage(jobs, count, moves_before, after=(), relay=None):
            nonlocal small, sent
            for _ in range(moves_before):
                small = doubled(small, moves.pop(0)(small))
            extra = (moves.pop(0)(small), small, False) if len(moves) > 0 else None
            flows, *sent = stage(count, jobs, (*sent, *after), extra, after, relay)
            if extra is not None:
                small = flows.pop(len(jobs))
            return flows

        down, late, tokens_grad = next_stage(
            [([down], (bits[2], 1)), ([late], (bits[1], 1))], 2, 0, (), tokens_grad
        )
        down, late = next_stage([([down], (bits[3], 1)), ([late], (bits[2], 1))], 2, 0)
        down, late = next_stage([([down], "sum"), ([late], (bits[3], 1))], 1, 0, (up_got,))
        last = moves.pop(0)(small)
        (late,) = next_stage([([late], "sum")], 1, 0)
        (
            first_gain_grad, second_gain_grad, all_up_bias_grad, down_bias_grad, ada_bias_grad,
            ada_weight_grad, cond_grad,
        ) = finish(small, last, own_embedded, ada_weight, hidden)
        (down_rows,) = joined(down, (width // 2,))
        qkv_rows = jnp.concatenate(joined(late, (width // 2,) * 3), axis=1)
    else:
        for move in moves:
            small = doubled(small, move(small))
        down_rows = plain_sum(down_keep, down_send, width)
        qkv_rows = jnp.concatenate(
            [
                plain_sum(keep, send, width)
                for keep, send in zip(qkv_parts[::2], qkv_parts[1::2])
            ],
            axis=1,
        )
        per_sequence, sums = small[:-8].reshape(-1, 8, width), small[-8:]
        d_mod_all = per_sequence[:, :6].reshape(per_sequence.shape[0], 6 * width)
        cond_all = per_sequence[:, 6, : cond.shape[1]]
        own_columns = d_mod_all.shape[1] // dp_size
        mine = lax.dynamic_slice_in_dim(d_mod_all, dp_rank * own_columns, own_columns, axis=1)
        ada_weight_grad = lax.dot_general(
            cond_all, mine, (((0,), (0,)), ((), ())), precision=highest
        )
        other = d_mod_all.shape[0] // 2
        d_mod_own = jnp.where(
            lax.axis_index("seq") == core, d_mod_all[:1], d_mod_all[other : other + 1]
        )
        _, silu_back = jax.vjp(jax.nn.silu, own_embedded)
        (cond_grad,) = silu_back(jnp.dot(d_mod_own, ada_float.T, precision=highest))
        first_gain_grad, second_gain_grad, down_bias_grad = sums[0], sums[1], sums[2]
        all_up_bias_grad = sums[3:7].reshape(-1)
        ada_bias_grad = jnp.sum(d_mod_all, axis=0)
    up_rows = up_rows.astype(jnp.float32) + up_got.astype(jnp.float32)
    return (
        mixed[None],
        swap_halves(tokens_grad).astype(jnp.float32)[None],
        cond_grad,
        first_gain_grad,
        qkv_rows,
        up_rows[:, hidden:],
        second_gain_grad,
        up_rows[:, :hidden],
        all_up_bias_grad,
        down_rows,
        down_bias_grad,
        ada_weight_grad,
        ada_bias_grad,
    )


def solution(mesh):
    placed = (
        P("dp", "seq", None),
        P("dp", "seq", None),
        P("dp"),
        P(),
        P(),
        P(),
        P(),
        P(),
        P(),
        P(),
        P(),
        P(),
        P(),
        P(),
    )
    return jax.shard_map(
        per_device,
        mesh=mesh,
        in_specs=placed,
        out_specs=(
            P("dp", "seq", None),
            P("dp", "seq", None),
            P("dp", None),
            P(),
            P("dp", None),
            P("dp", None),
            P(),
            P("dp", None),
            P(),
            P("dp", None),
            P(),
            P(None, "dp"),
            P(),
        ),
        check_vma=False,
    )
```

```python
import functools

import jax
import jax.numpy as jnp
from jax import lax
from jax.experimental import pallas as pl
from jax.experimental.pallas import tpu as pltpu
from jax.sharding import PartitionSpec as P

HD = 64
LOG2E = 1.4426950408889634


highest = lax.Precision.HIGHEST


def tables(positions):
    half_dim = HD // 2
    frequency = jnp.exp(
        -jnp.log(10000.0) * (2.0 * jnp.arange(half_dim, dtype=jnp.float32) / HD)
    )
    angles = positions.astype(jnp.float32)[:, None] * frequency[None, :]
    cosine, sine = jnp.cos(angles), jnp.sin(angles)
    return (
        jnp.concatenate([cosine] * 4, axis=1),
        jnp.concatenate([-sine, sine, -sine, sine], axis=1),
    )


def full(shape):
    return pl.BlockSpec(shape, lambda step: (0,) * len(shape))


def columns(rows, width, first=0):
    return pl.BlockSpec((rows, width), lambda step: (0, step + first))


def shaped(shape, kind):
    return jax.ShapeDtypeStruct(shape, kind)


def far(shape, kind):
    return pltpu.HBM(shape, kind)


def store_split(low, core, own, keep, send):
    pairs = low.shape[0] // (2 * own)

    def store(kept):
        for pair in range(pairs):
            rows = slice(pair * own, (pair + 1) * own)
            for parity, target in ((kept, keep), (1 - kept, send)):
                start = (2 * pair + parity) * own
                target[rows, :] = low[start : start + own, :]

    @pl.when(core[0] == 0)
    def _():
        store(0)

    @pl.when(core[0] == 1)
    def _():
        store(1)


def zero_shape():
    return jax.ShapeDtypeStruct((1, 1), jnp.float32)


def scalar_spec():
    return pl.BlockSpec(memory_space=pltpu.SMEM)


def kernel_call(body, steps, in_specs, out_specs, out_shape, scratch, grant):
    call = pl.pallas_call(
        body,
        grid=(steps,),
        in_specs=in_specs,
        out_specs=out_specs,
        out_shape=out_shape,
        scratch_shapes=scratch,
        compiler_params=pltpu.CompilerParams(
            dimension_semantics=("arbitrary",), vmem_limit_bytes=grant * 1024 * 1024
        ),
        cost_estimate=pl.CostEstimate(flops=1, bytes_accessed=1, transcendentals=0),
    )

    def run(*args, free=()):
        placed = []
        for arg in args:
            if arg.size > 4096 and not any(arg is other for other in free):
                arg = pltpu.with_memory_space_constraint(arg, pltpu.HBM)
            placed.append(arg)
        return call(*placed)

    return run


def dot(left, right, left_axis=1, right_axis=0):
    return lax.dot_general(
        left,
        right,
        (((left_axis,), (right_axis,)), ((), ())),
        preferred_element_type=jnp.float32,
    )


def normalized(inputs):
    center = inputs - jnp.mean(inputs, axis=-1, keepdims=True)
    inverse = lax.rsqrt(jnp.mean(center * center, axis=-1, keepdims=True) + 1e-05)
    return center * inverse, inverse


def norm_back(back, hat, inverse, factor):
    scaled = back * factor
    return inverse * (
        scaled
        - jnp.mean(scaled, axis=-1, keepdims=True)
        - hat * jnp.mean(scaled * hat, axis=-1, keepdims=True)
    )


def column_sum(values):
    return jnp.sum(values, axis=0, keepdims=True)


SHIFT1, SCALE1, GATE1, SHIFT2, SCALE2, GATE2, GAIN1, GAIN2, COND = range(9)


def row(ref, index):
    return ref[index : index + 1, :]


def rotate_lanes(values, cosine, sine):
    lane = lax.broadcasted_iota(jnp.int32, cosine.shape, 1)
    lower = (lane % HD) < HD // 2
    parts = []
    for start in range(0, values.shape[1], 128):
        part = values[:, start : start + 128]
        other = jnp.where(lower, pltpu.roll(part, 128 - HD // 2, 1), pltpu.roll(part, HD // 2, 1))
        parts.append(part * cosine + other * sine)
    return jnp.concatenate(parts, axis=1)


HEADS = 4


def key_value_body(
    tokens, mods, key_weight, value_weight, cosine, sine, normed, every, *parts
):
    step = pl.program_id(0)

    @pl.when(step == 0)
    def _():
        hat, _ = normalized(tokens[...].astype(jnp.float32))
        value = hat * row(mods, GAIN1) * (1.0 + row(mods, SCALE1)) + row(mods, SHIFT1)
        normed[...] = value.astype(jnp.bfloat16)

    keys = rotate_lanes(dot(normed[...], key_weight[...]), cosine[...], sine[...])
    values = dot(normed[...], value_weight[...])
    both = jnp.concatenate([keys, values], axis=1).astype(jnp.bfloat16)
    every[...] = both
    for index, part in enumerate(parts):

        @pl.when(step == index)
        def _(part=part):
            part[...] = both


def project_key_value(tokens, mods, weight, cosine, sine):
    rows, width = tokens.shape
    lanes = HEADS * HD
    steps = width // lanes
    low = jnp.bfloat16
    return kernel_call(
        key_value_body,
        steps,
        [
            full((rows, width)),
            full((16, width)),
            columns(width, lanes, steps),
            columns(width, lanes, 2 * steps),
            full((rows, 128)),
            full((rows, 128)),
        ],
        [full((rows, width)), columns(rows, 2 * lanes)] + [full((rows, 2 * lanes))] * steps,
        [far((rows, width), low), far((rows, 2 * width), low)]
        + [far((rows, 2 * lanes), low)] * steps,
        [],
        24,
    )(tokens, mods, weight, weight, cosine, sine, free=(tokens,))


def head_mask(shape, head):
    lane = lax.broadcasted_iota(jnp.int32, shape, 1)
    return jnp.where(lane // HD == head, 1.0, 0.0).astype(jnp.bfloat16)


def head_lanes(head):
    pair, place = divmod(head, 2)
    return slice(pair * 128, (pair + 1) * 128), place, slice(place * HD, (place + 1) * HD)


def value_lanes(lanes):
    return slice(HEADS * HD + lanes.start, HEADS * HD + lanes.stop)


def in_turn(count, first, rest):
    results = []
    ahead = first(0)
    for index in range(count):
        now = ahead
        if index + 1 < count:
            ahead = first(index + 1)
        results.append(rest(index, now))
    return results


def attend_heads(query, pair1, pair2, log_total, shifted):
    rows = query.shape[0]

    def first(head):
        lanes, place, _ = head_lanes(head)
        own = query[:, lanes] * head_mask((rows, 128), place)
        return dot(pair1[:, lanes], own, 1, 1), dot(pair2[:, lanes], own, 1, 1)

    def rest(head, scores):
        lanes, place, turned = head_lanes(head)
        scores1, scores2 = scores
        if shifted:
            top = jnp.maximum(
                jnp.max(scores1, axis=0, keepdims=True), jnp.max(scores2, axis=0, keepdims=True)
            )
            scores1, scores2 = scores1 - top, scores2 - top
        exps1, exps2 = jnp.exp2(scores1), jnp.exp2(scores2)
        total = column_sum(exps1) + column_sum(exps2)
        lanes = value_lanes(lanes)
        mixed = dot(pair1[:, lanes].T[turned], exps1.astype(jnp.bfloat16)) + dot(
            pair2[:, lanes].T[turned], exps2.astype(jnp.bfloat16)
        )
        log_sum = jnp.log2(total)
        log_total[0, head : head + 1, :] = top + log_sum if shifted else log_sum
        return mixed * (1.0 / total)

    parts = in_turn(HEADS, first, rest)
    logs = log_total[0]
    in_range = (jnp.min(logs) > -60.0) & (jnp.max(logs) < 60.0)
    return in_range, jnp.concatenate(
        [
            jnp.concatenate(parts[head : head + 2], axis=0).T.astype(jnp.bfloat16)
            for head in range(0, HEADS, 2)
        ],
        axis=1,
    )


def attend_back_body(second, query, pair, grad, attended, log_total, *refs):
    if second:
        before, cosine, sine = refs[:3]
    d_query, d_keys, d_values = refs[-3:]
    rows = query.shape[0]
    products = {}

    def first(head):
        lanes, place, _ = head_lanes(head)
        if place == 0:
            product = grad[:, lanes].astype(jnp.float32) * attended[:, lanes].astype(jnp.float32)
            products[head] = products[head + 1] = product.T
        own = query[:, lanes] * head_mask((rows, 128), place)
        own_grad = grad[:, lanes] * head_mask((rows, 128), place)
        scores = dot(pair[:, lanes], own, 1, 1)
        d_probs = dot(pair[:, value_lanes(lanes)], own_grad, 1, 1)
        return own, own_grad, scores, d_probs

    def rest(head, given):
        own, own_grad, scores, d_probs = given
        lanes, place, turned = head_lanes(head)
        delta = column_sum(products[head][turned])
        probs = jnp.exp2(scores - log_total[0, head : head + 1, :])
        d_scores = (probs * (d_probs - delta)).astype(jnp.bfloat16)
        return (
            dot(pair[:, lanes].T[turned], d_scores),
            dot(d_scores, own),
            dot(probs.astype(jnp.bfloat16), own_grad),
        )

    parts = in_turn(HEADS, first, rest)
    for head in range(0, HEADS, 2):
        lanes = head_lanes(head)[0]
        one, two = parts[head : head + 2]
        turned = jnp.concatenate([one[0], two[0]], axis=0).T * HD ** (-0.5)
        if second:
            turned = rotate_lanes(turned + before[:, lanes], cosine[...], -sine[...])
        d_query[:, lanes] = turned.astype(d_query.dtype)
        d_keys[:, lanes] = ((one[1] + two[1]) * (1.0 / LOG2E)).astype(jnp.bfloat16)
        d_values[:, lanes] = (one[2] + two[2]).astype(jnp.bfloat16)


def attend_back(query, pair, grad, attended, log_total, before=None, after=(), free=()):
    rows, width = query.shape
    lanes = HEADS * HD
    steps = width // lanes
    block = columns(rows, lanes)
    second = before is not None
    extra = list(before) if second else []
    extra_specs = [block, full((rows, 128)), full((rows, 128))] if second else []
    return kernel_call(
        functools.partial(attend_back_body, second),
        steps,
        [
            block,
            columns(rows, 2 * lanes),
            block,
            block,
            pl.BlockSpec((1, HEADS, rows), lambda step: (step, 0, 0)),
        ]
        + extra_specs
        + [pl.BlockSpec(memory_space=pl.ANY)] * len(after),
        [block, block, block],
        [shaped((rows, width), jnp.bfloat16)] * 3
        if second
        else [
            far((rows, width), jnp.float32),
            far((rows, width), jnp.bfloat16),
            far((rows, width), jnp.bfloat16),
        ],
        [],
        28,
    )(query, pair, grad, attended, log_total, *extra, *after, free=free)


def block_body(
    own_down, attend_steps, hidden_steps,
    core, normed1, query_weight, cosine, sine, mods, up_bias, down_bias, *refs,
):
    pairs_far, refs = refs[: 2 * attend_steps], refs[2 * attend_steps :]
    (
        tokens_far, cotangent_far, out_far, up_far, down_far,
        query, attended, log_total, mixed, d_middle, d_attended, up_grad,
        down_keep, down_send, bias_grad, sums, peer_far,
        tokens, cotangent, out_weight, up_weight, down_weight, arrived,
        own_pairs, peer_pairs, pair_arrived, left,
        all_attended, normed, d_ffn, branch, middle, forward, back,
    ) = refs
    step = pl.program_id(0)
    tile = up_bias.shape[1]
    lanes = 2 * HEADS * HD
    own_arrivals, peer_arrivals, departures = [], [], []
    for index in range(attend_steps):
        own_arrivals.append(
            pltpu.make_async_copy(
                pairs_far[index], own_pairs.at[index], pair_arrived.at[0, index]
            )
        )
        peer_arrivals.append(
            pltpu.make_async_copy(
                pairs_far[attend_steps + index], peer_pairs.at[index], pair_arrived.at[1, index]
            )
        )
        departures.append(
            pltpu.make_async_copy(
                peer_pairs.at[index],
                peer_far.at[:, pl.ds(index * lanes, lanes)],
                left.at[index],
            )
        )
    arrivals = [
        pltpu.make_async_copy(source, target, arrived.at[index])
        for index, (source, target) in enumerate(
            (
                (tokens_far, tokens),
                (cotangent_far, cotangent),
                (out_far, out_weight),
                (up_far, up_weight),
                (down_far, down_weight),
            )
        )
    ]

    @pl.when(step == 0)
    def _():
        for index in range(attend_steps):
            own_arrivals[index].start()
            peer_arrivals[index].start()
        for arrival in arrivals:
            arrival.start()

    for index in range(attend_steps):

        @pl.when(step == index)
        def _(index=index):
            own_arrivals[index].wait()
            peer_arrivals[index].wait()
            departures[index].start()

    @pl.when(step < attend_steps)
    def _():
        value = rotate_lanes(dot(normed1[...], query_weight[...]), cosine[...], sine[...])
        query[...] = (value * (LOG2E * HD ** (-0.5))).astype(jnp.bfloat16)
        pairs = own_pairs.at[step], peer_pairs.at[step]
        in_range, found = attend_heads(query, *pairs, log_total, False)
        attended[...] = found

        @pl.when(jnp.logical_not(in_range))
        def _():
            attended[...] = attend_heads(query, *pairs, log_total, True)[1]

        for index in range(attend_steps):

            @pl.when(step == index)
            def _(index=index):
                heads = HEADS * HD
                all_attended[:, index * heads : (index + 1) * heads] = attended[...]

    @pl.when(step == attend_steps)
    def _():
        for arrival in arrivals:
            arrival.wait()
        for departure in departures:
            departure.wait()
        turned = dot(all_attended[...], out_weight[...])
        branch[...] = turned.astype(jnp.bfloat16)
        value = tokens[...].astype(jnp.float32) + row(mods, GATE1) * turned
        middle[...] = value
        hat, _ = normalized(value)
        value = hat * row(mods, GAIN2) * (1.0 + row(mods, SCALE2)) + row(mods, SHIFT2)
        normed[...] = value.astype(jnp.bfloat16)
        low = (row(mods, GATE2) * cotangent[...].astype(jnp.float32)).astype(jnp.bfloat16)
        d_ffn[...] = low
        sums[4:5, :] = column_sum(low.astype(jnp.float32))
        forward[...] = jnp.zeros_like(forward)
        back[...] = jnp.zeros_like(back)

    @pl.when((step >= attend_steps) & (step < attend_steps + hidden_steps))
    def _():
        place = pl.ds(pl.multiple_of((step - attend_steps) * tile, tile), tile)
        pre = dot(normed[...], up_weight[:, place]) + up_bias[...]
        d_activated = dot(d_ffn[...], down_weight[place, :], 1, 1)
        root = 0.7978845608028654
        square = pre * pre
        bent = jnp.tanh(root * pre * (1.0 + 0.044715 * square))
        half = 0.5 + 0.5 * bent
        slope = half + (0.5 * root) * pre * (1.0 - bent * bent) * (1.0 + 0.134145 * square)
        low = (pre * half).astype(jnp.bfloat16)
        d_pre = d_activated * slope
        d_low = d_pre.astype(jnp.bfloat16)
        bias_grad[...] = column_sum(d_pre)
        down_grad = dot(low, d_ffn[...], 0, 0).astype(jnp.bfloat16)
        store_split(down_grad, core, own_down, down_keep, down_send)
        up_grad[...] = dot(normed[...], d_low, 0, 0).astype(jnp.bfloat16)
        forward[...] += dot(low, down_weight[place, :])
        back[...] += dot(d_low, up_weight[:, place], 1, 1)

    @pl.when(step == attend_steps + hidden_steps)
    def _():
        grad = cotangent[...].astype(jnp.float32)
        held = middle[...]
        hat, inverse = normalized(held)
        factor = row(mods, GAIN2) * (1.0 + row(mods, SCALE2))
        value = back[...]
        d_value = grad + norm_back(value, hat, inverse, factor)
        d_middle[...] = d_value
        d_branch = (row(mods, GATE1) * d_value).astype(jnp.bfloat16)
        d_attended[...] = dot(d_branch, out_weight[...], 1, 1).astype(jnp.bfloat16)
        up_grad[...] = dot(all_attended[...], d_branch, 0, 0).astype(jnp.bfloat16)
        ffn = forward[...] + down_bias[...]
        mixed[...] = (held + row(mods, GATE2) * ffn).astype(jnp.bfloat16)
        sums[0:1, :] = column_sum(value)
        sums[1:2, :] = column_sum(value * hat)
        sums[2:3, :] = column_sum(d_value * branch[...].astype(jnp.float32))
        sums[3:4, :] = column_sum(grad * ffn)
        sums[5:8, :] = jnp.zeros_like(sums[5:8, :])


def split_rows(rows):
    own = rows // lax.axis_size("dp")
    return own if own % 16 == 0 else rows // 2


def block_layer(
    core, normed1, qkv_weight, cosine, sine, mods, up_bias, down_bias, own, peer,
    tokens, cotangent, out_weight, up_weight, down_weight,
):
    rows, width = tokens.shape
    hidden = up_weight.shape[1]
    tile = width
    lanes = HEADS * HD
    attend_steps = width // lanes
    hidden_steps = hidden // tile
    own_down = hidden // lax.axis_size("dp")
    if own_down % 16 > 0:
        own_down = tile // 2

    def heads(first=0):
        return pl.BlockSpec(
            (rows, lanes), lambda step: (0, jnp.minimum(step, attend_steps - 1) + first)
        )

    def tiles(step):
        return jnp.clip(step - attend_steps, 0, hidden_steps - 1)

    def up_tiles(step):
        return jnp.clip(step - attend_steps, 0, hidden_steps)

    block = full((rows, width))
    far_spec = pl.BlockSpec(memory_space=pl.ANY)
    low = jnp.bfloat16
    up_spec = pl.BlockSpec((width, tile), lambda step: (0, up_tiles(step)))
    down_spec = pl.BlockSpec((tile // 2, width), lambda step: (tiles(step), 0))
    return kernel_call(
        functools.partial(block_body, own_down, attend_steps, hidden_steps),
        attend_steps + hidden_steps + 1,
        [
            scalar_spec(),
            block,
            pl.BlockSpec((width, lanes), lambda step: (0, jnp.minimum(step, attend_steps - 1))),
            full((rows, 128)),
            full((rows, 128)),
            full((16, width)),
            pl.BlockSpec((1, tile), lambda step: (0, tiles(step))),
            full((1, width)),
        ]
        + [far_spec] * (2 * attend_steps + 5),
        [
            heads(),
            heads(),
            pl.BlockSpec(
                (1, HEADS, rows), lambda step: (jnp.minimum(step, attend_steps - 1), 0, 0)
            ),
            block,
            block,
            block,
            up_spec,
            down_spec,
            down_spec,
            pl.BlockSpec((1, tile), lambda step: (0, tiles(step))),
            full((8, width)),
            far_spec,
        ],
        [
            far((rows, width), low),
            far((rows, width), low),
            far((attend_steps, HEADS, rows), jnp.float32),
            far((rows, width), low),
            far((rows, width), jnp.float32),
            far((rows, width), low),
            far((width, hidden + width), low),
            far((hidden // 2, width), low),
            far((hidden // 2, width), low),
            far((1, hidden), jnp.float32),
            far((8, width), jnp.float32),
            far((rows, 2 * width), low),
        ],
        [
            pltpu.VMEM((rows, width), low),
            pltpu.VMEM((rows, width), low),
            pltpu.VMEM((width, width), low),
            pltpu.VMEM((width, hidden), low),
            pltpu.VMEM((hidden, width), low),
            pltpu.SemaphoreType.DMA((5,)),
            pltpu.VMEM((attend_steps, rows, 2 * lanes), low),
            pltpu.VMEM((attend_steps, rows, 2 * lanes), low),
            pltpu.SemaphoreType.DMA((2, attend_steps)),
            pltpu.SemaphoreType.DMA((attend_steps,)),
            pltpu.VMEM((rows, width), low),
            pltpu.VMEM((rows, width), low),
            pltpu.VMEM((rows, width), low),
            pltpu.VMEM((rows, width), low),
            pltpu.VMEM((rows, width), jnp.float32),
            pltpu.VMEM((rows, width), jnp.float32),
            pltpu.VMEM((rows, width), jnp.float32),
        ],
        58,
    )(
        core, normed1, qkv_weight, cosine, sine, mods, up_bias, down_bias, *own, *peer,
        tokens, cotangent, out_weight, up_weight, down_weight,
        free=(*peer, cotangent, tokens),
    )


def projected_back_body(
    own, core, d_query, d_keys, d_values, peer_keys, peer_values, normed, cosine, sine,
    d_projected, *parts,
):
    lanes = HEADS * HD
    keys = d_keys[...].astype(jnp.float32) + peer_keys[...].astype(jnp.float32)
    keys = rotate_lanes(keys, cosine[...], -sine[...]).astype(jnp.bfloat16)
    values = d_values[...].astype(jnp.float32) + peer_values[...].astype(jnp.float32)
    low = jnp.concatenate([d_query[...], keys, values.astype(jnp.bfloat16)], axis=1)
    d_projected[...] = low
    grad = dot(normed[...], low, 0, 0).astype(jnp.bfloat16)
    for index in range(3):
        third = grad[:, index * lanes : (index + 1) * lanes]
        store_split(third, core, own, parts[2 * index], parts[2 * index + 1])


def projected_back(core, d_query, d_keys, d_values, peer_keys, peer_values, normed, cosine, sine):
    rows, width = normed.shape
    lanes = HEADS * HD
    block = columns(rows, lanes)
    return kernel_call(
        functools.partial(projected_back_body, split_rows(width)),
        width // lanes,
        [
            scalar_spec(),
            block,
            block,
            block,
            block,
            block,
            full((rows, width)),
            full((rows, 128)),
            full((rows, 128)),
        ],
        [columns(rows, 3 * lanes)] + [columns(width // 2, lanes)] * 6,
        [far((rows, 3 * width), jnp.bfloat16)] + [far((width // 2, width), jnp.bfloat16)] * 6,
        [],
        32,
    )(
        core, d_query, d_keys, d_values, peer_keys, peer_values, normed, cosine, sine,
        free=(d_query, d_keys, d_values, peer_keys, peer_values),
    )


def tokens_back_body(
    d_projected, weight1, weight2, weight3, tokens, d_middle, mods, sums, bias_grad, *refs
):
    out, small, total = refs[-3:]
    step = pl.program_id(0)
    width = tokens.shape[1]
    lanes = HEADS * HD
    part = sum(
        dot(d_projected[:, index * lanes : (index + 1) * lanes], weight[...], 1, 1)
        for index, weight in enumerate((weight1, weight2, weight3))
    )

    @pl.when(step == 0)
    def _():
        total[...] = part

    @pl.when(step > 0)
    def _():
        total[...] += part

    @pl.when(step == pl.num_programs(0) - 1)
    def _():
        back = total[...]
        hat, inverse = normalized(tokens[...].astype(jnp.float32))
        scale1 = 1.0 + row(mods, SCALE1)
        gain1 = row(mods, GAIN1)
        out[...] = (d_middle[...] + norm_back(back, hat, inverse, gain1 * scale1)).astype(
            jnp.bfloat16
        )
        hat_sum1 = column_sum(back * hat)
        hat_sum2 = row(sums, 1)
        rows = [
            column_sum(back),
            hat_sum1 * gain1,
            row(sums, 2),
            row(sums, 0),
            hat_sum2 * row(mods, GAIN2),
            row(sums, 3),
            row(mods, COND) * 0.5,
            jnp.zeros_like(hat_sum1),
            hat_sum1 * scale1,
            hat_sum2 * (1.0 + row(mods, SCALE2)),
            row(sums, 4),
        ]
        for index in range(bias_grad.shape[1] // width):
            rows.append(bias_grad[:, index * width : (index + 1) * width])
        for index, value in enumerate(rows):
            small[index : index + 1, :] = value
        small[len(rows) :, :] = jnp.zeros_like(small[len(rows) :, :])


def tokens_back(d_projected, weight, tokens, d_middle, mods, sums, bias_grad, after):
    rows, width = tokens.shape
    lanes = HEADS * HD
    steps = width // lanes
    block = full((rows, width))
    return kernel_call(
        tokens_back_body,
        steps,
        [
            columns(rows, 3 * lanes),
            columns(width, lanes),
            columns(width, lanes, steps),
            columns(width, lanes, 2 * steps),
            block,
            block,
            full((16, width)),
            full((8, width)),
            full(bias_grad.shape),
        ]
        + [pl.BlockSpec(memory_space=pl.ANY)] * len(after),
        [block, full((16, width))],
        [far((rows, width), jnp.bfloat16), far((16, width), jnp.float32)],
        [pltpu.VMEM((rows, width), jnp.float32)],
        36,
    )(d_projected, weight, weight, weight, tokens, d_middle, mods, sums, bias_grad, *after)


def finish_body(
    places, here, there, embedded, ada_weight,
    first_gain, second_gain, up_bias, down_bias, ada_bias, ada_grad, cond_grad, every,
):
    width = here.shape[1]
    sequences = (here.shape[0] - 8) // 8
    own_columns = ada_grad.shape[1]
    sums = here[8 * sequences :, :] + there[8 * sequences :, :]
    first_gain[...] = sums[0, :]
    second_gain[...] = sums[1, :]
    down_bias[...] = sums[2, :]
    for index in range(up_bias.shape[0] // width):
        up_bias[index * width : (index + 1) * width] = sums[3 + index, :]
    total = here[:8, :] + there[:8, :]
    for index in range(1, sequences):
        rows = slice(8 * index, 8 * index + 8)
        total = total + here[rows, :] + there[rows, :]
    conds = []
    for side, block in enumerate((here, there)):
        for index in range(sequences):
            conds.append(block[8 * index + 6 : 8 * index + 7, : embedded.shape[1]])
            for part in range(6):
                every[
                    side * sequences + index : side * sequences + index + 1,
                    part * width : (part + 1) * width,
                ] = block[8 * index + part : 8 * index + part + 1, :]
    for part in range(6):
        ada_bias[part * width : (part + 1) * width] = total[part, :]
    turned = pltpu.roll(every[...], places[0], 1)[:, : -(-own_columns // 128) * 128]
    grad = lax.dot_general(
        jnp.concatenate(conds, axis=0),
        turned,
        (((0,), (0,)), ((), ())),
        precision=highest,
        preferred_element_type=jnp.float32,
    )
    ada_grad[...] = grad[:, :own_columns]
    own = jnp.where(places[1] == 1, here[:8, :], there[:8, :])
    products = ada_weight[:, :width].astype(jnp.float32) * own[0:1, :]
    for part in range(1, 6):
        columns_here = ada_weight[:, part * width : (part + 1) * width].astype(jnp.float32)
        products = products + columns_here * own[part : part + 1, :]
    summed = jnp.sum(products, axis=1, keepdims=True)
    turned_sum = jnp.broadcast_to(summed, (summed.shape[0], 128)).T[0:1, :]
    value = embedded[...]
    sigmoid = 1.0 / (1.0 + jnp.exp(-value))
    cond_grad[...] = turned_sum * (sigmoid * (1.0 + value * (1.0 - sigmoid)))


def finish(here, there, embedded, ada_weight, hidden):
    width = here.shape[1]
    sequences = (here.shape[0] - 8) // 8
    dp_size, dp_rank = lax.axis_size("dp"), lax.axis_index("dp")
    all_columns = ada_weight.shape[1]
    own_columns = all_columns // dp_size
    turn = (all_columns - dp_rank * own_columns) % all_columns
    same = (lax.axis_index("seq") == dp_rank % 2).astype(jnp.int32)
    kind = jnp.float32
    whole = pl.BlockSpec(memory_space=pltpu.VMEM)
    return pl.pallas_call(
        finish_body,
        in_specs=[scalar_spec(), whole, whole, whole, whole],
        out_specs=[whole] * 7,
        out_shape=[
            shaped((width,), kind),
            shaped((width,), kind),
            shaped((hidden,), kind),
            shaped((width,), kind),
            shaped((all_columns,), kind),
            shaped((ada_weight.shape[0], own_columns), kind),
            shaped((1, ada_weight.shape[0]), kind),
        ],
        scratch_shapes=[pltpu.VMEM((2 * sequences, all_columns), kind)],
        compiler_params=pltpu.CompilerParams(vmem_limit_bytes=24 * 1024 * 1024),
        cost_estimate=pl.CostEstimate(flops=1, bytes_accessed=1, transcendentals=0),
    )(jnp.stack([turn, same]), here, there, embedded, ada_weight)


def swap_halves(block):
    count = lax.axis_size("dp") * lax.axis_size("seq")
    target = {1: 2, 2: 1}
    perm = [(i, i - i % 4 + target.get(i % 4, i % 4)) for i in range(count)]
    return lax.ppermute(block, ("dp", "seq"), perm)


def swap_bit(block, bit):
    return lax.ppermute(block, "dp", [(i, i ^ bit) for i in range(lax.axis_size("dp"))])


def swap_cores(block):
    return swap_bit(block, 1)


def swap_seq(block):
    return lax.ppermute(block, "seq", [(0, 1), (1, 0)])


def dp_bits():
    bits, bit = [], 1
    while bit < lax.axis_size("dp"):
        bits.append(bit)
        bit *= 2
    return bits


def pick(block, axis, index):
    return lax.dynamic_index_in_dim(block, index, axis, keepdims=False)


class Flow:
    def __init__(self, got, kept, lanes=None):
        self.got, self.kept = got, kept
        self.lanes = lanes or (0, kept.shape[2])
        self.count, self.rest = kept.shape[:2]
        self.width = self.lanes[1] - self.lanes[0]


def stage_body(jobs, counts, mine, *refs):
    inputs = refs[: counts[0]]
    outputs = refs[counts[0] + counts[1] :]

    def terms(sources, place):
        for one, two, lanes, rows in sources:
            total = inputs[one][place + (slice(None), lanes)].astype(jnp.float32)
            total = total + inputs[two][place + (slice(None), lanes)].astype(jnp.float32)
            total = total.astype(jnp.bfloat16)
            height = total.shape[-2]
            for start in range(0, height, rows):
                yield total if height == rows else total[..., start : start + rows, :]

    def store(out, place, values):
        at = 0
        for value in values:
            width = value.shape[-1]
            out[place + (slice(None), slice(at, at + width))] = value
            at += width

    def run(index, kind, stride, sources, target):
        if kind == "sum":
            store(outputs[target], (slice(None),), terms(sources, (slice(None),)))
            return

        def part(out, which):
            if kind == "half":
                halves = []
                for one, two, lanes, rows in sources:
                    middle = (lanes.start + lanes.stop) // 2
                    first, second = slice(lanes.start, middle), slice(middle, lanes.stop)
                    halves.append((one, two, second if which else first, rows))
                store(out, (slice(None),), terms(halves, (slice(None),)))
                return
            for block in range(out.shape[0]):
                high, low = divmod(block, stride)
                place = (2 * high + which) * stride + low
                store(out, (block,), terms(sources, (place,)))

        for which in range(2):

            @pl.when(mine[index] == which)
            def _(which=which):
                part(outputs[target + 1], which)
                part(outputs[target], 1 - which)

    for index, (kind, stride, sources, target, whole) in enumerate(jobs):
        if whole:

            @pl.when(pl.program_id(0) == 0)
            def _(args=(index, kind, stride, sources, target)):
                run(*args)

        else:
            run(index, kind, stride, sources, target)


def small_body(first, one, two, out):
    rows = one.shape[0] - 8

    @pl.when(pl.program_id(0) == 0)
    def _():
        if first:
            out[...] = one[...] + two[...]
        else:
            out[:rows, :] = one[:rows, :]
            out[rows : 2 * rows, :] = two[:rows, :]
            out[2 * rows :, :] = one[rows:, :] + two[rows:, :]


def stage(steps, jobs, after=(), small=None, free=(), relay=None):
    seq_rank, dp_rank = lax.axis_index("seq"), lax.axis_index("dp")
    inputs, in_specs, specs, out_specs, out_shape, mine = [], [], [], [], [], []
    free = [*free] + [flow.got for flows, _ in jobs for flow in flows]

    def spec(shape, whole):
        if whole:
            return full(shape)
        return pl.BlockSpec((shape[0] // steps,) + shape[1:], lambda at: (at, 0, 0))

    def place_of(array, whole):
        for index, other in enumerate(inputs):
            if other is array:
                return index
        inputs.append(array)
        in_specs.append(spec(array.shape, whole))
        return len(inputs) - 1

    for flows, step in jobs:
        bit, stride = step if isinstance(step, tuple) else (None, 1)
        rest, count = flows[0].rest, flows[0].count
        smallest = 1 if bit is None else 2 * stride
        whole = count % steps > 0 or (count // steps) % smallest > 0
        sources = [
            (place_of(flow.got, whole), place_of(flow.kept, whole), slice(*flow.lanes), rest)
            for flow in flows
        ]
        width = sum(flow.width * flow.rest // rest for flow in flows)
        if bit is not None:
            shape = (count // 2, rest, width)
            mine.append((dp_rank // bit) % 2)
        else:
            shape = (count, rest, width // 2 if step == "half" else width)
            mine.append(seq_rank)
        specs.append((step if bit is None else "bit", stride, sources, len(out_shape), whole))
        results = 1 if step == "sum" else 2
        out_shape += [far(shape, jnp.bfloat16)] * results
        out_specs += [spec(shape, whole)] * results
    counts = (len(inputs), len(after))
    extra = []
    if small is not None:
        got, kept, first = small
        extra = [kept, got]
        rows = kept.shape[0] if first else 2 * kept.shape[0] - 8
        out_shape.append(far((rows, kept.shape[1]), jnp.float32))
        out_specs.append(full((rows, kept.shape[1])))

    if relay is not None:
        extra.append(relay)
        out_shape.append(far(relay.shape, relay.dtype))
        out_specs.append(full(relay.shape))

    def body(mine, *refs):
        if relay is not None:
            place = sum(counts) + len(extra) - 1
            refs[-1][...] = refs[place][...]
            refs = (*refs[:place], *refs[place + 1 : -1])
        if small is None:
            stage_body(specs, counts, mine, *refs)
            return
        main, ends = refs[: sum(counts)], refs[sum(counts) :]
        small_body(first, ends[0], ends[1], ends[-1])
        stage_body(specs, counts, mine, *main, *ends[2:-1])

    results = kernel_call(
        body,
        steps,
        [scalar_spec()]
        + in_specs
        + [pl.BlockSpec(memory_space=pl.ANY)] * len(after)
        + [full(array.shape) for array in extra],
        out_specs,
        out_shape,
        [],
        40,
    )(jnp.stack(mine), *inputs, *after, *extra, free=(*free, *extra[1:2]))
    new = []
    for (flows, step), (_, _, _, target, _) in zip(jobs, specs):
        sent = results[target]
        got = swap_seq(sent) if isinstance(step, str) else swap_bit(sent, step[0])
        new.append(Flow(got, sent if step == "sum" else results[target + 1]))
    if small is not None:
        new.append(results[-1 if relay is None else -2])
    if relay is not None:
        new.append(results[-1])
    return new, results[0]


def from_tiles(kept, sent, tile):
    rows, width = 2 * kept.shape[0], kept.shape[1]
    core = lax.axis_index("dp") % 2
    first = jnp.where(core == 0, kept, sent).reshape(rows // tile, 1, tile // 2, width)
    second = jnp.where(core == 0, sent, kept).reshape(rows // tile, 1, tile // 2, width)
    return jnp.concatenate([first, second], axis=1).reshape(rows, width)


def plain_sum(kept, sent, tile):
    matrix = from_tiles(kept, sent, tile)
    return lax.psum(
        lax.psum_scatter(matrix, "dp", scatter_dimension=0, tiled=True).astype(jnp.float32), "seq"
    )


def joined(flow, widths):
    block, got = flow.kept[0].astype(jnp.float32), flow.got[0].astype(jnp.float32)
    here = lax.axis_index("seq") == 0
    first, second = jnp.where(here, block, got), jnp.where(here, got, block)
    parts, at = [], 0
    for width in widths:
        parts.append(
            jnp.concatenate([first[:, at : at + width], second[:, at : at + width]], axis=1)
        )
        at += width
    return parts


def per_device(
    tokens,
    cotangent,
    time_index,
    step_table,
    first_gain,
    attn_qkv,
    attn_out,
    second_gain,
    mlp_up,
    up_bias,
    mlp_down,
    down_bias,
    ada_weight,
    ada_bias,
):
    rows, width = tokens.shape[1:]
    dp_rank = lax.axis_index("dp")
    core = dp_rank % 2
    own_embedded = lax.dynamic_slice_in_dim(step_table, time_index[0], 1, axis=0)
    positions = core * rows + jnp.arange(rows, dtype=jnp.int32)
    cosine, sine = tables(positions)
    tokens = swap_halves(tokens[0])
    time_index = swap_halves(time_index)
    cotangent = swap_halves(cotangent[0])
    cond = jax.nn.silu(lax.dynamic_slice_in_dim(step_table, time_index[0], 1, axis=0))
    ada_float = ada_weight.astype(jnp.float32)
    modulation = jnp.dot(cond, ada_float, precision=highest) + ada_bias.astype(jnp.float32)
    gain1 = first_gain.astype(jnp.float32)
    gain2 = second_gain.astype(jnp.float32)
    cond_row = jnp.pad(cond, ((0, 0), (0, width - cond.shape[1])))
    mods = jnp.concatenate(
        [modulation.reshape(6, width), gain1[None], gain2[None], cond_row, jnp.zeros((7, width))]
    )
    normed1, own_pair, *own_parts = project_key_value(tokens, mods, attn_qkv, cosine, sine)
    peer_parts = [swap_cores(part) for part in own_parts]
    core_ref = core[None]
    (
        query, attended, log_total, mixed, d_middle, d_attended, up_grad,
        down_keep, down_send, up_bias_grad, sums2, peer_pair,
    ) = block_layer(
        core_ref, normed1, attn_qkv, cosine, sine, mods,
        up_bias.astype(jnp.float32)[None], down_bias.astype(jnp.float32)[None],
        own_parts, peer_parts,
        tokens, cotangent, attn_out, mlp_up, mlp_down,
    )
    hidden = mlp_up.shape[1]
    dp_size = lax.axis_size("dp")
    bits = dp_bits()
    by_steps = split_rows(width) == width // dp_size and len(bits) == 4
    up_rows = lax.psum_scatter(up_grad, "dp", scatter_dimension=0, tiled=True)
    up_got = swap_seq(up_rows)

    def blocks(part):
        return part.reshape(dp_size // 2, -1, part.shape[1])

    if by_steps:
        down = Flow(swap_cores(blocks(down_send)), blocks(down_keep))
    d_query, away_keys, away_values = attend_back(query, peer_pair, d_attended, attended, log_total)
    after = ()
    if by_steps:
        (down,), sent = stage(4, [([down], "half")], (away_keys,))
        after = (sent,)
    peer_keys, peer_values = swap_cores(away_keys), swap_cores(away_values)
    d_query, d_keys, d_values = attend_back(
        query, own_pair, d_attended, attended, log_total, (d_query, cosine, sine), after
    )
    d_projected, *qkv_parts = projected_back(
        core_ref, d_query, d_keys, d_values, peer_keys, peer_values, normed1, cosine, sine
    )
    sent = ()
    if by_steps:
        late = [
            Flow(swap_cores(blocks(send)), blocks(keep))
            for keep, send in zip(qkv_parts[::2], qkv_parts[1::2])
        ]
        (late,), *sent = stage(4, [(late, "half")])
        (down, mixed), *sent = stage(4, [([down], (bits[1], 1))], sent, relay=mixed)
    tokens_grad, small = tokens_back(
        d_projected, attn_qkv, tokens, d_middle, mods, sums2, up_bias_grad, sent
    )
    small = small + swap_cores(small)
    moves = [functools.partial(swap_bit, bit=bit) for bit in bits[2:] + bits[1:2]] + [swap_seq]

    def doubled(small, got):
        return jnp.concatenate([small[:-8], got[:-8], small[-8:] + got[-8:]], axis=0)

    if by_steps:

        def next_stage(jobs, count, moves_before, after=(), relay=None):
            nonlocal small, sent
            for _ in range(moves_before):
                small = doubled(small, moves.pop(0)(small))
            extra = (moves.pop(0)(small), small, False) if len(moves) > 0 else None
            flows, *sent = stage(count, jobs, (*sent, *after), extra, after, relay)
            if extra is not None:
                small = flows.pop(len(jobs))
            return flows

        down, late, tokens_grad = next_stage(
            [([down], (bits[2], 1)), ([late], (bits[1], 1))], 2, 0, (), tokens_grad
        )
        down, late = next_stage([([down], (bits[3], 1)), ([late], (bits[2], 1))], 2, 0)
        down, late = next_stage([([down], "sum"), ([late], (bits[3], 1))], 1, 0, (up_got,))
        last = moves.pop(0)(small)
        (late,) = next_stage([([late], "sum")], 1, 0)
        (
            first_gain_grad, second_gain_grad, all_up_bias_grad, down_bias_grad, ada_bias_grad,
            ada_weight_grad, cond_grad,
        ) = finish(small, last, own_embedded, ada_weight, hidden)
        (down_rows,) = joined(down, (width // 2,))
        qkv_rows = jnp.concatenate(joined(late, (width // 2,) * 3), axis=1)
    else:
        for move in moves:
            small = doubled(small, move(small))
        down_rows = plain_sum(down_keep, down_send, width)
        qkv_rows = jnp.concatenate(
            [
                plain_sum(keep, send, width)
                for keep, send in zip(qkv_parts[::2], qkv_parts[1::2])
            ],
            axis=1,
        )
        per_sequence, sums = small[:-8].reshape(-1, 8, width), small[-8:]
        d_mod_all = per_sequence[:, :6].reshape(per_sequence.shape[0], 6 * width)
        cond_all = per_sequence[:, 6, : cond.shape[1]]
        own_columns = d_mod_all.shape[1] // dp_size
        mine = lax.dynamic_slice_in_dim(d_mod_all, dp_rank * own_columns, own_columns, axis=1)
        ada_weight_grad = lax.dot_general(
            cond_all, mine, (((0,), (0,)), ((), ())), precision=highest
        )
        other = d_mod_all.shape[0] // 2
        d_mod_own = jnp.where(
            lax.axis_index("seq") == core, d_mod_all[:1], d_mod_all[other : other + 1]
        )
        _, silu_back = jax.vjp(jax.nn.silu, own_embedded)
        (cond_grad,) = silu_back(jnp.dot(d_mod_own, ada_float.T, precision=highest))
        first_gain_grad, second_gain_grad, down_bias_grad = sums[0], sums[1], sums[2]
        all_up_bias_grad = sums[3:7].reshape(-1)
        ada_bias_grad = jnp.sum(d_mod_all, axis=0)
    up_rows = up_rows.astype(jnp.float32) + up_got.astype(jnp.float32)
    return (
        swap_halves(mixed)[None],
        swap_halves(tokens_grad).astype(jnp.float32)[None],
        cond_grad,
        first_gain_grad,
        qkv_rows,
        up_rows[:, hidden:],
        second_gain_grad,
        up_rows[:, :hidden],
        all_up_bias_grad,
        down_rows,
        down_bias_grad,
        ada_weight_grad,
        ada_bias_grad,
    )


def solution(mesh):
    placed = (
        P("dp", "seq", None),
        P("dp", "seq", None),
        P("dp"),
        P(),
        P(),
        P(),
        P(),
        P(),
        P(),
        P(),
        P(),
        P(),
        P(),
        P(),
    )
    return jax.shard_map(
        per_device,
        mesh=mesh,
        in_specs=placed,
        out_specs=(
            P("dp", "seq", None),
            P("dp", "seq", None),
            P("dp", None),
            P(),
            P("dp", None),
            P("dp", None),
            P(),
            P("dp", None),
            P(),
            P("dp", None),
            P(),
            P(None, "dp"),
            P(),
        ),
        check_vma=False,
    )
```

```python
import functools

import jax
import jax.numpy as jnp
from jax import lax
from jax.experimental import pallas as pl
from jax.experimental.pallas import tpu as pltpu
from jax.sharding import PartitionSpec as P

HD = 64
LOG2E = 1.4426950408889634


highest = lax.Precision.HIGHEST


def tables(positions):
    half_dim = HD // 2
    frequency = jnp.exp(
        -jnp.log(10000.0) * (2.0 * jnp.arange(half_dim, dtype=jnp.float32) / HD)
    )
    angles = positions.astype(jnp.float32)[:, None] * frequency[None, :]
    cosine, sine = jnp.cos(angles), jnp.sin(angles)
    return (
        jnp.concatenate([cosine] * 4, axis=1),
        jnp.concatenate([-sine, sine, -sine, sine], axis=1),
    )


def full(shape):
    return pl.BlockSpec(shape, lambda step: (0,) * len(shape))


def columns(rows, width, first=0):
    return pl.BlockSpec((rows, width), lambda step: (0, step + first))


def shaped(shape, kind):
    return jax.ShapeDtypeStruct(shape, kind)


def far(shape, kind):
    return pltpu.HBM(shape, kind)


def store_split(low, core, own, keep, send):
    pairs = low.shape[0] // (2 * own)

    def store(kept):
        for pair in range(pairs):
            rows = slice(pair * own, (pair + 1) * own)
            for parity, target in ((kept, keep), (1 - kept, send)):
                start = (2 * pair + parity) * own
                target[rows, :] = low[start : start + own, :]

    @pl.when(core[0] == 0)
    def _():
        store(0)

    @pl.when(core[0] == 1)
    def _():
        store(1)


def zero_shape():
    return jax.ShapeDtypeStruct((1, 1), jnp.float32)


def scalar_spec():
    return pl.BlockSpec(memory_space=pltpu.SMEM)


def kernel_call(body, steps, in_specs, out_specs, out_shape, scratch, grant):
    call = pl.pallas_call(
        body,
        grid=(steps,),
        in_specs=in_specs,
        out_specs=out_specs,
        out_shape=out_shape,
        scratch_shapes=scratch,
        compiler_params=pltpu.CompilerParams(
            dimension_semantics=("arbitrary",), vmem_limit_bytes=grant * 1024 * 1024
        ),
        cost_estimate=pl.CostEstimate(flops=1, bytes_accessed=1, transcendentals=0),
    )

    def run(*args, free=()):
        placed = []
        for arg in args:
            if arg.size > 4096 and not any(arg is other for other in free):
                arg = pltpu.with_memory_space_constraint(arg, pltpu.HBM)
            placed.append(arg)
        return call(*placed)

    return run


def dot(left, right, left_axis=1, right_axis=0):
    return lax.dot_general(
        left,
        right,
        (((left_axis,), (right_axis,)), ((), ())),
        preferred_element_type=jnp.float32,
    )


def normalized(inputs):
    center = inputs - jnp.mean(inputs, axis=-1, keepdims=True)
    inverse = lax.rsqrt(jnp.mean(center * center, axis=-1, keepdims=True) + 1e-05)
    return center * inverse, inverse


def norm_back(back, hat, inverse, factor):
    scaled = back * factor
    return inverse * (
        scaled
        - jnp.mean(scaled, axis=-1, keepdims=True)
        - hat * jnp.mean(scaled * hat, axis=-1, keepdims=True)
    )


def column_sum(values):
    return jnp.sum(values, axis=0, keepdims=True)


SHIFT1, SCALE1, GATE1, SHIFT2, SCALE2, GATE2, GAIN1, GAIN2, COND = range(9)


def row(ref, index):
    return ref[index : index + 1, :]


def rotate_lanes(values, cosine, sine):
    lane = lax.broadcasted_iota(jnp.int32, cosine.shape, 1)
    lower = (lane % HD) < HD // 2
    parts = []
    for start in range(0, values.shape[1], 128):
        part = values[:, start : start + 128]
        other = jnp.where(lower, pltpu.roll(part, 128 - HD // 2, 1), pltpu.roll(part, HD // 2, 1))
        parts.append(part * cosine + other * sine)
    return jnp.concatenate(parts, axis=1)


HEADS = 4


def key_value_body(
    tokens, mods, key_weight, value_weight, cosine, sine, normed, every, *parts
):
    step = pl.program_id(0)

    @pl.when(step == 0)
    def _():
        hat, _ = normalized(tokens[...].astype(jnp.float32))
        value = hat * row(mods, GAIN1) * (1.0 + row(mods, SCALE1)) + row(mods, SHIFT1)
        normed[...] = value.astype(jnp.bfloat16)

    keys = rotate_lanes(dot(normed[...], key_weight[...]), cosine[...], sine[...])
    values = dot(normed[...], value_weight[...])
    both = jnp.concatenate([keys, values], axis=1).astype(jnp.bfloat16)
    every[...] = both
    for index, part in enumerate(parts):

        @pl.when(step == index)
        def _(part=part):
            part[...] = both


def project_key_value(tokens, mods, weight, cosine, sine):
    rows, width = tokens.shape
    lanes = HEADS * HD
    steps = width // lanes
    low = jnp.bfloat16
    return kernel_call(
        key_value_body,
        steps,
        [
            full((rows, width)),
            full((16, width)),
            columns(width, lanes, steps),
            columns(width, lanes, 2 * steps),
            full((rows, 128)),
            full((rows, 128)),
        ],
        [full((rows, width)), columns(rows, 2 * lanes)] + [full((rows, 2 * lanes))] * steps,
        [far((rows, width), low), far((rows, 2 * width), low)]
        + [far((rows, 2 * lanes), low)] * steps,
        [],
        24,
    )(tokens, mods, weight, weight, cosine, sine, free=(tokens,))


def head_mask(shape, head):
    lane = lax.broadcasted_iota(jnp.int32, shape, 1)
    return jnp.where(lane // HD == head, 1.0, 0.0).astype(jnp.bfloat16)


def head_lanes(head):
    pair, place = divmod(head, 2)
    return slice(pair * 128, (pair + 1) * 128), place, slice(place * HD, (place + 1) * HD)


def value_lanes(lanes):
    return slice(HEADS * HD + lanes.start, HEADS * HD + lanes.stop)


def in_turn(count, first, rest):
    results = []
    ahead = first(0)
    for index in range(count):
        now = ahead
        if index + 1 < count:
            ahead = first(index + 1)
        results.append(rest(index, now))
    return results


def attend_heads(query, pair1, pair2, log_total, shifted):
    rows = query.shape[0]

    def first(head):
        lanes, place, _ = head_lanes(head)
        own = query[:, lanes] * head_mask((rows, 128), place)
        return dot(pair1[:, lanes], own, 1, 1), dot(pair2[:, lanes], own, 1, 1)

    def rest(head, scores):
        lanes, place, turned = head_lanes(head)
        scores1, scores2 = scores
        if shifted:
            top = jnp.maximum(
                jnp.max(scores1, axis=0, keepdims=True), jnp.max(scores2, axis=0, keepdims=True)
            )
            scores1, scores2 = scores1 - top, scores2 - top
        exps1, exps2 = jnp.exp2(scores1), jnp.exp2(scores2)
        total = column_sum(exps1) + column_sum(exps2)
        lanes = value_lanes(lanes)
        mixed = dot(pair1[:, lanes].T[turned], exps1.astype(jnp.bfloat16)) + dot(
            pair2[:, lanes].T[turned], exps2.astype(jnp.bfloat16)
        )
        log_sum = jnp.log2(total)
        log_total[0, head : head + 1, :] = top + log_sum if shifted else log_sum
        return mixed * (1.0 / total)

    parts = in_turn(HEADS, first, rest)
    logs = log_total[0]
    in_range = (jnp.min(logs) > -60.0) & (jnp.max(logs) < 60.0)
    return in_range, jnp.concatenate(
        [
            jnp.concatenate(parts[head : head + 2], axis=0).T.astype(jnp.bfloat16)
            for head in range(0, HEADS, 2)
        ],
        axis=1,
    )


def attend_back_body(second, query, pair, grad, attended, log_total, *refs):
    if second:
        before, cosine, sine = refs[:3]
    d_query, d_keys, d_values = refs[-3:]
    rows = query.shape[0]
    products = {}

    def first(head):
        lanes, place, _ = head_lanes(head)
        if place == 0:
            product = grad[:, lanes].astype(jnp.float32) * attended[:, lanes].astype(jnp.float32)
            products[head] = products[head + 1] = product.T
        own = query[:, lanes] * head_mask((rows, 128), place)
        own_grad = grad[:, lanes] * head_mask((rows, 128), place)
        scores = dot(pair[:, lanes], own, 1, 1)
        d_probs = dot(pair[:, value_lanes(lanes)], own_grad, 1, 1)
        return own, own_grad, scores, d_probs

    def rest(head, given):
        own, own_grad, scores, d_probs = given
        lanes, place, turned = head_lanes(head)
        delta = column_sum(products[head][turned])
        probs = jnp.exp2(scores - log_total[0, head : head + 1, :])
        d_scores = (probs * (d_probs - delta)).astype(jnp.bfloat16)
        return (
            dot(pair[:, lanes].T[turned], d_scores),
            dot(d_scores, own),
            dot(probs.astype(jnp.bfloat16), own_grad),
        )

    parts = in_turn(HEADS, first, rest)
    for head in range(0, HEADS, 2):
        lanes = head_lanes(head)[0]
        one, two = parts[head : head + 2]
        turned = jnp.concatenate([one[0], two[0]], axis=0).T * HD ** (-0.5)
        if second:
            turned = rotate_lanes(turned + before[:, lanes], cosine[...], -sine[...])
        d_query[:, lanes] = turned.astype(d_query.dtype)
        d_keys[:, lanes] = ((one[1] + two[1]) * (1.0 / LOG2E)).astype(jnp.bfloat16)
        d_values[:, lanes] = (one[2] + two[2]).astype(jnp.bfloat16)


def attend_back(query, pair, grad, attended, log_total, before=None, after=(), free=()):
    rows, width = query.shape
    lanes = HEADS * HD
    steps = width // lanes
    block = columns(rows, lanes)
    second = before is not None
    extra = list(before) if second else []
    extra_specs = [block, full((rows, 128)), full((rows, 128))] if second else []
    return kernel_call(
        functools.partial(attend_back_body, second),
        steps,
        [
            block,
            columns(rows, 2 * lanes),
            block,
            block,
            pl.BlockSpec((1, HEADS, rows), lambda step: (step, 0, 0)),
        ]
        + extra_specs
        + [pl.BlockSpec(memory_space=pl.ANY)] * len(after),
        [block, block, block],
        [shaped((rows, width), jnp.bfloat16)] * 3
        if second
        else [
            far((rows, width), jnp.float32),
            far((rows, width), jnp.bfloat16),
            far((rows, width), jnp.bfloat16),
        ],
        [],
        28,
    )(query, pair, grad, attended, log_total, *extra, *after, free=free)


def block_body(
    own_down, attend_steps, hidden_steps,
    core, normed1, query_weight, cosine, sine, mods, up_bias, down_bias, *refs,
):
    pairs_far, refs = refs[: 2 * attend_steps], refs[2 * attend_steps :]
    (
        tokens_far, cotangent_far, out_far, up_far, down_far,
        query, attended, log_total, mixed, d_middle, d_attended, up_grad,
        down_keep, down_send, bias_grad, sums, peer_far,
        tokens, cotangent, out_weight, up_weight, down_weight, arrived,
        own_pairs, peer_pairs, pair_arrived, left,
        all_attended, normed, d_ffn, branch, middle, forward, back,
    ) = refs
    step = pl.program_id(0)
    tile = up_bias.shape[1]
    lanes = 2 * HEADS * HD
    own_arrivals, peer_arrivals, departures = [], [], []
    for index in range(attend_steps):
        own_arrivals.append(
            pltpu.make_async_copy(
                pairs_far[index], own_pairs.at[index], pair_arrived.at[0, index]
            )
        )
        peer_arrivals.append(
            pltpu.make_async_copy(
                pairs_far[attend_steps + index], peer_pairs.at[index], pair_arrived.at[1, index]
            )
        )
        departures.append(
            pltpu.make_async_copy(
                peer_pairs.at[index],
                peer_far.at[:, pl.ds(index * lanes, lanes)],
                left.at[index],
            )
        )
    arrivals = [
        pltpu.make_async_copy(source, target, arrived.at[index])
        for index, (source, target) in enumerate(
            (
                (tokens_far, tokens),
                (cotangent_far, cotangent),
                (out_far, out_weight),
                (up_far, up_weight),
                (down_far, down_weight),
            )
        )
    ]

    @pl.when(step == 0)
    def _():
        for index in range(attend_steps):
            own_arrivals[index].start()
            peer_arrivals[index].start()
        for arrival in arrivals:
            arrival.start()

    @pl.when(step < attend_steps)
    def _():
        value = rotate_lanes(dot(normed1[...], query_weight[...]), cosine[...], sine[...])
        query[...] = (value * (LOG2E * HD ** (-0.5))).astype(jnp.bfloat16)
        for index in range(attend_steps):

            @pl.when(step == index)
            def _(index=index):
                own_arrivals[index].wait()
                peer_arrivals[index].wait()
                departures[index].start()

        pairs = own_pairs.at[step], peer_pairs.at[step]
        in_range, found = attend_heads(query, *pairs, log_total, False)
        attended[...] = found

        @pl.when(jnp.logical_not(in_range))
        def _():
            attended[...] = attend_heads(query, *pairs, log_total, True)[1]

        for index in range(attend_steps):

            @pl.when(step == index)
            def _(index=index):
                heads = HEADS * HD
                all_attended[:, index * heads : (index + 1) * heads] = attended[...]

    @pl.when(step == attend_steps)
    def _():
        for arrival in arrivals:
            arrival.wait()
        for departure in departures:
            departure.wait()
        turned = dot(all_attended[...], out_weight[...])
        branch[...] = turned.astype(jnp.bfloat16)
        value = tokens[...].astype(jnp.float32) + row(mods, GATE1) * turned
        middle[...] = value
        hat, _ = normalized(value)
        value = hat * row(mods, GAIN2) * (1.0 + row(mods, SCALE2)) + row(mods, SHIFT2)
        normed[...] = value.astype(jnp.bfloat16)
        low = (row(mods, GATE2) * cotangent[...].astype(jnp.float32)).astype(jnp.bfloat16)
        d_ffn[...] = low
        sums[4:5, :] = column_sum(low.astype(jnp.float32))
        forward[...] = jnp.zeros_like(forward)
        back[...] = jnp.zeros_like(back)

    @pl.when((step >= attend_steps) & (step < attend_steps + hidden_steps))
    def _():
        place = pl.ds(pl.multiple_of((step - attend_steps) * tile, tile), tile)
        pre = dot(normed[...], up_weight[:, place]) + up_bias[...]
        d_activated = dot(d_ffn[...], down_weight[place, :], 1, 1)
        root = 0.7978845608028654
        square = pre * pre
        bent = jnp.tanh(root * pre * (1.0 + 0.044715 * square))
        half = 0.5 + 0.5 * bent
        slope = half + (0.5 * root) * pre * (1.0 - bent * bent) * (1.0 + 0.134145 * square)
        low = (pre * half).astype(jnp.bfloat16)
        d_pre = d_activated * slope
        d_low = d_pre.astype(jnp.bfloat16)
        bias_grad[...] = column_sum(d_pre)
        down_grad = dot(low, d_ffn[...], 0, 0).astype(jnp.bfloat16)
        store_split(down_grad, core, own_down, down_keep, down_send)
        up_grad[...] = dot(normed[...], d_low, 0, 0).astype(jnp.bfloat16)
        forward[...] += dot(low, down_weight[place, :])
        back[...] += dot(d_low, up_weight[:, place], 1, 1)

    @pl.when(step == attend_steps + hidden_steps)
    def _():
        grad = cotangent[...].astype(jnp.float32)
        held = middle[...]
        hat, inverse = normalized(held)
        factor = row(mods, GAIN2) * (1.0 + row(mods, SCALE2))
        value = back[...]
        d_value = grad + norm_back(value, hat, inverse, factor)
        d_middle[...] = d_value
        d_branch = (row(mods, GATE1) * d_value).astype(jnp.bfloat16)
        d_attended[...] = dot(d_branch, out_weight[...], 1, 1).astype(jnp.bfloat16)
        up_grad[...] = dot(all_attended[...], d_branch, 0, 0).astype(jnp.bfloat16)
        ffn = forward[...] + down_bias[...]
        mixed[...] = (held + row(mods, GATE2) * ffn).astype(jnp.bfloat16)
        sums[0:1, :] = column_sum(value)
        sums[1:2, :] = column_sum(value * hat)
        sums[2:3, :] = column_sum(d_value * branch[...].astype(jnp.float32))
        sums[3:4, :] = column_sum(grad * ffn)
        sums[5:8, :] = jnp.zeros_like(sums[5:8, :])


def split_rows(rows):
    own = rows // lax.axis_size("dp")
    return own if own % 16 == 0 else rows // 2


def block_layer(
    core, normed1, qkv_weight, cosine, sine, mods, up_bias, down_bias, own, peer,
    tokens, cotangent, out_weight, up_weight, down_weight,
):
    rows, width = tokens.shape
    hidden = up_weight.shape[1]
    tile = width
    lanes = HEADS * HD
    attend_steps = width // lanes
    hidden_steps = hidden // tile
    own_down = hidden // lax.axis_size("dp")
    if own_down % 16 > 0:
        own_down = tile // 2

    def heads(first=0):
        return pl.BlockSpec(
            (rows, lanes), lambda step: (0, jnp.minimum(step, attend_steps - 1) + first)
        )

    def tiles(step):
        return jnp.clip(step - attend_steps, 0, hidden_steps - 1)

    def up_tiles(step):
        return jnp.clip(step - attend_steps, 0, hidden_steps)

    block = full((rows, width))
    far_spec = pl.BlockSpec(memory_space=pl.ANY)
    low = jnp.bfloat16
    up_spec = pl.BlockSpec((width, tile), lambda step: (0, up_tiles(step)))
    down_spec = pl.BlockSpec((tile // 2, width), lambda step: (tiles(step), 0))
    return kernel_call(
        functools.partial(block_body, own_down, attend_steps, hidden_steps),
        attend_steps + hidden_steps + 1,
        [
            scalar_spec(),
            block,
            pl.BlockSpec((width, lanes), lambda step: (0, jnp.minimum(step, attend_steps - 1))),
            full((rows, 128)),
            full((rows, 128)),
            full((16, width)),
            pl.BlockSpec((1, tile), lambda step: (0, tiles(step))),
            full((1, width)),
        ]
        + [far_spec] * (2 * attend_steps + 5),
        [
            heads(),
            heads(),
            pl.BlockSpec(
                (1, HEADS, rows), lambda step: (jnp.minimum(step, attend_steps - 1), 0, 0)
            ),
            block,
            block,
            block,
            up_spec,
            down_spec,
            down_spec,
            pl.BlockSpec((1, tile), lambda step: (0, tiles(step))),
            full((8, width)),
            far_spec,
        ],
        [
            far((rows, width), low),
            far((rows, width), low),
            far((attend_steps, HEADS, rows), jnp.float32),
            far((rows, width), low),
            far((rows, width), jnp.float32),
            far((rows, width), low),
            far((width, hidden + width), low),
            far((hidden // 2, width), low),
            far((hidden // 2, width), low),
            far((1, hidden), jnp.float32),
            far((8, width), jnp.float32),
            far((rows, 2 * width), low),
        ],
        [
            pltpu.VMEM((rows, width), low),
            pltpu.VMEM((rows, width), low),
            pltpu.VMEM((width, width), low),
            pltpu.VMEM((width, hidden), low),
            pltpu.VMEM((hidden, width), low),
            pltpu.SemaphoreType.DMA((5,)),
            pltpu.VMEM((attend_steps, rows, 2 * lanes), low),
            pltpu.VMEM((attend_steps, rows, 2 * lanes), low),
            pltpu.SemaphoreType.DMA((2, attend_steps)),
            pltpu.SemaphoreType.DMA((attend_steps,)),
            pltpu.VMEM((rows, width), low),
            pltpu.VMEM((rows, width), low),
            pltpu.VMEM((rows, width), low),
            pltpu.VMEM((rows, width), low),
            pltpu.VMEM((rows, width), jnp.float32),
            pltpu.VMEM((rows, width), jnp.float32),
            pltpu.VMEM((rows, width), jnp.float32),
        ],
        58,
    )(
        core, normed1, qkv_weight, cosine, sine, mods, up_bias, down_bias, *own, *peer,
        tokens, cotangent, out_weight, up_weight, down_weight,
        free=(*peer, cotangent, tokens),
    )


def projected_back_body(
    own, core, d_query, d_keys, d_values, peer_keys, peer_values, normed, cosine, sine,
    d_projected, *parts,
):
    lanes = HEADS * HD
    keys = d_keys[...].astype(jnp.float32) + peer_keys[...].astype(jnp.float32)
    keys = rotate_lanes(keys, cosine[...], -sine[...]).astype(jnp.bfloat16)
    values = d_values[...].astype(jnp.float32) + peer_values[...].astype(jnp.float32)
    low = jnp.concatenate([d_query[...], keys, values.astype(jnp.bfloat16)], axis=1)
    d_projected[...] = low
    grad = dot(normed[...], low, 0, 0).astype(jnp.bfloat16)
    for index in range(3):
        third = grad[:, index * lanes : (index + 1) * lanes]
        store_split(third, core, own, parts[2 * index], parts[2 * index + 1])


def projected_back(core, d_query, d_keys, d_values, peer_keys, peer_values, normed, cosine, sine):
    rows, width = normed.shape
    lanes = HEADS * HD
    block = columns(rows, lanes)
    return kernel_call(
        functools.partial(projected_back_body, split_rows(width)),
        width // lanes,
        [
            scalar_spec(),
            block,
            block,
            block,
            block,
            block,
            full((rows, width)),
            full((rows, 128)),
            full((rows, 128)),
        ],
        [columns(rows, 3 * lanes)] + [columns(width // 2, lanes)] * 6,
        [far((rows, 3 * width), jnp.bfloat16)] + [far((width // 2, width), jnp.bfloat16)] * 6,
        [],
        32,
    )(
        core, d_query, d_keys, d_values, peer_keys, peer_values, normed, cosine, sine,
        free=(d_query, d_keys, d_values, peer_keys, peer_values),
    )


def tokens_back_body(
    d_projected, weight1, weight2, weight3, tokens, d_middle, mods, sums, bias_grad, *refs
):
    out, small, total = refs[-3:]
    step = pl.program_id(0)
    width = tokens.shape[1]
    lanes = HEADS * HD
    part = sum(
        dot(d_projected[:, index * lanes : (index + 1) * lanes], weight[...], 1, 1)
        for index, weight in enumerate((weight1, weight2, weight3))
    )

    @pl.when(step == 0)
    def _():
        total[...] = part

    @pl.when(step > 0)
    def _():
        total[...] += part

    @pl.when(step == pl.num_programs(0) - 1)
    def _():
        back = total[...]
        hat, inverse = normalized(tokens[...].astype(jnp.float32))
        scale1 = 1.0 + row(mods, SCALE1)
        gain1 = row(mods, GAIN1)
        out[...] = (d_middle[...] + norm_back(back, hat, inverse, gain1 * scale1)).astype(
            jnp.bfloat16
        )
        hat_sum1 = column_sum(back * hat)
        hat_sum2 = row(sums, 1)
        rows = [
            column_sum(back),
            hat_sum1 * gain1,
            row(sums, 2),
            row(sums, 0),
            hat_sum2 * row(mods, GAIN2),
            row(sums, 3),
            row(mods, COND) * 0.5,
            jnp.zeros_like(hat_sum1),
            hat_sum1 * scale1,
            hat_sum2 * (1.0 + row(mods, SCALE2)),
            row(sums, 4),
        ]
        for index in range(bias_grad.shape[1] // width):
            rows.append(bias_grad[:, index * width : (index + 1) * width])
        for index, value in enumerate(rows):
            small[index : index + 1, :] = value
        small[len(rows) :, :] = jnp.zeros_like(small[len(rows) :, :])


def tokens_back(d_projected, weight, tokens, d_middle, mods, sums, bias_grad, after):
    rows, width = tokens.shape
    lanes = HEADS * HD
    steps = width // lanes
    block = full((rows, width))
    return kernel_call(
        tokens_back_body,
        steps,
        [
            columns(rows, 3 * lanes),
            columns(width, lanes),
            columns(width, lanes, steps),
            columns(width, lanes, 2 * steps),
            block,
            block,
            full((16, width)),
            full((8, width)),
            full(bias_grad.shape),
        ]
        + [pl.BlockSpec(memory_space=pl.ANY)] * len(after),
        [block, full((16, width))],
        [far((rows, width), jnp.bfloat16), far((16, width), jnp.float32)],
        [pltpu.VMEM((rows, width), jnp.float32)],
        36,
    )(d_projected, weight, weight, weight, tokens, d_middle, mods, sums, bias_grad, *after)


def finish_body(
    places, here, there, embedded, ada_weight,
    first_gain, second_gain, up_bias, down_bias, ada_bias, ada_grad, cond_grad, every,
):
    width = here.shape[1]
    sequences = (here.shape[0] - 8) // 8
    own_columns = ada_grad.shape[0]
    sums = here[8 * sequences :, :] + there[8 * sequences :, :]
    first_gain[...] = sums[0, :]
    second_gain[...] = sums[1, :]
    down_bias[...] = sums[2, :]
    for index in range(up_bias.shape[0] // width):
        up_bias[index * width : (index + 1) * width] = sums[3 + index, :]
    total = here[:8, :] + there[:8, :]
    for index in range(1, sequences):
        rows = slice(8 * index, 8 * index + 8)
        total = total + here[rows, :] + there[rows, :]
    conds = []
    for side, block in enumerate((here, there)):
        for index in range(sequences):
            conds.append(block[8 * index + 6 : 8 * index + 7, : embedded.shape[1]])
            for part in range(6):
                every[
                    side * sequences + index : side * sequences + index + 1,
                    part * width : (part + 1) * width,
                ] = block[8 * index + part : 8 * index + part + 1, :]
    for part in range(6):
        ada_bias[part * width : (part + 1) * width] = total[part, :]
    turned = pltpu.roll(every[...], places[0], 1)[:, : -(-own_columns // 128) * 128]
    grad = lax.dot_general(
        turned,
        jnp.concatenate(conds, axis=0),
        (((0,), (0,)), ((), ())),
        precision=highest,
        preferred_element_type=jnp.float32,
    )
    ada_grad[...] = grad[:own_columns, :]
    own = jnp.where(places[1] == 1, here[:8, :], there[:8, :])
    products = ada_weight[:, :width].astype(jnp.float32) * own[0:1, :]
    for part in range(1, 6):
        columns_here = ada_weight[:, part * width : (part + 1) * width].astype(jnp.float32)
        products = products + columns_here * own[part : part + 1, :]
    summed = jnp.sum(products, axis=1, keepdims=True)
    turned_sum = jnp.broadcast_to(summed, (summed.shape[0], 128)).T[0:1, :]
    value = embedded[...]
    sigmoid = 1.0 / (1.0 + jnp.exp(-value))
    cond_grad[...] = turned_sum * (sigmoid * (1.0 + value * (1.0 - sigmoid)))


def finish(here, there, embedded, ada_weight, hidden):
    width = here.shape[1]
    sequences = (here.shape[0] - 8) // 8
    dp_size, dp_rank = lax.axis_size("dp"), lax.axis_index("dp")
    all_columns = ada_weight.shape[1]
    own_columns = all_columns // dp_size
    turn = (all_columns - dp_rank * own_columns) % all_columns
    same = (lax.axis_index("seq") == dp_rank % 2).astype(jnp.int32)
    kind = jnp.float32
    whole = pl.BlockSpec(memory_space=pltpu.VMEM)
    return pl.pallas_call(
        finish_body,
        in_specs=[scalar_spec(), whole, whole, whole, whole],
        out_specs=[whole] * 7,
        out_shape=[
            shaped((width,), kind),
            shaped((width,), kind),
            shaped((hidden,), kind),
            shaped((width,), kind),
            shaped((all_columns,), kind),
            shaped((own_columns, ada_weight.shape[0]), kind),
            shaped((1, ada_weight.shape[0]), kind),
        ],
        scratch_shapes=[pltpu.VMEM((2 * sequences, all_columns), kind)],
        compiler_params=pltpu.CompilerParams(vmem_limit_bytes=24 * 1024 * 1024),
        cost_estimate=pl.CostEstimate(flops=1, bytes_accessed=1, transcendentals=0),
    )(jnp.stack([turn, same]), here, there, embedded, ada_weight)


def swap_halves(block):
    count = lax.axis_size("dp") * lax.axis_size("seq")
    target = {1: 2, 2: 1}
    perm = [(i, i - i % 4 + target.get(i % 4, i % 4)) for i in range(count)]
    return lax.ppermute(block, ("dp", "seq"), perm)


def swap_bit(block, bit):
    return lax.ppermute(block, "dp", [(i, i ^ bit) for i in range(lax.axis_size("dp"))])


def swap_cores(block):
    return swap_bit(block, 1)


def swap_seq(block):
    return lax.ppermute(block, "seq", [(0, 1), (1, 0)])


def dp_bits():
    bits, bit = [], 1
    while bit < lax.axis_size("dp"):
        bits.append(bit)
        bit *= 2
    return bits


def pick(block, axis, index):
    return lax.dynamic_index_in_dim(block, index, axis, keepdims=False)


class Flow:
    def __init__(self, got, kept, lanes=None):
        self.got, self.kept = got, kept
        self.lanes = lanes or (0, kept.shape[2])
        self.count, self.rest = kept.shape[:2]
        self.width = self.lanes[1] - self.lanes[0]


def stage_body(jobs, counts, mine, *refs):
    inputs = refs[: counts[0]]
    outputs = refs[counts[0] + counts[1] :]

    def terms(sources, place):
        for one, two, lanes, rows in sources:
            total = inputs[one][place + (slice(None), lanes)].astype(jnp.float32)
            total = total + inputs[two][place + (slice(None), lanes)].astype(jnp.float32)
            total = total.astype(jnp.bfloat16)
            height = total.shape[-2]
            for start in range(0, height, rows):
                yield total if height == rows else total[..., start : start + rows, :]

    def store(out, place, values):
        at = 0
        for value in values:
            width = value.shape[-1]
            out[place + (slice(None), slice(at, at + width))] = value
            at += width

    def run(index, kind, stride, sources, target):
        if kind == "sum":
            store(outputs[target], (slice(None),), terms(sources, (slice(None),)))
            return

        def part(out, which):
            if kind == "half":
                halves = []
                for one, two, lanes, rows in sources:
                    middle = (lanes.start + lanes.stop) // 2
                    first, second = slice(lanes.start, middle), slice(middle, lanes.stop)
                    halves.append((one, two, second if which else first, rows))
                store(out, (slice(None),), terms(halves, (slice(None),)))
                return
            for block in range(out.shape[0]):
                high, low = divmod(block, stride)
                place = (2 * high + which) * stride + low
                store(out, (block,), terms(sources, (place,)))

        for which in range(2):

            @pl.when(mine[index] == which)
            def _(which=which):
                part(outputs[target + 1], which)
                part(outputs[target], 1 - which)

    for index, (kind, stride, sources, target, whole) in enumerate(jobs):
        if whole:

            @pl.when(pl.program_id(0) == 0)
            def _(args=(index, kind, stride, sources, target)):
                run(*args)

        else:
            run(index, kind, stride, sources, target)


def small_body(first, one, two, out):
    rows = one.shape[0] - 8

    @pl.when(pl.program_id(0) == 0)
    def _():
        if first:
            out[...] = one[...] + two[...]
        else:
            out[:rows, :] = one[:rows, :]
            out[rows : 2 * rows, :] = two[:rows, :]
            out[2 * rows :, :] = one[rows:, :] + two[rows:, :]


def stage(steps, jobs, after=(), small=None, free=(), relay=None):
    seq_rank, dp_rank = lax.axis_index("seq"), lax.axis_index("dp")
    inputs, in_specs, specs, out_specs, out_shape, mine = [], [], [], [], [], []
    free = [*free] + [flow.got for flows, _ in jobs for flow in flows]

    def spec(shape, whole):
        if whole:
            return full(shape)
        return pl.BlockSpec((shape[0] // steps,) + shape[1:], lambda at: (at, 0, 0))

    def place_of(array, whole):
        for index, other in enumerate(inputs):
            if other is array:
                return index
        inputs.append(array)
        in_specs.append(spec(array.shape, whole))
        return len(inputs) - 1

    for flows, step in jobs:
        bit, stride = step if isinstance(step, tuple) else (None, 1)
        rest, count = flows[0].rest, flows[0].count
        smallest = 1 if bit is None else 2 * stride
        whole = count % steps > 0 or (count // steps) % smallest > 0
        sources = [
            (place_of(flow.got, whole), place_of(flow.kept, whole), slice(*flow.lanes), rest)
            for flow in flows
        ]
        width = sum(flow.width * flow.rest // rest for flow in flows)
        if bit is not None:
            shape = (count // 2, rest, width)
            mine.append((dp_rank // bit) % 2)
        else:
            shape = (count, rest, width // 2 if step == "half" else width)
            mine.append(seq_rank)
        specs.append((step if bit is None else "bit", stride, sources, len(out_shape), whole))
        results = 1 if step == "sum" else 2
        out_shape += [far(shape, jnp.bfloat16)] * results
        out_specs += [spec(shape, whole)] * results
    counts = (len(inputs), len(after))
    extra = []
    if small is not None:
        got, kept, first = small
        extra = [kept, got]
        rows = kept.shape[0] if first else 2 * kept.shape[0] - 8
        out_shape.append(far((rows, kept.shape[1]), jnp.float32))
        out_specs.append(full((rows, kept.shape[1])))

    if relay is not None:
        extra.append(relay)
        out_shape.append(far(relay.shape, relay.dtype))
        out_specs.append(full(relay.shape))

    def body(mine, *refs):
        if relay is not None:
            place = sum(counts) + len(extra) - 1
            refs[-1][...] = refs[place][...]
            refs = (*refs[:place], *refs[place + 1 : -1])
        if small is None:
            stage_body(specs, counts, mine, *refs)
            return
        main, ends = refs[: sum(counts)], refs[sum(counts) :]
        small_body(first, ends[0], ends[1], ends[-1])
        stage_body(specs, counts, mine, *main, *ends[2:-1])

    results = kernel_call(
        body,
        steps,
        [scalar_spec()]
        + in_specs
        + [pl.BlockSpec(memory_space=pl.ANY)] * len(after)
        + [full(array.shape) for array in extra],
        out_specs,
        out_shape,
        [],
        40,
    )(jnp.stack(mine), *inputs, *after, *extra, free=(*free, *extra[1:2]))
    new = []
    for (flows, step), (_, _, _, target, _) in zip(jobs, specs):
        sent = results[target]
        got = swap_seq(sent) if isinstance(step, str) else swap_bit(sent, step[0])
        new.append(Flow(got, sent if step == "sum" else results[target + 1]))
    if small is not None:
        new.append(results[-1 if relay is None else -2])
    if relay is not None:
        new.append(results[-1])
    return new, results[0]


def from_tiles(kept, sent, tile):
    rows, width = 2 * kept.shape[0], kept.shape[1]
    core = lax.axis_index("dp") % 2
    first = jnp.where(core == 0, kept, sent).reshape(rows // tile, 1, tile // 2, width)
    second = jnp.where(core == 0, sent, kept).reshape(rows // tile, 1, tile // 2, width)
    return jnp.concatenate([first, second], axis=1).reshape(rows, width)


def plain_sum(kept, sent, tile):
    matrix = from_tiles(kept, sent, tile)
    return lax.psum(
        lax.psum_scatter(matrix, "dp", scatter_dimension=0, tiled=True).astype(jnp.float32), "seq"
    )


def joined(flow, widths):
    block, got = flow.kept[0].astype(jnp.float32), flow.got[0].astype(jnp.float32)
    here = lax.axis_index("seq") == 0
    first, second = jnp.where(here, block, got), jnp.where(here, got, block)
    parts, at = [], 0
    for width in widths:
        parts.append(
            jnp.concatenate([first[:, at : at + width], second[:, at : at + width]], axis=1)
        )
        at += width
    return parts


def per_device(
    tokens,
    cotangent,
    time_index,
    step_table,
    first_gain,
    attn_qkv,
    attn_out,
    second_gain,
    mlp_up,
    up_bias,
    mlp_down,
    down_bias,
    ada_weight,
    ada_bias,
):
    rows, width = tokens.shape[1:]
    dp_rank = lax.axis_index("dp")
    core = dp_rank % 2
    own_embedded = lax.dynamic_slice_in_dim(step_table, time_index[0], 1, axis=0)
    positions = core * rows + jnp.arange(rows, dtype=jnp.int32)
    cosine, sine = tables(positions)
    tokens = swap_halves(tokens[0])
    time_index = swap_halves(time_index)
    cotangent = swap_halves(cotangent[0])
    cond = jax.nn.silu(lax.dynamic_slice_in_dim(step_table, time_index[0], 1, axis=0))
    ada_float = ada_weight.astype(jnp.float32)
    modulation = jnp.dot(cond, ada_float, precision=highest) + ada_bias.astype(jnp.float32)
    gain1 = first_gain.astype(jnp.float32)
    gain2 = second_gain.astype(jnp.float32)
    cond_row = jnp.pad(cond, ((0, 0), (0, width - cond.shape[1])))
    mods = jnp.concatenate(
        [modulation.reshape(6, width), gain1[None], gain2[None], cond_row, jnp.zeros((7, width))]
    )
    normed1, own_pair, *own_parts = project_key_value(tokens, mods, attn_qkv, cosine, sine)
    peer_parts = [swap_cores(part) for part in own_parts]
    core_ref = core[None]
    (
        query, attended, log_total, mixed, d_middle, d_attended, up_grad,
        down_keep, down_send, up_bias_grad, sums2, peer_pair,
    ) = block_layer(
        core_ref, normed1, attn_qkv, cosine, sine, mods,
        up_bias.astype(jnp.float32)[None], down_bias.astype(jnp.float32)[None],
        own_parts, peer_parts,
        tokens, cotangent, attn_out, mlp_up, mlp_down,
    )
    hidden = mlp_up.shape[1]
    dp_size = lax.axis_size("dp")
    bits = dp_bits()
    by_steps = split_rows(width) == width // dp_size and len(bits) == 4
    up_rows = lax.psum_scatter(up_grad, "dp", scatter_dimension=0, tiled=True)
    up_got = swap_seq(up_rows)

    def blocks(part):
        return part.reshape(dp_size // 2, -1, part.shape[1])

    if by_steps:
        down = Flow(swap_cores(blocks(down_send)), blocks(down_keep))
    d_query, away_keys, away_values = attend_back(query, peer_pair, d_attended, attended, log_total)
    after = ()
    if by_steps:
        (down,), sent = stage(2, [([down], "half")], (away_keys,))
        after = (sent,)
    peer_keys, peer_values = swap_cores(away_keys), swap_cores(away_values)
    d_query, d_keys, d_values = attend_back(
        query, own_pair, d_attended, attended, log_total, (d_query, cosine, sine), after
    )
    d_projected, *qkv_parts = projected_back(
        core_ref, d_query, d_keys, d_values, peer_keys, peer_values, normed1, cosine, sine
    )
    sent = ()
    if by_steps:
        late = [
            Flow(swap_cores(blocks(send)), blocks(keep))
            for keep, send in zip(qkv_parts[::2], qkv_parts[1::2])
        ]
        (late,), *sent = stage(2, [(late, "half")])
        (down, mixed), *sent = stage(2, [([down], (bits[1], 1))], sent, relay=mixed)
    tokens_grad, small = tokens_back(
        d_projected, attn_qkv, tokens, d_middle, mods, sums2, up_bias_grad, sent
    )
    small = small + swap_cores(small)
    moves = [functools.partial(swap_bit, bit=bit) for bit in bits[2:] + bits[1:2]] + [swap_seq]

    def doubled(small, got):
        return jnp.concatenate([small[:-8], got[:-8], small[-8:] + got[-8:]], axis=0)

    if by_steps:

        def next_stage(jobs, count, moves_before, after=(), relay=None):
            nonlocal small, sent
            for _ in range(moves_before):
                small = doubled(small, moves.pop(0)(small))
            extra = (moves.pop(0)(small), small, False) if len(moves) > 0 else None
            flows, *sent = stage(count, jobs, (*sent, *after), extra, after, relay)
            if extra is not None:
                small = flows.pop(len(jobs))
            return flows

        down, late, tokens_grad = next_stage(
            [([down], (bits[2], 1)), ([late], (bits[1], 1))], 2, 0, (), tokens_grad
        )
        down, late = next_stage([([down], (bits[3], 1)), ([late], (bits[2], 1))], 2, 0)
        down, late = next_stage([([down], "sum"), ([late], (bits[3], 1))], 1, 0, (up_got,))
        last = moves.pop(0)(small)
        (late,) = next_stage([([late], "sum")], 1, 0)
        (
            first_gain_grad, second_gain_grad, all_up_bias_grad, down_bias_grad, ada_bias_grad,
            ada_turned, cond_grad,
        ) = finish(small, last, own_embedded, ada_weight, hidden)
        ada_weight_grad = ada_turned.T
        (down_rows,) = joined(down, (width // 2,))
        qkv_rows = jnp.concatenate(joined(late, (width // 2,) * 3), axis=1)
    else:
        for move in moves:
            small = doubled(small, move(small))
        down_rows = plain_sum(down_keep, down_send, width)
        qkv_rows = jnp.concatenate(
            [
                plain_sum(keep, send, width)
                for keep, send in zip(qkv_parts[::2], qkv_parts[1::2])
            ],
            axis=1,
        )
        per_sequence, sums = small[:-8].reshape(-1, 8, width), small[-8:]
        d_mod_all = per_sequence[:, :6].reshape(per_sequence.shape[0], 6 * width)
        cond_all = per_sequence[:, 6, : cond.shape[1]]
        own_columns = d_mod_all.shape[1] // dp_size
        mine = lax.dynamic_slice_in_dim(d_mod_all, dp_rank * own_columns, own_columns, axis=1)
        ada_weight_grad = lax.dot_general(
            cond_all, mine, (((0,), (0,)), ((), ())), precision=highest
        )
        other = d_mod_all.shape[0] // 2
        d_mod_own = jnp.where(
            lax.axis_index("seq") == core, d_mod_all[:1], d_mod_all[other : other + 1]
        )
        _, silu_back = jax.vjp(jax.nn.silu, own_embedded)
        (cond_grad,) = silu_back(jnp.dot(d_mod_own, ada_float.T, precision=highest))
        first_gain_grad, second_gain_grad, down_bias_grad = sums[0], sums[1], sums[2]
        all_up_bias_grad = sums[3:7].reshape(-1)
        ada_bias_grad = jnp.sum(d_mod_all, axis=0)
    up_rows = up_rows.astype(jnp.float32) + up_got.astype(jnp.float32)
    return (
        swap_halves(mixed)[None],
        swap_halves(tokens_grad).astype(jnp.float32)[None],
        cond_grad,
        first_gain_grad,
        qkv_rows,
        up_rows[:, hidden:],
        second_gain_grad,
        up_rows[:, :hidden],
        all_up_bias_grad,
        down_rows,
        down_bias_grad,
        ada_weight_grad,
        ada_bias_grad,
    )


def solution(mesh):
    placed = (
        P("dp", "seq", None),
        P("dp", "seq", None),
        P("dp"),
        P(),
        P(),
        P(),
        P(),
        P(),
        P(),
        P(),
        P(),
        P(),
        P(),
        P(),
    )
    return jax.shard_map(
        per_device,
        mesh=mesh,
        in_specs=placed,
        out_specs=(
            P("dp", "seq", None),
            P("dp", "seq", None),
            P("dp", None),
            P(),
            P("dp", None),
            P("dp", None),
            P(),
            P("dp", None),
            P(),
            P("dp", None),
            P(),
            P(None, "dp"),
            P(),
        ),
        check_vma=False,
    )
```

```python
import functools

import jax
import jax.numpy as jnp
from jax import lax
from jax.experimental import pallas as pl
from jax.experimental.pallas import tpu as pltpu
from jax.sharding import PartitionSpec as P

HD = 64
LOG2E = 1.4426950408889634


highest = lax.Precision.HIGHEST


def tables(positions):
    half_dim = HD // 2
    frequency = jnp.exp(
        -jnp.log(10000.0) * (2.0 * jnp.arange(half_dim, dtype=jnp.float32) / HD)
    )
    angles = positions.astype(jnp.float32)[:, None] * frequency[None, :]
    cosine, sine = jnp.cos(angles), jnp.sin(angles)
    return (
        jnp.concatenate([cosine] * 4, axis=1),
        jnp.concatenate([-sine, sine, -sine, sine], axis=1),
    )


def full(shape):
    return pl.BlockSpec(shape, lambda step: (0,) * len(shape))


def columns(rows, width, first=0):
    return pl.BlockSpec((rows, width), lambda step: (0, step + first))


def shaped(shape, kind):
    return jax.ShapeDtypeStruct(shape, kind)


def far(shape, kind):
    return pltpu.HBM(shape, kind)


def store_split(low, core, own, keep, send):
    pairs = low.shape[0] // (2 * own)

    def store(kept):
        for pair in range(pairs):
            rows = slice(pair * own, (pair + 1) * own)
            for parity, target in ((kept, keep), (1 - kept, send)):
                start = (2 * pair + parity) * own
                target[rows, :] = low[start : start + own, :]

    @pl.when(core[0] == 0)
    def _():
        store(0)

    @pl.when(core[0] == 1)
    def _():
        store(1)


def zero_shape():
    return jax.ShapeDtypeStruct((1, 1), jnp.float32)


def scalar_spec():
    return pl.BlockSpec(memory_space=pltpu.SMEM)


def kernel_call(body, steps, in_specs, out_specs, out_shape, scratch, grant):
    call = pl.pallas_call(
        body,
        grid=(steps,),
        in_specs=in_specs,
        out_specs=out_specs,
        out_shape=out_shape,
        scratch_shapes=scratch,
        compiler_params=pltpu.CompilerParams(
            dimension_semantics=("arbitrary",), vmem_limit_bytes=grant * 1024 * 1024
        ),
        cost_estimate=pl.CostEstimate(flops=1, bytes_accessed=1, transcendentals=0),
    )

    def run(*args, free=()):
        placed = []
        for arg in args:
            if arg.size > 4096 and not any(arg is other for other in free):
                arg = pltpu.with_memory_space_constraint(arg, pltpu.HBM)
            placed.append(arg)
        return call(*placed)

    return run


def dot(left, right, left_axis=1, right_axis=0):
    return lax.dot_general(
        left,
        right,
        (((left_axis,), (right_axis,)), ((), ())),
        preferred_element_type=jnp.float32,
    )


def normalized(inputs):
    center = inputs - jnp.mean(inputs, axis=-1, keepdims=True)
    inverse = lax.rsqrt(jnp.mean(center * center, axis=-1, keepdims=True) + 1e-05)
    return center * inverse, inverse


def norm_back(back, hat, inverse, factor):
    scaled = back * factor
    return inverse * (
        scaled
        - jnp.mean(scaled, axis=-1, keepdims=True)
        - hat * jnp.mean(scaled * hat, axis=-1, keepdims=True)
    )


def column_sum(values):
    return jnp.sum(values, axis=0, keepdims=True)


SHIFT1, SCALE1, GATE1, SHIFT2, SCALE2, GATE2, GAIN1, GAIN2, COND = range(9)


def row(ref, index):
    return ref[index : index + 1, :]


def rotate_lanes(values, cosine, sine):
    lane = lax.broadcasted_iota(jnp.int32, cosine.shape, 1)
    lower = (lane % HD) < HD // 2
    parts = []
    for start in range(0, values.shape[1], 128):
        part = values[:, start : start + 128]
        other = jnp.where(lower, pltpu.roll(part, 128 - HD // 2, 1), pltpu.roll(part, HD // 2, 1))
        parts.append(part * cosine + other * sine)
    return jnp.concatenate(parts, axis=1)


HEADS = 4


def key_value_body(
    tokens, mods, key_weight, value_weight, cosine, sine, normed, *parts
):
    step = pl.program_id(0)

    @pl.when(step == 0)
    def _():
        hat, _ = normalized(tokens[...].astype(jnp.float32))
        value = hat * row(mods, GAIN1) * (1.0 + row(mods, SCALE1)) + row(mods, SHIFT1)
        normed[...] = value.astype(jnp.bfloat16)

    keys = rotate_lanes(dot(normed[...], key_weight[...]), cosine[...], sine[...])
    values = dot(normed[...], value_weight[...])
    both = jnp.concatenate([keys, values], axis=1).astype(jnp.bfloat16)
    for index, part in enumerate(parts):

        @pl.when(step == index)
        def _(part=part):
            part[...] = both


def project_key_value(tokens, mods, weight, cosine, sine):
    rows, width = tokens.shape
    lanes = HEADS * HD
    steps = width // lanes
    low = jnp.bfloat16
    return kernel_call(
        key_value_body,
        steps,
        [
            full((rows, width)),
            full((16, width)),
            columns(width, lanes, steps),
            columns(width, lanes, 2 * steps),
            full((rows, 128)),
            full((rows, 128)),
        ],
        [full((rows, width))] + [full((rows, 2 * lanes))] * steps,
        [far((rows, width), low)] + [far((rows, 2 * lanes), low)] * steps,
        [],
        24,
    )(tokens, mods, weight, weight, cosine, sine, free=(tokens,))


def head_mask(shape, head):
    lane = lax.broadcasted_iota(jnp.int32, shape, 1)
    return jnp.where(lane // HD == head, 1.0, 0.0).astype(jnp.bfloat16)


def head_lanes(head):
    pair, place = divmod(head, 2)
    return slice(pair * 128, (pair + 1) * 128), place, slice(place * HD, (place + 1) * HD)


def value_lanes(lanes):
    return slice(HEADS * HD + lanes.start, HEADS * HD + lanes.stop)


def in_turn(count, first, rest):
    results = []
    ahead = first(0)
    for index in range(count):
        now = ahead
        if index + 1 < count:
            ahead = first(index + 1)
        results.append(rest(index, now))
    return results


def attend_heads(query, pair1, pair2, log_total, shifted):
    rows = query.shape[0]

    def first(head):
        lanes, place, _ = head_lanes(head)
        own = query[:, lanes] * head_mask((rows, 128), place)
        return dot(pair1[:, lanes], own, 1, 1), dot(pair2[:, lanes], own, 1, 1)

    def rest(head, scores):
        lanes, place, turned = head_lanes(head)
        scores1, scores2 = scores
        if shifted:
            top = jnp.maximum(
                jnp.max(scores1, axis=0, keepdims=True), jnp.max(scores2, axis=0, keepdims=True)
            )
            scores1, scores2 = scores1 - top, scores2 - top
        exps1, exps2 = jnp.exp2(scores1), jnp.exp2(scores2)
        total = column_sum(exps1) + column_sum(exps2)
        lanes = value_lanes(lanes)
        mixed = dot(pair1[:, lanes].T[turned], exps1.astype(jnp.bfloat16)) + dot(
            pair2[:, lanes].T[turned], exps2.astype(jnp.bfloat16)
        )
        log_sum = jnp.log2(total)
        log_total[0, head : head + 1, :] = top + log_sum if shifted else log_sum
        return mixed * (1.0 / total)

    parts = in_turn(HEADS, first, rest)
    logs = log_total[0]
    in_range = (jnp.min(logs) > -60.0) & (jnp.max(logs) < 60.0)
    return in_range, jnp.concatenate(
        [
            jnp.concatenate(parts[head : head + 2], axis=0).T.astype(jnp.bfloat16)
            for head in range(0, HEADS, 2)
        ],
        axis=1,
    )


def attend_back_body(second, parts, query, grad, attended, log_total, *refs):
    step = pl.program_id(0)
    pairs, arrived = refs[-2:]
    arrivals = [
        pltpu.make_async_copy(refs[index], pairs.at[index], arrived.at[index])
        for index in range(parts)
    ]
    refs = refs[parts:-2]

    @pl.when(step == 0)
    def _():
        for arrival in arrivals:
            arrival.start()

    for index in range(parts):

        @pl.when(step == index)
        def _(index=index):
            arrivals[index].wait()

    pair = pairs.at[step]
    if second:
        before, cosine, sine = refs[:3]
    d_query, d_keys, d_values = refs[-3:]
    rows = query.shape[0]
    products = {}

    def first(head):
        lanes, place, _ = head_lanes(head)
        if place == 0:
            product = grad[:, lanes].astype(jnp.float32) * attended[:, lanes].astype(jnp.float32)
            products[head] = products[head + 1] = product.T
        own = query[:, lanes] * head_mask((rows, 128), place)
        own_grad = grad[:, lanes] * head_mask((rows, 128), place)
        scores = dot(pair[:, lanes], own, 1, 1)
        d_probs = dot(pair[:, value_lanes(lanes)], own_grad, 1, 1)
        return own, own_grad, scores, d_probs

    def rest(head, given):
        own, own_grad, scores, d_probs = given
        lanes, place, turned = head_lanes(head)
        delta = column_sum(products[head][turned])
        probs = jnp.exp2(scores - log_total[0, head : head + 1, :])
        d_scores = (probs * (d_probs - delta)).astype(jnp.bfloat16)
        return (
            dot(pair[:, lanes].T[turned], d_scores),
            dot(d_scores, own),
            dot(probs.astype(jnp.bfloat16), own_grad),
        )

    parts = in_turn(HEADS, first, rest)
    for head in range(0, HEADS, 2):
        lanes = head_lanes(head)[0]
        one, two = parts[head : head + 2]
        turned = jnp.concatenate([one[0], two[0]], axis=0).T * HD ** (-0.5)
        if second:
            turned = rotate_lanes(turned + before[:, lanes], cosine[...], -sine[...])
        d_query[:, lanes] = turned.astype(d_query.dtype)
        d_keys[:, lanes] = ((one[1] + two[1]) * (1.0 / LOG2E)).astype(jnp.bfloat16)
        d_values[:, lanes] = (one[2] + two[2]).astype(jnp.bfloat16)


def attend_back(query, parts, grad, attended, log_total, before=None, after=(), free=()):
    rows, width = query.shape
    lanes = HEADS * HD
    steps = width // lanes
    block = columns(rows, lanes)
    second = before is not None
    extra = list(before) if second else []
    extra_specs = [block, full((rows, 128)), full((rows, 128))] if second else []
    return kernel_call(
        functools.partial(attend_back_body, second, steps),
        steps,
        [
            block,
            block,
            block,
            pl.BlockSpec((1, HEADS, rows), lambda step: (step, 0, 0)),
        ]
        + [pl.BlockSpec(memory_space=pl.ANY)] * steps
        + extra_specs
        + [pl.BlockSpec(memory_space=pl.ANY)] * len(after),
        [block, block, block],
        [shaped((rows, width), jnp.bfloat16)] * 3
        if second
        else [
            far((rows, width), jnp.float32),
            far((rows, width), jnp.bfloat16),
            far((rows, width), jnp.bfloat16),
        ],
        [
            pltpu.VMEM((steps, rows, 2 * lanes), jnp.bfloat16),
            pltpu.SemaphoreType.DMA((steps,)),
        ],
        30,
    )(query, grad, attended, log_total, *parts, *extra, *after, free=free)


def block_body(
    own_down, attend_steps, hidden_steps,
    core, normed1, query_weight, cosine, sine, mods, up_bias, down_bias, *refs,
):
    pairs_far, refs = refs[: 2 * attend_steps], refs[2 * attend_steps :]
    (
        tokens_far, cotangent_far, out_far, up_far, down_far, cotangent_own,
        query, attended, log_total, mixed, d_middle, d_attended, up_grad,
        down_keep, down_send, bias_grad, sums,
        tokens, cotangent, out_weight, up_weight, down_weight, arrived,
        own_pairs, peer_pairs, pair_arrived,
        all_attended, normed, d_ffn, branch, middle, forward, back,
    ) = refs
    step = pl.program_id(0)
    tile = up_bias.shape[1]
    own_arrivals, peer_arrivals = [], []
    for index in range(attend_steps):
        own_arrivals.append(
            pltpu.make_async_copy(
                pairs_far[index], own_pairs.at[index], pair_arrived.at[0, index]
            )
        )
        peer_arrivals.append(
            pltpu.make_async_copy(
                pairs_far[attend_steps + index], peer_pairs.at[index], pair_arrived.at[1, index]
            )
        )
    arrivals = [
        pltpu.make_async_copy(source, target, arrived.at[index])
        for index, (source, target) in enumerate(
            (
                (tokens_far, tokens),
                (cotangent_far, cotangent),
                (out_far, out_weight),
                (up_far, up_weight),
                (down_far, down_weight),
            )
        )
    ]

    @pl.when(step == 0)
    def _():
        for index in range(attend_steps):
            own_arrivals[index].start()
            peer_arrivals[index].start()
        for index, arrival in enumerate(arrivals):
            if index != 1:
                arrival.start()

        @pl.when(core[1] == 0)
        def _():
            arrivals[1].start()

        @pl.when(core[1] == 1)
        def _():
            pltpu.make_async_copy(cotangent_own, cotangent, arrived.at[1]).start()

    @pl.when(step < attend_steps)
    def _():
        value = rotate_lanes(dot(normed1[...], query_weight[...]), cosine[...], sine[...])
        query[...] = (value * (LOG2E * HD ** (-0.5))).astype(jnp.bfloat16)
        for index in range(attend_steps):

            @pl.when(step == index)
            def _(index=index):
                own_arrivals[index].wait()
                peer_arrivals[index].wait()

        pairs = own_pairs.at[step], peer_pairs.at[step]
        in_range, found = attend_heads(query, *pairs, log_total, False)
        attended[...] = found

        @pl.when(jnp.logical_not(in_range))
        def _():
            attended[...] = attend_heads(query, *pairs, log_total, True)[1]

        for index in range(attend_steps):

            @pl.when(step == index)
            def _(index=index):
                heads = HEADS * HD
                all_attended[:, index * heads : (index + 1) * heads] = attended[...]

    @pl.when(step == attend_steps)
    def _():
        for arrival in arrivals:
            arrival.wait()
        turned = dot(all_attended[...], out_weight[...])
        branch[...] = turned.astype(jnp.bfloat16)
        value = tokens[...].astype(jnp.float32) + row(mods, GATE1) * turned
        middle[...] = value
        hat, _ = normalized(value)
        value = hat * row(mods, GAIN2) * (1.0 + row(mods, SCALE2)) + row(mods, SHIFT2)
        normed[...] = value.astype(jnp.bfloat16)
        low = (row(mods, GATE2) * cotangent[...].astype(jnp.float32)).astype(jnp.bfloat16)
        d_ffn[...] = low
        sums[4:5, :] = column_sum(low.astype(jnp.float32))
        forward[...] = jnp.zeros_like(forward)
        back[...] = jnp.zeros_like(back)

    @pl.when((step >= attend_steps) & (step < attend_steps + hidden_steps))
    def _():
        place = pl.ds(pl.multiple_of((step - attend_steps) * tile, tile), tile)
        pre = dot(normed[...], up_weight[:, place]) + up_bias[...]
        d_activated = dot(d_ffn[...], down_weight[place, :], 1, 1)
        root = 0.7978845608028654
        square = pre * pre
        bent = jnp.tanh(root * pre * (1.0 + 0.044715 * square))
        half = 0.5 + 0.5 * bent
        slope = half + (0.5 * root) * pre * (1.0 - bent * bent) * (1.0 + 0.134145 * square)
        low = (pre * half).astype(jnp.bfloat16)
        d_pre = d_activated * slope
        d_low = d_pre.astype(jnp.bfloat16)
        bias_grad[...] = column_sum(d_pre)
        down_grad = dot(low, d_ffn[...], 0, 0).astype(jnp.bfloat16)
        store_split(down_grad, core, own_down, down_keep, down_send)
        up_grad[...] = dot(normed[...], d_low, 0, 0).astype(jnp.bfloat16)
        forward[...] += dot(low, down_weight[place, :])
        back[...] += dot(d_low, up_weight[:, place], 1, 1)

    @pl.when(step == attend_steps + hidden_steps)
    def _():
        grad = cotangent[...].astype(jnp.float32)
        held = middle[...]
        hat, inverse = normalized(held)
        factor = row(mods, GAIN2) * (1.0 + row(mods, SCALE2))
        value = back[...]
        d_value = grad + norm_back(value, hat, inverse, factor)
        d_middle[...] = d_value
        d_branch = (row(mods, GATE1) * d_value).astype(jnp.bfloat16)
        d_attended[...] = dot(d_branch, out_weight[...], 1, 1).astype(jnp.bfloat16)
        up_grad[...] = dot(all_attended[...], d_branch, 0, 0).astype(jnp.bfloat16)
        ffn = forward[...] + down_bias[...]
        mixed[...] = (held + row(mods, GATE2) * ffn).astype(jnp.bfloat16)
        sums[0:1, :] = column_sum(value)
        sums[1:2, :] = column_sum(value * hat)
        sums[2:3, :] = column_sum(d_value * branch[...].astype(jnp.float32))
        sums[3:4, :] = column_sum(grad * ffn)
        sums[5:8, :] = jnp.zeros_like(sums[5:8, :])


def split_rows(rows):
    own = rows // lax.axis_size("dp")
    return own if own % 16 == 0 else rows // 2


def block_layer(
    core, normed1, qkv_weight, cosine, sine, mods, up_bias, down_bias, own, peer,
    tokens, cotangent, out_weight, up_weight, down_weight, cotangent_own,
):
    rows, width = tokens.shape
    hidden = up_weight.shape[1]
    tile = width
    lanes = HEADS * HD
    attend_steps = width // lanes
    hidden_steps = hidden // tile
    own_down = hidden // lax.axis_size("dp")
    if own_down % 16 > 0:
        own_down = tile // 2

    def heads(first=0):
        return pl.BlockSpec(
            (rows, lanes), lambda step: (0, jnp.minimum(step, attend_steps - 1) + first)
        )

    def tiles(step):
        return jnp.clip(step - attend_steps, 0, hidden_steps - 1)

    def up_tiles(step):
        return jnp.clip(step - attend_steps, 0, hidden_steps)

    block = full((rows, width))
    far_spec = pl.BlockSpec(memory_space=pl.ANY)
    low = jnp.bfloat16
    up_spec = pl.BlockSpec((width, tile), lambda step: (0, up_tiles(step)))
    down_spec = pl.BlockSpec((tile // 2, width), lambda step: (tiles(step), 0))
    return kernel_call(
        functools.partial(block_body, own_down, attend_steps, hidden_steps),
        attend_steps + hidden_steps + 1,
        [
            scalar_spec(),
            block,
            pl.BlockSpec((width, lanes), lambda step: (0, jnp.minimum(step, attend_steps - 1))),
            full((rows, 128)),
            full((rows, 128)),
            full((16, width)),
            pl.BlockSpec((1, tile), lambda step: (0, tiles(step))),
            full((1, width)),
        ]
        + [far_spec] * (2 * attend_steps + 6),
        [
            heads(),
            heads(),
            pl.BlockSpec(
                (1, HEADS, rows), lambda step: (jnp.minimum(step, attend_steps - 1), 0, 0)
            ),
            block,
            block,
            block,
            up_spec,
            down_spec,
            down_spec,
            pl.BlockSpec((1, tile), lambda step: (0, tiles(step))),
            full((8, width)),
        ],
        [
            far((rows, width), low),
            far((rows, width), low),
            far((attend_steps, HEADS, rows), jnp.float32),
            far((rows, width), low),
            far((rows, width), jnp.float32),
            far((rows, width), low),
            far((width, hidden + width), low),
            far((hidden // 2, width), low),
            far((hidden // 2, width), low),
            far((1, hidden), jnp.float32),
            far((8, width), jnp.float32),
        ],
        [
            pltpu.VMEM((rows, width), low),
            pltpu.VMEM((rows, width), low),
            pltpu.VMEM((width, width), low),
            pltpu.VMEM((width, hidden), low),
            pltpu.VMEM((hidden, width), low),
            pltpu.SemaphoreType.DMA((5,)),
            pltpu.VMEM((attend_steps, rows, 2 * lanes), low),
            pltpu.VMEM((attend_steps, rows, 2 * lanes), low),
            pltpu.SemaphoreType.DMA((2, attend_steps)),
            pltpu.VMEM((rows, width), low),
            pltpu.VMEM((rows, width), low),
            pltpu.VMEM((rows, width), low),
            pltpu.VMEM((rows, width), low),
            pltpu.VMEM((rows, width), jnp.float32),
            pltpu.VMEM((rows, width), jnp.float32),
            pltpu.VMEM((rows, width), jnp.float32),
        ],
        58,
    )(
        core, normed1, qkv_weight, cosine, sine, mods, up_bias, down_bias, *own, *peer,
        tokens, cotangent, out_weight, up_weight, down_weight, cotangent_own,
        free=(cotangent, tokens),
    )


def projected_back_body(
    own, core, d_query, d_keys, d_values, peer_keys, peer_values, normed, cosine, sine,
    d_projected, *parts,
):
    lanes = HEADS * HD
    keys = d_keys[...].astype(jnp.float32) + peer_keys[...].astype(jnp.float32)
    keys = rotate_lanes(keys, cosine[...], -sine[...]).astype(jnp.bfloat16)
    values = d_values[...].astype(jnp.float32) + peer_values[...].astype(jnp.float32)
    low = jnp.concatenate([d_query[...], keys, values.astype(jnp.bfloat16)], axis=1)
    d_projected[...] = low
    grad = dot(normed[...], low, 0, 0).astype(jnp.bfloat16)
    for index in range(3):
        third = grad[:, index * lanes : (index + 1) * lanes]
        store_split(third, core, own, parts[2 * index], parts[2 * index + 1])


def projected_back(core, d_query, d_keys, d_values, peer_keys, peer_values, normed, cosine, sine):
    rows, width = normed.shape
    lanes = HEADS * HD
    block = columns(rows, lanes)
    return kernel_call(
        functools.partial(projected_back_body, split_rows(width)),
        width // lanes,
        [
            scalar_spec(),
            block,
            block,
            block,
            block,
            block,
            full((rows, width)),
            full((rows, 128)),
            full((rows, 128)),
        ],
        [columns(rows, 3 * lanes)] + [columns(width // 2, lanes)] * 6,
        [far((rows, 3 * width), jnp.bfloat16)] + [far((width // 2, width), jnp.bfloat16)] * 6,
        [],
        32,
    )(
        core, d_query, d_keys, d_values, peer_keys, peer_values, normed, cosine, sine,
        free=(d_query, d_keys, d_values, peer_keys, peer_values),
    )


def tokens_back_body(
    d_projected, weight1, weight2, weight3, tokens, d_middle, mods, sums, bias_grad, *refs
):
    out, small, total = refs[-3:]
    step = pl.program_id(0)
    width = tokens.shape[1]
    lanes = HEADS * HD
    part = sum(
        dot(d_projected[:, index * lanes : (index + 1) * lanes], weight[...], 1, 1)
        for index, weight in enumerate((weight1, weight2, weight3))
    )

    @pl.when(step == 0)
    def _():
        total[...] = part

    @pl.when(step > 0)
    def _():
        total[...] += part

    @pl.when(step == pl.num_programs(0) - 1)
    def _():
        back = total[...]
        hat, inverse = normalized(tokens[...].astype(jnp.float32))
        scale1 = 1.0 + row(mods, SCALE1)
        gain1 = row(mods, GAIN1)
        out[...] = (d_middle[...] + norm_back(back, hat, inverse, gain1 * scale1)).astype(
            jnp.bfloat16
        )
        hat_sum1 = column_sum(back * hat)
        hat_sum2 = row(sums, 1)
        rows = [
            column_sum(back),
            hat_sum1 * gain1,
            row(sums, 2),
            row(sums, 0),
            hat_sum2 * row(mods, GAIN2),
            row(sums, 3),
            row(mods, COND) * 0.5,
            jnp.zeros_like(hat_sum1),
            hat_sum1 * scale1,
            hat_sum2 * (1.0 + row(mods, SCALE2)),
            row(sums, 4),
        ]
        for index in range(bias_grad.shape[1] // width):
            rows.append(bias_grad[:, index * width : (index + 1) * width])
        for index, value in enumerate(rows):
            small[index : index + 1, :] = value
        small[len(rows) :, :] = jnp.zeros_like(small[len(rows) :, :])


def tokens_back(d_projected, weight, tokens, d_middle, mods, sums, bias_grad, after):
    rows, width = tokens.shape
    lanes = HEADS * HD
    steps = width // lanes
    block = full((rows, width))
    return kernel_call(
        tokens_back_body,
        steps,
        [
            columns(rows, 3 * lanes),
            columns(width, lanes),
            columns(width, lanes, steps),
            columns(width, lanes, 2 * steps),
            block,
            block,
            full((16, width)),
            full((8, width)),
            full(bias_grad.shape),
        ]
        + [pl.BlockSpec(memory_space=pl.ANY)] * len(after),
        [block, full((16, width))],
        [far((rows, width), jnp.bfloat16), far((16, width), jnp.float32)],
        [pltpu.VMEM((rows, width), jnp.float32)],
        36,
    )(d_projected, weight, weight, weight, tokens, d_middle, mods, sums, bias_grad, *after)


def finish_body(
    places, here, there, embedded, ada_weight,
    first_gain, second_gain, up_bias, down_bias, ada_bias, ada_grad, cond_grad, every,
):
    width = here.shape[1]
    sequences = (here.shape[0] - 8) // 8
    own_columns = ada_grad.shape[0]
    sums = here[8 * sequences :, :] + there[8 * sequences :, :]
    first_gain[...] = sums[0, :]
    second_gain[...] = sums[1, :]
    down_bias[...] = sums[2, :]
    for index in range(up_bias.shape[0] // width):
        up_bias[index * width : (index + 1) * width] = sums[3 + index, :]
    total = here[:8, :] + there[:8, :]
    for index in range(1, sequences):
        rows = slice(8 * index, 8 * index + 8)
        total = total + here[rows, :] + there[rows, :]
    conds = []
    for side, block in enumerate((here, there)):
        for index in range(sequences):
            conds.append(block[8 * index + 6 : 8 * index + 7, : embedded.shape[1]])
            for part in range(6):
                every[
                    side * sequences + index : side * sequences + index + 1,
                    part * width : (part + 1) * width,
                ] = block[8 * index + part : 8 * index + part + 1, :]
    for part in range(6):
        ada_bias[part * width : (part + 1) * width] = total[part, :]
    turned = pltpu.roll(every[...], places[0], 1)[:, : -(-own_columns // 128) * 128]
    grad = lax.dot_general(
        turned,
        jnp.concatenate(conds, axis=0),
        (((0,), (0,)), ((), ())),
        precision=highest,
        preferred_element_type=jnp.float32,
    )
    ada_grad[...] = grad[:own_columns, :]
    own = jnp.where(places[1] == 1, here[:8, :], there[:8, :])
    products = ada_weight[:, :width].astype(jnp.float32) * own[0:1, :]
    for part in range(1, 6):
        columns_here = ada_weight[:, part * width : (part + 1) * width].astype(jnp.float32)
        products = products + columns_here * own[part : part + 1, :]
    summed = jnp.sum(products, axis=1, keepdims=True)
    turned_sum = jnp.broadcast_to(summed, (summed.shape[0], 128)).T[0:1, :]
    value = embedded[...]
    sigmoid = 1.0 / (1.0 + jnp.exp(-value))
    cond_grad[...] = turned_sum * (sigmoid * (1.0 + value * (1.0 - sigmoid)))


def finish(here, there, embedded, ada_weight, hidden):
    width = here.shape[1]
    sequences = (here.shape[0] - 8) // 8
    dp_size, dp_rank = lax.axis_size("dp"), lax.axis_index("dp")
    all_columns = ada_weight.shape[1]
    own_columns = all_columns // dp_size
    turn = (all_columns - dp_rank * own_columns) % all_columns
    same = (lax.axis_index("seq") == dp_rank % 2).astype(jnp.int32)
    kind = jnp.float32
    whole = pl.BlockSpec(memory_space=pltpu.VMEM)
    return pl.pallas_call(
        finish_body,
        in_specs=[scalar_spec(), whole, whole, whole, whole],
        out_specs=[whole] * 7,
        out_shape=[
            shaped((width,), kind),
            shaped((width,), kind),
            shaped((hidden,), kind),
            shaped((width,), kind),
            shaped((all_columns,), kind),
            shaped((own_columns, ada_weight.shape[0]), kind),
            shaped((1, ada_weight.shape[0]), kind),
        ],
        scratch_shapes=[pltpu.VMEM((2 * sequences, all_columns), kind)],
        compiler_params=pltpu.CompilerParams(vmem_limit_bytes=24 * 1024 * 1024),
        cost_estimate=pl.CostEstimate(flops=1, bytes_accessed=1, transcendentals=0),
    )(jnp.stack([turn, same]), here, there, embedded, ada_weight)


def swap_halves(block, alone=True):
    count = lax.axis_size("dp") * lax.axis_size("seq")
    target = {1: 2, 2: 1}
    perm = [(i, i - i % 4 + target.get(i % 4, i % 4)) for i in range(count)]
    if not alone:
        perm = [(source, partner) for source, partner in perm if source != partner]
    return lax.ppermute(block, ("dp", "seq"), perm)


def swap_bit(block, bit):
    return lax.ppermute(block, "dp", [(i, i ^ bit) for i in range(lax.axis_size("dp"))])


def swap_cores(block):
    return swap_bit(block, 1)


def swap_seq(block):
    return lax.ppermute(block, "seq", [(0, 1), (1, 0)])


def dp_bits():
    bits, bit = [], 1
    while bit < lax.axis_size("dp"):
        bits.append(bit)
        bit *= 2
    return bits


def pick(block, axis, index):
    return lax.dynamic_index_in_dim(block, index, axis, keepdims=False)


class Flow:
    def __init__(self, got, kept, lanes=None):
        self.got, self.kept = got, kept
        self.lanes = lanes or (0, kept.shape[2])
        self.count, self.rest = kept.shape[:2]
        self.width = self.lanes[1] - self.lanes[0]


def stage_body(jobs, counts, mine, *refs):
    inputs = refs[: counts[0]]
    outputs = refs[counts[0] + counts[1] :]

    def terms(sources, place):
        for one, two, lanes, rows in sources:
            total = inputs[one][place + (slice(None), lanes)].astype(jnp.float32)
            total = total + inputs[two][place + (slice(None), lanes)].astype(jnp.float32)
            total = total.astype(jnp.bfloat16)
            height = total.shape[-2]
            for start in range(0, height, rows):
                yield total if height == rows else total[..., start : start + rows, :]

    def store(out, place, values):
        at = 0
        for value in values:
            width = value.shape[-1]
            out[place + (slice(None), slice(at, at + width))] = value
            at += width

    def run(index, kind, stride, sources, target):
        if kind == "sum":
            store(outputs[target], (slice(None),), terms(sources, (slice(None),)))
            return

        def part(out, which):
            if kind == "half":
                halves = []
                for one, two, lanes, rows in sources:
                    middle = (lanes.start + lanes.stop) // 2
                    first, second = slice(lanes.start, middle), slice(middle, lanes.stop)
                    halves.append((one, two, second if which else first, rows))
                store(out, (slice(None),), terms(halves, (slice(None),)))
                return
            for block in range(out.shape[0]):
                high, low = divmod(block, stride)
                place = (2 * high + which) * stride + low
                store(out, (block,), terms(sources, (place,)))

        for which in range(2):

            @pl.when(mine[index] == which)
            def _(which=which):
                part(outputs[target + 1], which)
                part(outputs[target], 1 - which)

    for index, (kind, stride, sources, target, whole) in enumerate(jobs):
        if whole:

            @pl.when(pl.program_id(0) == 0)
            def _(args=(index, kind, stride, sources, target)):
                run(*args)

        else:
            run(index, kind, stride, sources, target)


def small_body(first, one, two, out):
    rows = one.shape[0] - 8

    @pl.when(pl.program_id(0) == 0)
    def _():
        if first:
            out[...] = one[...] + two[...]
        else:
            out[:rows, :] = one[:rows, :]
            out[rows : 2 * rows, :] = two[:rows, :]
            out[2 * rows :, :] = one[rows:, :] + two[rows:, :]


def stage(steps, jobs, after=(), small=None, free=(), relay=None):
    seq_rank, dp_rank = lax.axis_index("seq"), lax.axis_index("dp")
    inputs, in_specs, specs, out_specs, out_shape, mine = [], [], [], [], [], []
    free = [*free] + [flow.got for flows, _ in jobs for flow in flows]

    def spec(shape, whole):
        if whole:
            return full(shape)
        return pl.BlockSpec((shape[0] // steps,) + shape[1:], lambda at: (at, 0, 0))

    def place_of(array, whole):
        for index, other in enumerate(inputs):
            if other is array:
                return index
        inputs.append(array)
        in_specs.append(spec(array.shape, whole))
        return len(inputs) - 1

    for flows, step in jobs:
        bit, stride = step if isinstance(step, tuple) else (None, 1)
        rest, count = flows[0].rest, flows[0].count
        smallest = 1 if bit is None else 2 * stride
        whole = count % steps > 0 or (count // steps) % smallest > 0
        sources = [
            (place_of(flow.got, whole), place_of(flow.kept, whole), slice(*flow.lanes), rest)
            for flow in flows
        ]
        width = sum(flow.width * flow.rest // rest for flow in flows)
        if bit is not None:
            shape = (count // 2, rest, width)
            mine.append((dp_rank // bit) % 2)
        else:
            shape = (count, rest, width // 2 if step == "half" else width)
            mine.append(seq_rank)
        specs.append((step if bit is None else "bit", stride, sources, len(out_shape), whole))
        results = 1 if step == "sum" else 2
        out_shape += [far(shape, jnp.bfloat16)] * results
        out_specs += [spec(shape, whole)] * results
    counts = (len(inputs), len(after))
    extra = []
    if small is not None:
        got, kept, first = small
        extra = [kept, got]
        rows = kept.shape[0] if first else 2 * kept.shape[0] - 8
        out_shape.append(far((rows, kept.shape[1]), jnp.float32))
        out_specs.append(full((rows, kept.shape[1])))

    if relay is not None:
        extra.append(relay)
        out_shape.append(far(relay.shape, relay.dtype))
        out_specs.append(full(relay.shape))

    def body(mine, *refs):
        if relay is not None:
            place = sum(counts) + len(extra) - 1
            refs[-1][...] = refs[place][...]
            refs = (*refs[:place], *refs[place + 1 : -1])
        if small is None:
            stage_body(specs, counts, mine, *refs)
            return
        main, ends = refs[: sum(counts)], refs[sum(counts) :]
        small_body(first, ends[0], ends[1], ends[-1])
        stage_body(specs, counts, mine, *main, *ends[2:-1])

    results = kernel_call(
        body,
        steps,
        [scalar_spec()]
        + in_specs
        + [pl.BlockSpec(memory_space=pl.ANY)] * len(after)
        + [full(array.shape) for array in extra],
        out_specs,
        out_shape,
        [],
        40,
    )(jnp.stack(mine), *inputs, *after, *extra, free=(*free, *extra[1:2]))
    new = []
    for (flows, step), (_, _, _, target, _) in zip(jobs, specs):
        sent = results[target]
        got = swap_seq(sent) if isinstance(step, str) else swap_bit(sent, step[0])
        new.append(Flow(got, sent if step == "sum" else results[target + 1]))
    if small is not None:
        new.append(results[-1 if relay is None else -2])
    if relay is not None:
        new.append(results[-1])
    return new, results[0]


def from_tiles(kept, sent, tile):
    rows, width = 2 * kept.shape[0], kept.shape[1]
    core = lax.axis_index("dp") % 2
    first = jnp.where(core == 0, kept, sent).reshape(rows // tile, 1, tile // 2, width)
    second = jnp.where(core == 0, sent, kept).reshape(rows // tile, 1, tile // 2, width)
    return jnp.concatenate([first, second], axis=1).reshape(rows, width)


def plain_sum(kept, sent, tile):
    matrix = from_tiles(kept, sent, tile)
    return lax.psum(
        lax.psum_scatter(matrix, "dp", scatter_dimension=0, tiled=True).astype(jnp.float32), "seq"
    )


def joined(flow, widths):
    block, got = flow.kept[0].astype(jnp.float32), flow.got[0].astype(jnp.float32)
    here = lax.axis_index("seq") == 0
    first, second = jnp.where(here, block, got), jnp.where(here, got, block)
    parts, at = [], 0
    for width in widths:
        parts.append(
            jnp.concatenate([first[:, at : at + width], second[:, at : at + width]], axis=1)
        )
        at += width
    return parts


def per_device(
    tokens,
    cotangent,
    time_index,
    step_table,
    first_gain,
    attn_qkv,
    attn_out,
    second_gain,
    mlp_up,
    up_bias,
    mlp_down,
    down_bias,
    ada_weight,
    ada_bias,
):
    rows, width = tokens.shape[1:]
    dp_rank = lax.axis_index("dp")
    core = dp_rank % 2
    own_embedded = lax.dynamic_slice_in_dim(step_table, time_index[0], 1, axis=0)
    positions = core * rows + jnp.arange(rows, dtype=jnp.int32)
    cosine, sine = tables(positions)
    tokens = swap_halves(tokens[0])
    time_index = swap_halves(time_index)
    cotangent_own = cotangent[0]
    cotangent = swap_halves(cotangent_own, alone=False)
    cond = jax.nn.silu(lax.dynamic_slice_in_dim(step_table, time_index[0], 1, axis=0))
    ada_float = ada_weight.astype(jnp.float32)
    modulation = jnp.dot(cond, ada_float, precision=highest) + ada_bias.astype(jnp.float32)
    gain1 = first_gain.astype(jnp.float32)
    gain2 = second_gain.astype(jnp.float32)
    cond_row = jnp.pad(cond, ((0, 0), (0, width - cond.shape[1])))
    mods = jnp.concatenate(
        [modulation.reshape(6, width), gain1[None], gain2[None], cond_row, jnp.zeros((7, width))]
    )
    normed1, *own_parts = project_key_value(tokens, mods, attn_qkv, cosine, sine)
    peer_parts = [swap_cores(part) for part in own_parts]
    core_ref = jnp.stack([core, (lax.axis_index("seq") == core).astype(jnp.int32)])
    (
        query, attended, log_total, mixed, d_middle, d_attended, up_grad,
        down_keep, down_send, up_bias_grad, sums2,
    ) = block_layer(
        core_ref, normed1, attn_qkv, cosine, sine, mods,
        up_bias.astype(jnp.float32)[None], down_bias.astype(jnp.float32)[None],
        own_parts, peer_parts,
        tokens, cotangent, attn_out, mlp_up, mlp_down, cotangent_own,
    )
    hidden = mlp_up.shape[1]
    dp_size = lax.axis_size("dp")
    bits = dp_bits()
    by_steps = split_rows(width) == width // dp_size and len(bits) == 4
    up_rows = lax.psum_scatter(up_grad, "dp", scatter_dimension=0, tiled=True)
    up_got = swap_seq(up_rows)

    def blocks(part):
        return part.reshape(dp_size // 2, -1, part.shape[1])

    if by_steps:
        down = Flow(swap_cores(blocks(down_send)), blocks(down_keep))
    d_query, away_keys, away_values = attend_back(query, peer_parts, d_attended, attended, log_total)
    after = ()
    if by_steps:
        (down,), sent = stage(2, [([down], "half")], (away_keys,))
        after = (sent,)
    peer_keys, peer_values = swap_cores(away_keys), swap_cores(away_values)
    d_query, d_keys, d_values = attend_back(
        query, own_parts, d_attended, attended, log_total, (d_query, cosine, sine), after
    )
    d_projected, *qkv_parts = projected_back(
        core_ref, d_query, d_keys, d_values, peer_keys, peer_values, normed1, cosine, sine
    )
    sent = ()
    if by_steps:
        late = [
            Flow(swap_cores(blocks(send)), blocks(keep))
            for keep, send in zip(qkv_parts[::2], qkv_parts[1::2])
        ]
        (late,), *sent = stage(2, [(late, "half")])
        (down, mixed), *sent = stage(2, [([down], (bits[1], 1))], sent, relay=mixed)
    tokens_grad, small = tokens_back(
        d_projected, attn_qkv, tokens, d_middle, mods, sums2, up_bias_grad, sent
    )
    small = small + swap_cores(small)
    moves = [functools.partial(swap_bit, bit=bit) for bit in bits[2:] + bits[1:2]] + [swap_seq]

    def doubled(small, got):
        return jnp.concatenate([small[:-8], got[:-8], small[-8:] + got[-8:]], axis=0)

    if by_steps:

        def next_stage(jobs, count, moves_before, after=(), relay=None):
            nonlocal small, sent
            for _ in range(moves_before):
                small = doubled(small, moves.pop(0)(small))
            extra = (moves.pop(0)(small), small, False) if len(moves) > 0 else None
            flows, *sent = stage(count, jobs, (*sent, *after), extra, after, relay)
            if extra is not None:
                small = flows.pop(len(jobs))
            return flows

        down, late, tokens_grad = next_stage(
            [([down], (bits[2], 1)), ([late], (bits[1], 1))], 2, 0, (), tokens_grad
        )
        down, late = next_stage([([down], (bits[3], 1)), ([late], (bits[2], 1))], 2, 0)
        down, late = next_stage([([down], "sum"), ([late], (bits[3], 1))], 1, 0, (up_got,))
        last = moves.pop(0)(small)
        (late,) = next_stage([([late], "sum")], 1, 0)
        (
            first_gain_grad, second_gain_grad, all_up_bias_grad, down_bias_grad, ada_bias_grad,
            ada_turned, cond_grad,
        ) = finish(small, last, own_embedded, ada_weight, hidden)
        ada_weight_grad = ada_turned.T
        (down_rows,) = joined(down, (width // 2,))
        qkv_rows = jnp.concatenate(joined(late, (width // 2,) * 3), axis=1)
    else:
        for move in moves:
            small = doubled(small, move(small))
        down_rows = plain_sum(down_keep, down_send, width)
        qkv_rows = jnp.concatenate(
            [
                plain_sum(keep, send, width)
                for keep, send in zip(qkv_parts[::2], qkv_parts[1::2])
            ],
            axis=1,
        )
        per_sequence, sums = small[:-8].reshape(-1, 8, width), small[-8:]
        d_mod_all = per_sequence[:, :6].reshape(per_sequence.shape[0], 6 * width)
        cond_all = per_sequence[:, 6, : cond.shape[1]]
        own_columns = d_mod_all.shape[1] // dp_size
        mine = lax.dynamic_slice_in_dim(d_mod_all, dp_rank * own_columns, own_columns, axis=1)
        ada_weight_grad = lax.dot_general(
            cond_all, mine, (((0,), (0,)), ((), ())), precision=highest
        )
        other = d_mod_all.shape[0] // 2
        d_mod_own = jnp.where(
            lax.axis_index("seq") == core, d_mod_all[:1], d_mod_all[other : other + 1]
        )
        _, silu_back = jax.vjp(jax.nn.silu, own_embedded)
        (cond_grad,) = silu_back(jnp.dot(d_mod_own, ada_float.T, precision=highest))
        first_gain_grad, second_gain_grad, down_bias_grad = sums[0], sums[1], sums[2]
        all_up_bias_grad = sums[3:7].reshape(-1)
        ada_bias_grad = jnp.sum(d_mod_all, axis=0)
    up_rows = up_rows.astype(jnp.float32) + up_got.astype(jnp.float32)
    return (
        swap_halves(mixed)[None],
        swap_halves(tokens_grad).astype(jnp.float32)[None],
        cond_grad,
        first_gain_grad,
        qkv_rows,
        up_rows[:, hidden:],
        second_gain_grad,
        up_rows[:, :hidden],
        all_up_bias_grad,
        down_rows,
        down_bias_grad,
        ada_weight_grad,
        ada_bias_grad,
    )


def solution(mesh):
    placed = (
        P("dp", "seq", None),
        P("dp", "seq", None),
        P("dp"),
        P(),
        P(),
        P(),
        P(),
        P(),
        P(),
        P(),
        P(),
        P(),
        P(),
        P(),
    )
    return jax.shard_map(
        per_device,
        mesh=mesh,
        in_specs=placed,
        out_specs=(
            P("dp", "seq", None),
            P("dp", "seq", None),
            P("dp", None),
            P(),
            P("dp", None),
            P("dp", None),
            P(),
            P("dp", None),
            P(),
            P("dp", None),
            P(),
            P(None, "dp"),
            P(),
        ),
        check_vma=False,
    )
```
